128 devices in a mesh: slide: 4 (over y), seq: 32 (over x, z, core).
Axes of the slice: x: 4, y: 4, z: 4, core: 2. Of those that a mesh axis runs over, the one named last changes fastest.
Arguments:
- query_tiles: bfloat16 [131072, 768], P(('slide', 'seq')), parts along dimension 0, may hold values from -160 to 160
- key_tiles: bfloat16 [131072, 768], P(('slide', 'seq')), parts along dimension 0, may hold values from -4.04 to 4.04
- value_tiles: bfloat16 [131072, 768], P(('slide', 'seq')), parts along dimension 0, may hold values from -6 to 6
- slide_length: int32 [4], P('slide'), parts along dimension 0, may hold values from 32256 to 32768
Outputs:
- attended: bfloat16 [131072, 768], P(('slide', 'seq')), parts along dimension 0
The draws below stay inside these ranges and needn't reach their ends.
There are 4 independent parts, one for each index of `slide`. The reference program is written for one: setup_inputs(seed, part) draws one part's arguments, and reference() takes and returns one part's arrays. A program takes and returns all parts, laid end to end along the dimension named above; each array names one. Nothing has to cross between parts.
All inputs are finite; a program needn't handle non-finite values.
Results may differ from the reference program's by a relative error of at most 0.0045.
Values may be sent and summed in bfloat16 or wider, within the bound.
No kernel may reach another device: no remote copies, remote signals or barrier semaphores. Data moves between devices by JAX's collectives and lax.ppermute only.
A program may use at most 128 MiB of HBM per device.

```python
from functools import reduce
import jax
import jax.numpy as jnp
import numpy as np
from jax import lax

HEADS = 12
HEAD_DIM = 64
WIDTH = 768
TOK_DEV = 1024
TOKENS = 32768
SEG0 = 512
BRANCHES = 5


def shared_rows(key):
    base = jnp.clip(jax.random.normal(jax.random.fold_in(key, 11), (TOKENS, WIDTH), jnp.float32), -4.0, 4.0)
    return base


def draw_key_tiles(key, part):
    base = shared_rows(key)
    return base.astype(jnp.bfloat16)


def draw_query_tiles(key, part):
    key = jax.random.fold_in(key, 2)
    own = jnp.clip(jax.random.normal(key, (TOKENS, WIDTH), jnp.float32), -4.0, 4.0)
    return own.astype(jnp.bfloat16)


def level_of(rng, shape, shards, least, high):
    level, own = 1.0, jax.random.fold_in(rng, 6)
    for axis_at, blocks in shards:
        steps = jnp.exp(jax.random.uniform(jax.random.fold_in(own, axis_at), (blocks,), jnp.float32, least / len(shards), high / len(shards)))
        level = level * jnp.repeat(steps, shape[axis_at] // blocks).reshape([-1 if axis == axis_at else 1 for axis in range(len(shape))])
    return level


def noise(stream_key, shape, width, reach, cuts=(), held_as=jnp.bfloat16):
    values = jax.random.normal(stream_key, shape, jnp.float32) * width
    if len(cuts) > 0:
        values = level_of(stream_key, shape, cuts, -0.22, 0.18) * values
    return jnp.clip(values, min=-reach, max=reach).astype(held_as)


def setup_inputs(seed: int = 0, part: int = 0) -> dict:
    key_of = jax.random.split(jax.random.key(seed), 5)
    part_keys = jax.random.split(jax.random.fold_in(key_of[4], part), 5)
    query_tiles = draw_query_tiles(jax.random.fold_in(jax.random.fold_in(key_of[4], part), 71), part)
    key_tiles = draw_key_tiles(jax.random.fold_in(jax.random.fold_in(key_of[4], part), 71), part)
    value_tiles = noise(part_keys[2], (TOKENS, WIDTH), 1.0, 6.0, ((0, 32),))
    slide_length = jax.random.randint(part_keys[3], (1,), TOKENS - TOK_DEV // 2, TOKENS + 1).astype(jnp.int32)
    return dict(query_tiles=query_tiles, key_tiles=key_tiles, value_tiles=value_tiles, slide_length=slide_length)


scale_factor = 0.125
mask_fill = -1e9
lse_fill = -1e30
ref_block = 1024


def offsets(stride):
    return np.arange(HEADS) % stride


def dilate(source, stride):
    count = source.shape[0] // stride
    shaped = source.reshape(count, stride, HEADS, HEAD_DIM)
    picked = shaped[:, offsets(stride), np.arange(HEADS), :]
    return picked.reshape(count, HEADS * HEAD_DIM)


def spread(compact, stride, fill_value):
    selector = np.arange(stride)[:, None] == offsets(stride)[None, :]
    widened = jnp.where(selector[None, :, :, None], compact[:, None], fill_value)
    return widened.reshape(compact.shape[0] * stride, HEADS, compact.shape[-1])


def attend(query_part, key_part, value_part, key_valid):
    query_count = query_part.shape[0]
    key_count = key_part.shape[0]
    query_heads = query_part.astype(jnp.float32).reshape(query_count, HEADS, HEAD_DIM)
    key_heads = key_part.astype(jnp.float32).reshape(key_count, HEADS, HEAD_DIM)
    value_heads = value_part.astype(jnp.float32).reshape(key_count, HEADS, HEAD_DIM)
    scores = jnp.einsum("qhd,khd->hqk", query_heads, key_heads) * scale_factor
    scores = jnp.where(jnp.transpose(key_valid)[:, None, :], scores, mask_fill)
    row_max = jnp.max(scores, axis=-1, keepdims=True)
    weights = jnp.exp(scores - row_max)
    totals = jnp.sum(weights, axis=-1)
    rounded = lax.optimization_barrier(weights.astype(jnp.bfloat16)).astype(jnp.float32)
    mixed_out = jnp.einsum("hqk,khd->qhd", rounded, value_heads) / jnp.transpose(totals)[:, :, None]
    log_total = jnp.transpose(row_max[..., 0] + jnp.log(totals))
    return mixed_out, log_total


def attend_blocked(query_part, key_part, value_part, key_valid):
    query_count = query_part.shape[0]
    if query_count <= ref_block or query_count % ref_block != 0:
        return attend(query_part, key_part, value_part, key_valid)
    grouped = query_part.reshape(query_count // ref_block, ref_block, query_part.shape[1])

    def one_block(block_queries):
        return attend(block_queries, key_part, value_part, key_valid)

    mixed_out, log_total = lax.map(one_block, grouped)
    return mixed_out.reshape(query_count, HEADS, HEAD_DIM), log_total.reshape(query_count, HEADS)


def reference(query_tiles, key_tiles, value_tiles, slide_length):
    len_bound = slide_length[0]
    parts_out = []
    parts_lse = []
    for branch in range(BRANCHES):
        stride = 2 ** branch
        segment = min(SEG0 * stride, TOKENS) if branch < BRANCHES - 1 else TOKENS
        per_segment = segment // stride
        seg_count = TOKENS // segment
        shaped = [dilate(source, stride).reshape(seg_count, per_segment, HEADS * HEAD_DIM) for source in (query_tiles, key_tiles, value_tiles)]
        positions = (np.arange(TOKENS // stride)[:, None] * stride + offsets(stride)[None, :]).astype(np.int32)
        valid = (jnp.asarray(positions) < len_bound).reshape(seg_count, per_segment, HEADS)

        def one_segment(members):
            return attend_blocked(members[0], members[1], members[2], members[3])

        mixed_out, log_total = lax.map(one_segment, (shaped[0], shaped[1], shaped[2], valid))
        parts_out.append(spread(mixed_out.reshape(TOKENS // stride, HEADS, HEAD_DIM), stride, 0.0))
        parts_lse.append(spread(log_total.reshape(TOKENS // stride, HEADS, 1), stride, lse_fill))
    lse_peak = reduce(jnp.maximum, parts_lse)
    numerator = jnp.zeros((TOKENS, HEADS, HEAD_DIM), jnp.float32)
    denominator = jnp.zeros((TOKENS, HEADS, 1), jnp.float32)
    for branch in range(BRANCHES):
        factor = jnp.exp(parts_lse[branch] - lse_peak)
        numerator = numerator + factor * parts_out[branch]
        denominator = denominator + factor
    blended = (numerator / denominator).reshape(TOKENS, HEADS * HEAD_DIM)
    row_valid = jnp.arange(TOKENS, dtype=jnp.int32) < len_bound
    return jnp.where(row_valid[:, None], blended, 0.0).astype(jnp.bfloat16)
```

```python
import functools

import jax
import jax.numpy as jnp
import numpy as np
from jax import lax
from jax.experimental import pallas as pl
from jax.experimental.pallas import tpu as pltpu
from jax.sharding import PartitionSpec as P

HEADS = 12
HEAD_DIM = 64
WIDTH = 768
ROWS = 1024
RES = 16
GROUPS = ROWS // RES
HALF = GROUPS // 2
PAIRS = HEADS // 2
NX, NZ, NC = 4, 4, 2
MASKED = -1e30

BF = jnp.bfloat16
F32 = jnp.float32

ODD = [1, 3, 5, 7, 9, 11, 13, 15]
EVEN = [2, 6, 10, 14, 4, 12, 8, 0]
SHARED = [0, 8, 4, 12]
CLASS_U = {"A": ODD, "B": [2, 6, 10, 14], "C": [4, 12], "D": [8, 0]}
PAIR_OF = [0, 2, 3, 5]
LONE_OF = [2, 3, 8, 9]


def level(u):
    return 4 if u == 0 else min((u & -u).bit_length() - 1, 4)


def tables():
    lane = np.arange(256)
    ints = np.zeros((8, 256), np.int32)
    ints[0] = np.array(ODD)[lane // 32]
    ints[1] = np.array(EVEN)[lane // 32]
    ints[2] = lane % 32 * 16
    ints[3] = np.array(SHARED)[lane // 64]
    ints[4] = lane % 64 * 16
    ints[5] = np.array([0, 8, 0, 8])[lane // 64]
    even = np.array([level(u) for u in EVEN])[lane // 32]
    shared = np.array([level(u) for u in SHARED])[lane // 64]
    floats = np.zeros((8, 256), np.float32)
    floats[1] = np.log(1.0 + np.minimum(even, 1))
    floats[2] = np.log(1.0 + np.minimum(even, 2))
    floats[3] = np.log(1.0 + np.minimum(even, 3))
    floats[4] = np.log(1.0 * np.minimum(even, 2))
    floats[5] = np.log(1.0 * np.minimum(even, 3))
    floats[6] = np.log(np.minimum(shared, 3) - 1.0)
    return ints, floats


def swap_matrix():
    row = lax.broadcasted_iota(jnp.int32, (256, 256), 0)
    col = lax.broadcasted_iota(jnp.int32, (256, 256), 1)
    return jnp.where(((row & 15) * 16 + (row >> 4)) == col, 1.0, 0.0).astype(BF)


def lane_low(rows):
    return lax.broadcasted_iota(jnp.int32, (rows, 128), 1) < 64


def split_kernel(meta, q_ref, k_ref, v_ref, qt, kt, vt, sel, sel8, z0, z1, z2, z3, stage):
    step = pl.program_id(0)
    zpos = meta[1] // 2 % NZ
    swap = swap_matrix()
    for source, target in ((q_ref, qt), (k_ref, kt), (v_ref, vt)):
        for block in range(4):
            moved = jnp.dot(
                swap, source[block * 256 : (block + 1) * 256, :], preferred_element_type=F32
            ).astype(BF)
            for res in range(RES):
                target[res, block * 16 : (block + 1) * 16, :] = moved[res * 16 : (res + 1) * 16, :]
    low = lane_low(GROUPS)

    def picked(ref, u):
        return jnp.where(low, ref[(u + 2 * step) & 15], ref[(u + 2 * step + 1) & 15])

    for at, u in enumerate(SHARED):
        for kv, ref in enumerate((kt, vt)):
            rows = picked(ref, u)
            sel[at, kv] = rows
            if at < 2:
                sel8[at, kv] = rows
    q0, k0, v0 = picked(qt, 0), sel[0, 0], sel[0, 1]
    zero = jnp.zeros_like(q0)

    for group in range(NZ):
        slot = (group - zpos) & 3

        @pl.when(step == PAIR_OF[group])
        def _():
            stage[slot, :, 0:128] = q0
            stage[slot, :, 256:384] = k0
            stage[slot, :, 384:512] = v0

        @pl.when(step == LONE_OF[group] // 2)
        def _():
            def other(rows):
                return pltpu.roll(rows.astype(F32), 64, 1).astype(BF)

            if LONE_OF[group] % 2 == 0:
                lone_q, lone_k, lone_v = q0, k0, other(v0)
            else:
                lone_q, lone_k, lone_v = other(q0), other(k0), v0
            stage[slot, :, 128:256] = jnp.where(low, lone_q, zero)
            stage[slot, :, 512:640] = jnp.where(low, lone_k, lone_v)

    @pl.when(step == PAIRS - 1)
    def _():
        for slot, out in enumerate((z0, z1, z2, z3)):
            out[...] = stage[slot]


def softmax_parts(query, keys, values, biases):
    scores = [
        lax.dot_general(query, key, (((1,), (1,)), ((), ())), preferred_element_type=F32) + bias
        for key, bias in zip(keys, biases)
    ]
    peak = functools.reduce(jnp.maximum, scores)
    peak = jnp.max(peak, axis=1, keepdims=True)
    total = None
    for score, value in zip(scores, values):
        weight = jnp.exp(score - peak).astype(BF)
        part = jnp.dot(weight, value, preferred_element_type=F32)
        total = part if total is None else total + part
    return total, peak


def local_kernel(classes, meta, ints, floats, q_ref, k_ref, v_ref, *rest):
    far = classes == "CD"
    if far:
        sel, near, cross, before, out, o0, lse0 = rest
        out[...] = before[...]
    else:
        (out,) = rest
    bound = meta[0]
    device = meta[1]
    low = lane_low(256)
    for parity in range(2):
        head = 2 * pl.program_id(0) + parity
        mine = low if parity == 0 else jnp.logical_not(low)

        def gathered(ref, order, half):
            return jnp.concatenate(
                [ref[(u + head) & 15, half * HALF : (half + 1) * HALF, :] for u in order], axis=0
            )

        def widened(value):
            return jnp.where(mine, value, jnp.ones_like(value))

        def bias(kind, place, device_of, offset, row):
            position = (
                device_of * ROWS
                + offset
                + ints[place : place + 1, :]
                + ((ints[kind : kind + 1, :] + head) & 15)
            )
            return jnp.where(position < bound, floats[row : row + 1, :], MASKED)

        odd_k = [gathered(k_ref, ODD, half) for half in range(2)]
        even_k = [gathered(k_ref, EVEN, half) for half in range(2)]
        odd_v = [widened(gathered(v_ref, ODD, half)) for half in range(2)]
        even_v = [widened(gathered(v_ref, EVEN, half)) for half in range(2)]
        if far:
            pair_k = sel[:, 0].reshape(256, 128)
            pair_v = widened(sel[:, 1].reshape(256, 128))
            next_k = jnp.concatenate([near[0, 0], near[1, 0], cross[0, 0], cross[1, 0]], axis=0)
            next_v = widened(
                jnp.concatenate([near[0, 1], near[1, 1], cross[0, 1], cross[1, 1]], axis=0)
            )
            lane = lax.broadcasted_iota(jnp.int32, (1, 256), 1)
            next_device = jnp.where(lane < 128, device ^ 2, device ^ 3)
        for half in range(2):
            own = half * 512
            away = 512 - own
            for name in classes:
                order = CLASS_U[name]
                query = gathered(q_ref, order, half)
                count = query.shape[0]
                query = jnp.where(mine[:count], query, jnp.zeros_like(query)) * 0.125
                query = query.astype(BF)
                keys = [odd_k[half], even_k[half]]
                values = [odd_v[half], even_v[half]]
                cap = "ABCD".index(name)
                biases = [bias(0, 2, device, own, 0), bias(1, 2, device, own, cap)]
                if cap >= 1:
                    keys.append(even_k[1 - half])
                    values.append(even_v[1 - half])
                    biases.append(bias(1, 2, device, away, (0, 0, 4, 5)[cap]))
                if cap >= 2:
                    keys.append(pair_k)
                    values.append(pair_v)
                    biases.append(bias(3, 4, device ^ 1, 0, (0, 0, 0, 6)[cap]))
                if cap >= 3:
                    keys.append(next_k)
                    values.append(next_v)
                    biases.append(bias(5, 4, next_device, 0, 0))
                total, peak = softmax_parts(query, keys, values, biases)
                sums = pltpu.roll(total, 64, 1)
                result = total / sums
                rounded = result.astype(BF)
                for at, u in enumerate(order):
                    spot = ((u + head) & 15, slice(half * HALF, (half + 1) * HALF), slice(None))
                    out[spot] = jnp.where(
                        mine[:HALF], rounded[at * HALF : (at + 1) * HALF, :], out[spot]
                    )
                if name == "D":
                    rows = slice(half * HALF, (half + 1) * HALF)
                    log_total = peak[HALF:] + jnp.log(sums[HALF:])
                    o0[rows, :] = jnp.where(mine[:HALF], result[HALF:], o0[rows, :])
                    lse0[rows, :] = jnp.where(mine[:HALF], log_total, lse0[rows, :])


def far_kernel(meta, a0, a1, a2, a3, *rest):
    blocks, outs = rest[:8], rest[8:]
    bound = meta[0]
    device = meta[1]
    xpos, zpos, core = device // 8, device // 2 % NZ, device % 2
    low256 = lane_low(256)
    group = zpos
    lane = lax.broadcasted_iota(jnp.int32, (1, 256), 1)
    part = lane >> 6
    pair = jnp.where(group == 0, 0, jnp.where(group == 1, 4, jnp.where(group == 2, 6, 10)))
    lone = jnp.where(group == 0, 2, jnp.where(group == 1, 3, jnp.where(group == 2, 8, 9)))
    results = []
    for which in range(3):
        head = (pair, pair + 1, lone)[which]
        if which < 2:
            mine = low256 if which == 0 else jnp.logical_not(low256)
        else:
            mine = jnp.logical_not(low256)
        keys, values, biases = [], [], []
        for at, block in enumerate(blocks):
            from_x = (xpos - at % 4) & 3
            from_c = core if at < 4 else 1 - core
            from_z = (zpos - part) & 3
            position = ((from_x * NZ + from_z) * NC + from_c) * ROWS + (lane & 63) * 16 + head
            biases.append(jnp.where(position < bound, 0.0, MASKED))
            if which < 2:
                keys.append(block[:, 0:128])
                value = block[:, 128:256]
            else:
                keys.append(block[:, 256:384])
                value = block[:, 256:384]
            values.append(jnp.where(mine, value, jnp.ones_like(value)))
        parts = []
        for source in (a0, a1, a2, a3):
            if which < 2:
                query = jnp.where(mine[:64], source[:, 0:128], jnp.zeros((64, 128), BF))
            else:
                query = source[:, 128:256]
            query = (query * 0.125).astype(BF)
            total, peak = softmax_parts(query, keys, values, biases)
            sums = pltpu.roll(total, 64, 1)
            parts.append((total / sums, peak + jnp.log(sums), peak + jnp.log(total)))
        results.append(parts)
    low = low256[:64]
    for at, out in enumerate(outs):
        first, second, third = (results[which][at] for which in range(3))
        out[:, 0:128] = jnp.where(low, first[0], second[0])
        out[:, 128:256] = jnp.where(low, third[2], third[0])
        out[:, 256:384] = jnp.where(low, first[1], second[1])


def merge_kernel(meta, mixed, o0, lse0, r0, r1, r2, r3, out, stage, grid_rows):
    bound = meta[0]
    device = meta[1]
    zpos = device // 2 % NZ
    for slot, ref in enumerate((r0, r1, r2, r3)):
        stage[slot] = ref[...]
    low = lane_low(GROUPS)
    for pair in range(PAIRS):
        lanes = slice(pair * 128, pair * 128 + 128)
        if pair in PAIR_OF:
            slot = (PAIR_OF.index(pair) - zpos) & 3
            away, away_lse = stage[slot, :, 0:128], stage[slot, :, 256:384]
        else:
            first = LONE_OF.index(2 * pair)
            left = stage[(first - zpos) & 3, :, 128:256]
            right = stage[(first + 1 - zpos) & 3, :, 128:256]
            away = jnp.where(low, pltpu.roll(left, 64, 1), right)
            away_lse = jnp.where(low, left, pltpu.roll(right, 64, 1))
        here, here_lse = o0[:, lanes], lse0[:, lanes]
        top = jnp.maximum(here_lse, away_lse)
        weight = jnp.exp(here_lse - top)
        away_weight = jnp.exp(away_lse - top)
        blended = (here * weight + away * away_weight) / (weight + away_weight)
        blended = blended.astype(BF)
        for res in range(RES):
            rows = mixed[res, :, lanes]
            if res == 2 * pair:
                rows = jnp.where(low, blended, rows)
            if res == 2 * pair + 1:
                rows = jnp.where(low, rows, blended)
            for block in range(4):
                grid_rows[block, res * 16 : (res + 1) * 16, lanes] = rows[
                    block * 16 : (block + 1) * 16, :
                ]
    swap = swap_matrix()
    index = lax.broadcasted_iota(jnp.int32, (256, WIDTH), 0)
    for block in range(4):
        rows = jnp.dot(swap, grid_rows[block], preferred_element_type=F32)
        position = device * ROWS + block * 256 + index
        out[block * 256 : (block + 1) * 256, :] = jnp.where(position < bound, rows, 0.0).astype(BF)


def smem():
    return pl.BlockSpec(memory_space=pltpu.SMEM)


def vmem():
    return pl.BlockSpec(memory_space=pltpu.VMEM)


def whole(shape):
    return pl.BlockSpec(shape, lambda i: (0,) * len(shape))


def params(mib):
    return pltpu.CompilerParams(vmem_limit_bytes=mib * 1024 * 1024)


def shape(dims, dtype=BF):
    return jax.ShapeDtypeStruct(dims, dtype)


def by_residue():
    return pl.BlockSpec((RES, GROUPS, 128), lambda i: (0, 0, i))


def by_part(parts):
    return pl.BlockSpec((parts, 2, GROUPS, 128), lambda i: (0, 0, 0, i))


def flat(block):
    return pl.BlockSpec((GROUPS, 128), lambda i: (0, i))


def split(meta, q, k, v):
    rows = pl.BlockSpec((ROWS, 128), lambda i: (0, i))
    return pl.pallas_call(
        split_kernel,
        grid=(PAIRS,),
        in_specs=[smem(), rows, rows, rows],
        out_specs=[by_residue()] * 3 + [by_part(4), by_part(2)] + [whole((GROUPS, 640))] * 4,
        out_shape=[shape((RES, GROUPS, WIDTH))] * 3
        + [shape((4, 2, GROUPS, WIDTH)), shape((2, 2, GROUPS, WIDTH))]
        + [shape((GROUPS, 640))] * 4,
        scratch_shapes=[pltpu.VMEM((4, GROUPS, 640), BF)],
        compiler_params=params(40),
        name="split_rows",
    )(meta, q, k, v)


def local_near(meta, ints, floats, q, k, v):
    return pl.pallas_call(
        functools.partial(local_kernel, "AB"),
        grid=(PAIRS,),
        in_specs=[smem(), whole((8, 256)), whole((8, 256))] + [by_residue()] * 3,
        out_specs=by_residue(),
        out_shape=shape((RES, GROUPS, WIDTH)),
        compiler_params=params(40),
        cost_estimate=pl.CostEstimate(flops=3000000000, bytes_accessed=6000000, transcendentals=6000000),
        name="near_queries",
    )(meta, ints, floats, q, k, v)


def local_far(meta, ints, floats, q, k, v, sel, near, cross, before):
    return pl.pallas_call(
        functools.partial(local_kernel, "CD"),
        grid=(PAIRS,),
        in_specs=[smem(), whole((8, 256)), whole((8, 256))]
        + [by_residue()] * 3
        + [by_part(4), by_part(2), by_part(2), by_residue()],
        out_specs=[by_residue(), flat(None), flat(None)],
        out_shape=[
            shape((RES, GROUPS, WIDTH)),
            shape((GROUPS, WIDTH), F32),
            shape((GROUPS, WIDTH), F32),
        ],
        compiler_params=params(40),
        cost_estimate=pl.CostEstimate(flops=2000000000, bytes_accessed=9000000, transcendentals=4000000),
        name="wide_queries",
    )(meta, ints, floats, q, k, v, sel, near, cross, before)


def slide_wide(meta, queries, blocks):
    return pl.pallas_call(
        far_kernel,
        in_specs=[smem()] + [vmem()] * 12,
        out_specs=[vmem()] * 4,
        out_shape=[shape((GROUPS, 384), F32)] * 4,
        compiler_params=params(40),
        cost_estimate=pl.CostEstimate(flops=800000000, bytes_accessed=2000000, transcendentals=1600000),
        name="slide_queries",
    )(meta, *queries, *blocks)


def merge(meta, mixed, o0, lse0, back):
    return pl.pallas_call(
        merge_kernel,
        in_specs=[smem()] + [vmem()] * 7,
        out_specs=vmem(),
        out_shape=shape((ROWS, WIDTH)),
        scratch_shapes=[
            pltpu.VMEM((4, GROUPS, 384), F32),
            pltpu.VMEM((4, 256, WIDTH), BF),
        ],
        compiler_params=params(40),
        name="merge_rows",
    )(meta, mixed, o0, lse0, *back)


def at(x, z, c):
    return (x % NX * NZ + z % NZ) * NC + c


def move(block, to):
    route = [
        (at(x, z, c), at(*to(x, z, c))) for x in range(NX) for z in range(NZ) for c in range(NC)
    ]
    return lax.ppermute(block, "seq", route)


def along_x(steps):
    return lambda x, z, c: (x + steps, z, c)


def along_z(steps):
    return lambda x, z, c: (x, z + steps, c)


def other_core(x, z, c):
    return (x, z, 1 - c)


def next_chip(x, z, c):
    return (x, z ^ 1, c)


def per_device(query_tiles, key_tiles, value_tiles, slide_length):
    device = lax.axis_index("seq").astype(jnp.int32)
    meta = jnp.stack([slide_length[0], device])
    ints, floats = (jnp.asarray(table) for table in tables())
    qt, kt, vt, sel, sel8, z0, z1, z2, z3 = split(meta, query_tiles, key_tiles, value_tiles)
    slabs = [z0] + [move(slab, along_z(step)) for step, slab in ((1, z1), (2, z2), (3, z3))]
    near = move(sel8, next_chip)
    pair = move(sel, other_core)
    mixed = local_near(meta, ints, floats, qt, kt, vt)
    own = jnp.concatenate([slab[:, 256:640] for slab in slabs], axis=0)
    blocks = [own] + [move(own, along_x(step)) for step in (1, 2, 3)]
    cross = move(near, other_core)
    blocks += [move(block, other_core) for block in blocks]
    mixed, o0, lse0 = local_far(meta, ints, floats, qt, kt, vt, pair, near, cross, mixed)
    back = slide_wide(meta, [slab[:, 0:256] for slab in slabs], blocks)
    back = [back[0]] + [move(back[step], along_z(-step)) for step in (1, 2, 3)]
    return merge(meta, mixed, o0, lse0, back)


def solution(mesh):
    placed = (
        P(("slide", "seq"), None),
        P(("slide", "seq"), None),
        P(("slide", "seq"), None),
        P("slide"),
    )
    return jax.shard_map(
        per_device, mesh=mesh, in_specs=placed, out_specs=P(("slide", "seq"), None), check_vma=False
    )
```

```python
import functools

import jax
import jax.numpy as jnp
import numpy as np
from jax import lax
from jax.experimental import pallas as pl
from jax.experimental.pallas import tpu as pltpu
from jax.sharding import PartitionSpec as P

HEADS = 12
HEAD_DIM = 64
WIDTH = 768
ROWS = 1024
RES = 16
GROUPS = ROWS // RES
HALF = GROUPS // 2
PAIRS = HEADS // 2
NX, NZ, NC = 4, 4, 2
MASKED = -1e30

BF = jnp.bfloat16
F32 = jnp.float32

ODD = [1, 3, 5, 7, 9, 11, 13, 15]
EVEN = [2, 6, 10, 14, 4, 12, 8, 0]
SHARED = [0, 8, 4, 12]
CLASS_U = {"A": ODD, "B": [2, 6, 10, 14], "C": [4, 12], "D": [8, 0]}
PAIR_OF = [0, 2, 3, 5]
LONE_OF = [2, 3, 8, 9]


def level(u):
    return 4 if u == 0 else min((u & -u).bit_length() - 1, 4)


def tables():
    lane = np.arange(256)
    ints = np.zeros((8, 256), np.int32)
    ints[0] = np.array(ODD)[lane // 32]
    ints[1] = np.array(EVEN)[lane // 32]
    ints[2] = lane % 32 * 16
    ints[3] = np.array(SHARED)[lane // 64]
    ints[4] = lane % 64 * 16
    ints[5] = np.array([0, 8, 0, 8])[lane // 64]
    even = np.array([level(u) for u in EVEN])[lane // 32]
    shared = np.array([level(u) for u in SHARED])[lane // 64]
    floats = np.zeros((8, 256), np.float32)
    floats[1] = np.log(1.0 + np.minimum(even, 1))
    floats[2] = np.log(1.0 + np.minimum(even, 2))
    floats[3] = np.log(1.0 + np.minimum(even, 3))
    floats[4] = np.log(1.0 * np.minimum(even, 2))
    floats[5] = np.log(1.0 * np.minimum(even, 3))
    floats[6] = np.log(np.minimum(shared, 3) - 1.0)
    return ints, floats


def swap_matrix():
    row = lax.broadcasted_iota(jnp.int32, (256, 256), 0)
    col = lax.broadcasted_iota(jnp.int32, (256, 256), 1)
    return jnp.where(((row & 15) * 16 + (row >> 4)) == col, 1.0, 0.0).astype(BF)


def lane_low(rows):
    return lax.broadcasted_iota(jnp.int32, (rows, 128), 1) < 64


def split_kernel(meta, q_ref, k_ref, v_ref, qt, kt, vt, sel, sel8, z0, z1, z2, z3, stage):
    step = pl.program_id(0)
    zpos = meta[1] // 2 % NZ
    swap = swap_matrix()
    for source, target in ((q_ref, qt), (k_ref, kt), (v_ref, vt)):
        for block in range(4):
            moved = jnp.dot(
                swap, source[block * 256 : (block + 1) * 256, :], preferred_element_type=F32
            ).astype(BF)
            for res in range(RES):
                target[res, block * 16 : (block + 1) * 16, :] = moved[res * 16 : (res + 1) * 16, :]
    low = lane_low(GROUPS)

    def picked(ref, u):
        return jnp.where(low, ref[(u + 2 * step) & 15], ref[(u + 2 * step + 1) & 15])

    for at, u in enumerate(SHARED):
        for kv, ref in enumerate((kt, vt)):
            rows = picked(ref, u)
            sel[at, kv] = rows
            if at < 2:
                sel8[at, kv] = rows
    q0, k0, v0 = picked(qt, 0), sel[0, 0], sel[0, 1]
    zero = jnp.zeros_like(q0)

    for group in range(NZ):
        slot = (group - zpos) & 3

        @pl.when(step == PAIR_OF[group])
        def _():
            stage[slot, :, 0:128] = q0
            stage[slot, :, 256:384] = k0
            stage[slot, :, 384:512] = v0

        @pl.when(step == LONE_OF[group] // 2)
        def _():
            def other(rows):
                return pltpu.roll(rows.astype(F32), 64, 1).astype(BF)

            if LONE_OF[group] % 2 == 0:
                lone_q, lone_k, lone_v = q0, k0, other(v0)
            else:
                lone_q, lone_k, lone_v = other(q0), other(k0), v0
            stage[slot, :, 128:256] = jnp.where(low, lone_q, zero)
            stage[slot, :, 512:640] = jnp.where(low, lone_k, lone_v)

    @pl.when(step == PAIRS - 1)
    def _():
        for slot, out in enumerate((z0, z1, z2, z3)):
            out[...] = stage[slot]


def softmax_parts(query, keys, values, biases):
    scores = [
        lax.dot_general(query, key, (((1,), (1,)), ((), ())), preferred_element_type=F32) + bias
        for key, bias in zip(keys, biases)
    ]
    peak = functools.reduce(jnp.maximum, scores)
    peak = jnp.max(peak, axis=1, keepdims=True)
    total = None
    for score, value in zip(scores, values):
        weight = jnp.exp(score - peak).astype(BF)
        part = jnp.dot(weight, value, preferred_element_type=F32)
        total = part if total is None else total + part
    return total, peak


def local_kernel(classes, first, many, meta, ints, floats, *refs):
    def body(step, carry):
        lanes = pl.ds(pl.multiple_of((first + step) * 128, 128), 128)
        here = pl.ds(pl.multiple_of(step * 128, 128), 128)
        views = [ref.at[:, :, lanes] for ref in refs[:3]]
        if classes == "CD":
            views += [ref.at[:, :, :, lanes] for ref in refs[3:6]]
            views += [ref.at[:, :, here] for ref in refs[6:8]]
            views += [ref.at[:, here] for ref in refs[8:10]]
        else:
            views += [refs[3].at[:, :, here]]
        local_pair(classes, first + step, meta, ints, floats, *views)
        return carry

    lax.fori_loop(0, many, body, 0)


def local_pair(classes, pair, meta, ints, floats, q_ref, k_ref, v_ref, *rest):
    far = classes == "CD"
    if far:
        sel, near, cross, before, out, o0, lse0 = rest
        out[...] = before[...]
    else:
        (out,) = rest
    bound = meta[0]
    device = meta[1]
    low = lane_low(256)
    low_all = lane_low(256 if far else 768)
    high_all = jnp.logical_not(low_all)
    for parity in range(2):
        head = 2 * pair + parity
        mine = low if parity == 0 else jnp.logical_not(low)

        def gathered(ref, order, half):
            return jnp.concatenate(
                [ref[(u + head) & 15, half * HALF : (half + 1) * HALF, :] for u in order], axis=0
            )

        def widened(value):
            return jnp.where(mine, value, jnp.ones_like(value))

        def bias(kind, place, device_of, offset, row):
            position = (
                device_of * ROWS
                + offset
                + ints[place : place + 1, :]
                + ((ints[kind : kind + 1, :] + head) & 15)
            )
            return jnp.where(position < bound, floats[row : row + 1, :], MASKED)

        odd_k = [gathered(k_ref, ODD, half) for half in range(2)]
        even_k = [gathered(k_ref, EVEN, half) for half in range(2)]
        odd_v = [widened(gathered(v_ref, ODD, half)) for half in range(2)]
        even_v = [widened(gathered(v_ref, EVEN, half)) for half in range(2)]
        if far:
            pair_k = sel[:, 0].reshape(256, 128)
            pair_v = widened(sel[:, 1].reshape(256, 128))
            next_k = jnp.concatenate([near[0, 0], near[1, 0], cross[0, 0], cross[1, 0]], axis=0)
            next_v = widened(
                jnp.concatenate([near[0, 1], near[1, 1], cross[0, 1], cross[1, 1]], axis=0)
            )
            lane = lax.broadcasted_iota(jnp.int32, (1, 256), 1)
            next_device = jnp.where(lane < 128, device ^ 2, device ^ 3)
        groups = [(name, 0) for name in classes] + [(name, 1) for name in classes[::-1]]
        tiles = []
        for half in range(2):
            tiles.append((odd_k[half], odd_v[half], lambda cap, side, half=half: side == half))
            tiles.append(
                (even_k[half], even_v[half], lambda cap, side, half=half: side == half or cap >= 1)
            )
        if far:
            tiles.append((pair_k, pair_v, lambda cap, side: True))
            tiles.append((next_k, next_v, lambda cap, side: cap >= 3))

        def tile_bias(tile, cap, side):
            if tile >= 4:
                if tile == 5:
                    return bias(5, 4, next_device, 0, 0)
                return bias(3, 4, device ^ 1, 0, (0, 0, 0, 6)[cap])
            offset = tile // 2 * 512
            if tile % 2 == 0:
                return bias(0, 2, device, offset, 0)
            row = cap if tile // 2 == side else (0, 0, 4, 5)[cap]
            return bias(1, 2, device, offset, row)

        pieces, starts, count = [], [], 0
        for name, side in groups:
            pieces.append(gathered(q_ref, CLASS_U[name], side))
            starts.append(count)
            count += pieces[-1].shape[0]
        starts.append(count)
        query = jnp.concatenate(pieces, axis=0)
        query = (jnp.where(low_all if parity == 0 else high_all, query, jnp.zeros_like(query)) * 0.125).astype(BF)
        caps = [("ABCD".index(name), side) for name, side in groups]
        scores, spans = [], []
        for key, value, member in tiles:
            inside = [at for at, (cap, side) in enumerate(caps) if member(cap, side)]
            first, last = inside[0], inside[-1] + 1
            spans.append((first, last))
            scores.append(
                lax.dot_general(
                    query[starts[first] : starts[last]],
                    key,
                    (((1,), (1,)), ((), ())),
                    preferred_element_type=F32,
                )
            )
        weights = [[] for _ in tiles]
        peaks = []
        for at, (cap, side) in enumerate(caps):
            held = []
            for tile, (first, last) in enumerate(spans):
                if first <= at < last:
                    base = starts[first]
                    held.append(
                        (
                            tile,
                            scores[tile][starts[at] - base : starts[at + 1] - base]
                            + tile_bias(tile, cap, side),
                        )
                    )
            peak = functools.reduce(jnp.maximum, [score for _, score in held])
            peak = jnp.max(peak, axis=1, keepdims=True)
            peaks.append(peak)
            for tile, score in held:
                weights[tile].append(jnp.exp(score - peak).astype(BF))
        totals = [None] * len(caps)
        for tile, (first, last) in enumerate(spans):
            part = jnp.dot(
                jnp.concatenate(weights[tile], axis=0), tiles[tile][1], preferred_element_type=F32
            )
            for at in range(first, last):
                rows = part[starts[at] - starts[first] : starts[at + 1] - starts[first]]
                totals[at] = rows if totals[at] is None else totals[at] + rows
        for at, (name, half) in enumerate(groups):
            total, peak = totals[at], peaks[at]
            sums = pltpu.roll(total, 64, 1)
            result = total / sums
            rounded = result.astype(BF)
            for row, u in enumerate(CLASS_U[name]):
                spot = ((u + head) & 15, slice(half * HALF, (half + 1) * HALF), slice(None))
                out[spot] = jnp.where(
                    mine[:HALF], rounded[row * HALF : (row + 1) * HALF, :], out[spot]
                )
            if name == "D":
                rows = slice(half * HALF, (half + 1) * HALF)
                log_total = peak[HALF:] + jnp.log(sums[HALF:])
                o0[rows, :] = jnp.where(mine[:HALF], result[HALF:], o0[rows, :])
                lse0[rows, :] = jnp.where(mine[:HALF], log_total, lse0[rows, :])


def far_kernel(meta, a0, a1, a2, a3, *rest):
    blocks, outs = rest[:8], rest[8:]
    bound = meta[0]
    device = meta[1]
    xpos, zpos, core = device // 8, device // 2 % NZ, device % 2
    low256 = lane_low(256)
    group = zpos
    lane = lax.broadcasted_iota(jnp.int32, (1, 256), 1)
    part = lane >> 6
    pair = jnp.where(group == 0, 0, jnp.where(group == 1, 4, jnp.where(group == 2, 6, 10)))
    lone = jnp.where(group == 0, 2, jnp.where(group == 1, 3, jnp.where(group == 2, 8, 9)))
    results = []
    for which in range(3):
        head = (pair, pair + 1, lone)[which]
        if which < 2:
            mine = low256 if which == 0 else jnp.logical_not(low256)
        else:
            mine = jnp.logical_not(low256)
        keys, values, biases = [], [], []
        for at, block in enumerate(blocks):
            from_x = (xpos - at % 4) & 3
            from_c = core if at < 4 else 1 - core
            from_z = (zpos - part) & 3
            position = ((from_x * NZ + from_z) * NC + from_c) * ROWS + (lane & 63) * 16 + head
            biases.append(jnp.where(position < bound, 0.0, MASKED))
            if which < 2:
                keys.append(block[:, 0:128])
                value = block[:, 128:256]
            else:
                keys.append(block[:, 256:384])
                value = block[:, 256:384]
            values.append(jnp.where(mine, value, jnp.ones_like(value)))
        parts = []
        for source in (a0, a1, a2, a3):
            if which < 2:
                query = jnp.where(mine[:64], source[:, 0:128], jnp.zeros((64, 128), BF))
            else:
                query = source[:, 128:256]
            query = (query * 0.125).astype(BF)
            total, peak = softmax_parts(query, keys, values, biases)
            sums = pltpu.roll(total, 64, 1)
            parts.append((total / sums, peak + jnp.log(sums), peak + jnp.log(total)))
        results.append(parts)
    low = low256[:64]
    for at, out in enumerate(outs):
        first, second, third = (results[which][at] for which in range(3))
        out[:, 0:128] = jnp.where(low, first[0], second[0])
        out[:, 128:256] = jnp.where(low, third[2], third[0])
        out[:, 256:384] = jnp.where(low, first[1], second[1])


def merge_kernel(meta, *refs):
    mixed, o0, lse0 = refs[0:2], refs[2:4], refs[4:6]
    r0, r1, r2, r3, out, stage, grid_rows = refs[6:]
    bound = meta[0]
    device = meta[1]
    zpos = device // 2 % NZ
    for slot, ref in enumerate((r0, r1, r2, r3)):
        stage[slot] = ref[...]
    low = lane_low(GROUPS)
    for pair in range(PAIRS):
        lanes = slice(pair * 128, pair * 128 + 128)
        piece, inner = pair // 3, slice(pair % 3 * 128, pair % 3 * 128 + 128)
        if pair in PAIR_OF:
            slot = (PAIR_OF.index(pair) - zpos) & 3
            away, away_lse = stage[slot, :, 0:128], stage[slot, :, 256:384]
        else:
            first = LONE_OF.index(2 * pair)
            left = stage[(first - zpos) & 3, :, 128:256]
            right = stage[(first + 1 - zpos) & 3, :, 128:256]
            away = jnp.where(low, pltpu.roll(left, 64, 1), right)
            away_lse = jnp.where(low, left, pltpu.roll(right, 64, 1))
        here, here_lse = o0[piece][:, inner], lse0[piece][:, inner]
        top = jnp.maximum(here_lse, away_lse)
        weight = jnp.exp(here_lse - top)
        away_weight = jnp.exp(away_lse - top)
        blended = (here * weight + away * away_weight) / (weight + away_weight)
        blended = blended.astype(BF)
        for res in range(RES):
            rows = mixed[piece][res, :, inner]
            if res == 2 * pair:
                rows = jnp.where(low, blended, rows)
            if res == 2 * pair + 1:
                rows = jnp.where(low, rows, blended)
            for block in range(4):
                grid_rows[block, res * 16 : (res + 1) * 16, lanes] = rows[
                    block * 16 : (block + 1) * 16, :
                ]
    swap = swap_matrix()
    index = lax.broadcasted_iota(jnp.int32, (256, WIDTH), 0)
    for block in range(4):
        rows = jnp.dot(swap, grid_rows[block], preferred_element_type=F32)
        position = device * ROWS + block * 256 + index
        out[block * 256 : (block + 1) * 256, :] = jnp.where(position < bound, rows, 0.0).astype(BF)


def smem():
    return pl.BlockSpec(memory_space=pltpu.SMEM)


def vmem():
    return pl.BlockSpec(memory_space=pltpu.VMEM)


def whole(shape):
    return pl.BlockSpec(shape, lambda i: (0,) * len(shape))


def params(mib):
    return pltpu.CompilerParams(vmem_limit_bytes=mib * 1024 * 1024)


def shape(dims, dtype=BF):
    return jax.ShapeDtypeStruct(dims, dtype)


def by_residue():
    return pl.BlockSpec((RES, GROUPS, 128), lambda i: (0, 0, i))


def by_part(parts):
    return pl.BlockSpec((parts, 2, GROUPS, 128), lambda i: (0, 0, 0, i))


def flat(block):
    return pl.BlockSpec((GROUPS, 128), lambda i: (0, i))


def split(meta, q, k, v):
    rows = pl.BlockSpec((ROWS, 128), lambda i: (0, i))
    return pl.pallas_call(
        split_kernel,
        grid=(PAIRS,),
        in_specs=[smem(), rows, rows, rows],
        out_specs=[by_residue()] * 3 + [by_part(4), by_part(2)] + [whole((GROUPS, 640))] * 4,
        out_shape=[shape((RES, GROUPS, WIDTH))] * 3
        + [shape((4, 2, GROUPS, WIDTH)), shape((2, 2, GROUPS, WIDTH))]
        + [shape((GROUPS, 640))] * 4,
        scratch_shapes=[pltpu.VMEM((4, GROUPS, 640), BF)],
        compiler_params=params(40),
        name="split_rows",
    )(meta, q, k, v)


def local_near(first, many, meta, ints, floats, q, k, v):
    return pl.pallas_call(
        functools.partial(local_kernel, "AB", first, many),
        in_specs=[smem()] + [vmem()] * 5,
        out_specs=vmem(),
        out_shape=shape((RES, GROUPS, many * 128)),
        compiler_params=params(40),
        cost_estimate=pl.CostEstimate(
            flops=many * 500000000, bytes_accessed=1000000, transcendentals=many * 900000
        ),
        name="near_queries",
    )(meta, ints, floats, q, k, v)


def local_far(first, many, meta, ints, floats, q, k, v, sel, near, cross, before):
    return pl.pallas_call(
        functools.partial(local_kernel, "CD", first, many),
        in_specs=[smem()] + [vmem()] * 9,
        out_specs=[vmem()] * 3,
        out_shape=[
            shape((RES, GROUPS, many * 128)),
            shape((GROUPS, many * 128), F32),
            shape((GROUPS, many * 128), F32),
        ],
        compiler_params=params(40),
        cost_estimate=pl.CostEstimate(
            flops=many * 400000000, bytes_accessed=1000000, transcendentals=many * 600000
        ),
        name="wide_queries",
    )(meta, ints, floats, q, k, v, sel, near, cross, before)


def slide_wide(meta, queries, blocks):
    return pl.pallas_call(
        far_kernel,
        in_specs=[smem()] + [vmem()] * 12,
        out_specs=[vmem()] * 4,
        out_shape=[shape((GROUPS, 384), F32)] * 4,
        compiler_params=params(40),
        cost_estimate=pl.CostEstimate(flops=800000000, bytes_accessed=2000000, transcendentals=1600000),
        name="slide_queries",
    )(meta, *queries, *blocks)


def merge(meta, mixed, o0, lse0, back):
    return pl.pallas_call(
        merge_kernel,
        in_specs=[smem()] + [vmem()] * 10,
        out_specs=vmem(),
        out_shape=shape((ROWS, WIDTH)),
        scratch_shapes=[
            pltpu.VMEM((4, GROUPS, 384), F32),
            pltpu.VMEM((4, 256, WIDTH), BF),
        ],
        compiler_params=params(40),
        name="merge_rows",
    )(meta, *mixed, *o0, *lse0, *back)


def at(x, z, c):
    return (x % NX * NZ + z % NZ) * NC + c


def move(block, to):
    route = [
        (at(x, z, c), at(*to(x, z, c))) for x in range(NX) for z in range(NZ) for c in range(NC)
    ]
    return lax.ppermute(block, "seq", route)


def along_x(steps):
    return lambda x, z, c: (x + steps, z, c)


def along_z(steps):
    return lambda x, z, c: (x, z + steps, c)


def other_core(x, z, c):
    return (x, z, 1 - c)


def next_chip(x, z, c):
    return (x, z ^ 1, c)


def per_device(query_tiles, key_tiles, value_tiles, slide_length):
    device = lax.axis_index("seq").astype(jnp.int32)
    meta = jnp.stack([slide_length[0], device])
    ints, floats = (jnp.asarray(table) for table in tables())
    qt, kt, vt, sel, sel8, z0, z1, z2, z3 = split(meta, query_tiles, key_tiles, value_tiles)
    slabs = [z0] + [move(slab, along_z(step)) for step, slab in ((1, z1), (2, z2), (3, z3))]
    near = move(sel8, next_chip)
    pair = move(sel, other_core)
    local = (ints, floats, qt, kt, vt)
    mixed = [local_near(0, 3, meta, *local)]
    slabs, mixed[0] = lax.optimization_barrier((slabs, mixed[0]))
    own = jnp.concatenate([slab[:, 256:640] for slab in slabs], axis=0)
    own, later = lax.optimization_barrier((own, meta))
    moved = [move(own, along_x(step)) for step in (1, 2, 3)]
    cross = move(near, other_core)
    mixed.append(local_near(3, 3, later, *local))
    moved, mixed[1] = lax.optimization_barrier((moved, mixed[1]))
    blocks = [own] + moved
    blocks += [move(block, other_core) for block in blocks]
    moved, last = lax.optimization_barrier((moved, meta))
    wide = [local_far(0, 3, last, *local, pair, near, cross, mixed[0])]
    blocks, wide[0] = lax.optimization_barrier((blocks, wide[0]))
    back = slide_wide(meta, [slab[:, 0:256] for slab in slabs], blocks)
    back, last = lax.optimization_barrier((back, meta))
    back = [back[0]] + [move(back[step], along_z(-step)) for step in (1, 2, 3)]
    wide.append(local_far(3, 3, last, *local, pair, near, cross, mixed[1]))
    mixed, o0, lse0 = zip(*wide)
    return merge(meta, mixed, o0, lse0, back)


def solution(mesh):
    placed = (
        P(("slide", "seq"), None),
        P(("slide", "seq"), None),
        P(("slide", "seq"), None),
        P("slide"),
    )
    return jax.shard_map(
        per_device, mesh=mesh, in_specs=placed, out_specs=P(("slide", "seq"), None), check_vma=False
    )
```

```python
import functools

import jax
import jax.numpy as jnp
import numpy as np
from jax import lax
from jax.experimental import pallas as pl
from jax.experimental.pallas import tpu as pltpu
from jax.sharding import PartitionSpec as P

HEADS = 12
HEAD_DIM = 64
WIDTH = 768
ROWS = 1024
RES = 16
GROUPS = ROWS // RES
HALF = GROUPS // 2
PAIRS = HEADS // 2
NX, NZ, NC = 4, 4, 2
MASKED = -1e30

BF = jnp.bfloat16
F32 = jnp.float32

ODD = [1, 3, 5, 7, 9, 11, 13, 15]
EVEN = [2, 6, 10, 14, 4, 12, 8, 0]
SHARED = [0, 8, 4, 12]
CLASS_U = {"A": ODD, "B": [2, 6, 10, 14], "C": [4, 12], "D": [8, 0]}
PAIR_OF = [0, 2, 3, 5]
LONE_OF = [2, 3, 8, 9]
NEAR_PARTS = [(0, 2), (2, 3), (5, 1)]
WIDE_PARTS = [(0, 3), (3, 3)]


def level(u):
    return 4 if u == 0 else min((u & -u).bit_length() - 1, 4)


def tables():
    lane = np.arange(256)
    ints = np.zeros((8, 256), np.int32)
    ints[0] = np.array(ODD)[lane // 32]
    ints[1] = np.array(EVEN)[lane // 32]
    ints[2] = lane % 32 * 16
    ints[3] = np.array(SHARED)[lane // 64]
    ints[4] = lane % 64 * 16
    ints[5] = np.array([0, 8, 0, 8])[lane // 64]
    even = np.array([level(u) for u in EVEN])[lane // 32]
    shared = np.array([level(u) for u in SHARED])[lane // 64]
    floats = np.zeros((8, 256), np.float32)
    floats[1] = np.log(1.0 + np.minimum(even, 1))
    floats[2] = np.log(1.0 + np.minimum(even, 2))
    floats[3] = np.log(1.0 + np.minimum(even, 3))
    floats[4] = np.log(1.0 * np.minimum(even, 2))
    floats[5] = np.log(1.0 * np.minimum(even, 3))
    floats[6] = np.log(np.minimum(shared, 3) - 1.0)
    return ints, floats


def swap_matrix():
    row = lax.broadcasted_iota(jnp.int32, (256, 256), 0)
    col = lax.broadcasted_iota(jnp.int32, (256, 256), 1)
    return jnp.where(((row & 15) * 16 + (row >> 4)) == col, 1.0, 0.0).astype(BF)


def lane_low(rows):
    return lax.broadcasted_iota(jnp.int32, (rows, 128), 1) < 64


def reorder(source, target):
    swap = swap_matrix()
    for block in range(4):
        moved = jnp.dot(
            swap, source[block * 256 : (block + 1) * 256, :], preferred_element_type=F32
        ).astype(BF)
        for res in range(RES):
            target[res, block * 16 : (block + 1) * 16, :] = moved[res * 16 : (res + 1) * 16, :]


def split_kernel(meta, q_in, kt, vt, qt, sel, sel8, z0, z1, z2, z3, stage):
    reorder(q_in, qt)
    zpos = meta[1] // 2 % NZ
    low = lane_low(GROUPS)

    def other(rows):
        return pltpu.roll(rows.astype(F32), 64, 1).astype(BF)

    for pair in range(PAIRS):
        lanes = slice(pair * 128, pair * 128 + 128)

        def picked(ref, u):
            return jnp.where(
                low, ref[(u + 2 * pair) % RES, :, lanes], ref[(u + 2 * pair + 1) % RES, :, lanes]
            )

        for at, u in enumerate(SHARED):
            for kv, ref in enumerate((kt, vt)):
                rows = picked(ref, u)
                sel[at, kv, :, lanes] = rows
                if at < 2:
                    sel8[at, kv, :, lanes] = rows
                if at == 0 and kv == 0:
                    k0 = rows
                if at == 0 and kv == 1:
                    v0 = rows
        q0 = picked(qt, 0)
        for group in range(NZ):
            slot = (group - zpos) & 3
            if pair == PAIR_OF[group]:
                stage[slot, :, 0:128] = q0
                stage[slot, :, 256:384] = k0
                stage[slot, :, 384:512] = v0
            if pair == LONE_OF[group] // 2:
                if LONE_OF[group] % 2 == 0:
                    lone_q, lone_k, lone_v = q0, k0, other(v0)
                else:
                    lone_q, lone_k, lone_v = other(q0), other(k0), v0
                stage[slot, :, 128:256] = jnp.where(low, lone_q, jnp.zeros_like(lone_q))
                stage[slot, :, 512:640] = jnp.where(low, lone_k, lone_v)
    for slot, out in enumerate((z0, z1, z2, z3)):
        out[...] = stage[slot]


def softmax_parts(query, keys, values, biases):
    scores = [
        lax.dot_general(query, key, (((1,), (1,)), ((), ())), preferred_element_type=F32) + bias
        for key, bias in zip(keys, biases)
    ]
    peak = functools.reduce(jnp.maximum, scores)
    peak = jnp.max(peak, axis=1, keepdims=True)
    total = None
    for score, value in zip(scores, values):
        weight = jnp.exp(score - peak).astype(BF)
        part = jnp.dot(weight, value, preferred_element_type=F32)
        total = part if total is None else total + part
    return total, peak


def local_kernel(classes, first, many, meta, ints, floats, *refs):
    def body(step, carry):
        lanes = pl.ds(pl.multiple_of((first + step) * 128, 128), 128)
        here = pl.ds(pl.multiple_of(step * 128, 128), 128)
        views = [ref.at[:, :, lanes] for ref in refs[:3]]
        if classes == "CD":
            views += [ref.at[:, :, :, lanes] for ref in refs[3:6]]
            views += [refs[6].at[:, :, here]]
            views += [ref.at[:, here] for ref in refs[7:9]]
        else:
            views += [refs[3].at[:, :, here]]
        local_pair(classes, first + step, meta, ints, floats, *views)
        return carry

    lax.fori_loop(0, many, body, 0)


def local_pair(classes, pair, meta, ints, floats, q_ref, k_ref, v_ref, *rest):
    far = classes == "CD"
    if far:
        sel, near, cross, out, o0, lse0 = rest
    else:
        (out,) = rest
    bound = meta[0]
    device = meta[1]
    low = lane_low(256)
    low_all = lane_low(256 if far else 768)
    high_all = jnp.logical_not(low_all)
    for parity in range(2):
        head = 2 * pair + parity
        mine = low if parity == 0 else jnp.logical_not(low)

        def gathered(ref, order, half):
            return jnp.concatenate(
                [ref[(u + head) & 15, half * HALF : (half + 1) * HALF, :] for u in order], axis=0
            )

        def widened(value):
            return jnp.where(mine, value, jnp.ones_like(value))

        def bias(kind, place, device_of, offset, row):
            position = (
                device_of * ROWS
                + offset
                + ints[place : place + 1, :]
                + ((ints[kind : kind + 1, :] + head) & 15)
            )
            return jnp.where(position < bound, floats[row : row + 1, :], MASKED)

        odd_k = [gathered(k_ref, ODD, half) for half in range(2)]
        even_k = [gathered(k_ref, EVEN, half) for half in range(2)]
        odd_v = [widened(gathered(v_ref, ODD, half)) for half in range(2)]
        even_v = [widened(gathered(v_ref, EVEN, half)) for half in range(2)]
        if far:
            pair_k = sel[:, 0].reshape(256, 128)
            pair_v = widened(sel[:, 1].reshape(256, 128))
            next_k = jnp.concatenate([near[0, 0], near[1, 0], cross[0, 0], cross[1, 0]], axis=0)
            next_v = widened(
                jnp.concatenate([near[0, 1], near[1, 1], cross[0, 1], cross[1, 1]], axis=0)
            )
            lane = lax.broadcasted_iota(jnp.int32, (1, 256), 1)
            next_device = jnp.where(lane < 128, device ^ 2, device ^ 3)
        groups = [(name, 0) for name in classes] + [(name, 1) for name in classes[::-1]]
        tiles = []
        for half in range(2):
            tiles.append((odd_k[half], odd_v[half], lambda cap, side, half=half: side == half))
            tiles.append(
                (even_k[half], even_v[half], lambda cap, side, half=half: side == half or cap >= 1)
            )
        if far:
            tiles.append((pair_k, pair_v, lambda cap, side: True))
            tiles.append((next_k, next_v, lambda cap, side: cap >= 3))

        def tile_bias(tile, cap, side):
            if tile >= 4:
                if tile == 5:
                    return bias(5, 4, next_device, 0, 0)
                return bias(3, 4, device ^ 1, 0, (0, 0, 0, 6)[cap])
            offset = tile // 2 * 512
            if tile % 2 == 0:
                return bias(0, 2, device, offset, 0)
            row = cap if tile // 2 == side else (0, 0, 4, 5)[cap]
            return bias(1, 2, device, offset, row)

        pieces, starts, count = [], [], 0
        for name, side in groups:
            pieces.append(gathered(q_ref, CLASS_U[name], side))
            starts.append(count)
            count += pieces[-1].shape[0]
        starts.append(count)
        query = jnp.concatenate(pieces, axis=0)
        query = (jnp.where(low_all if parity == 0 else high_all, query, jnp.zeros_like(query)) * 0.125).astype(BF)
        caps = [("ABCD".index(name), side) for name, side in groups]
        scores, spans = [], []
        for key, value, member in tiles:
            inside = [at for at, (cap, side) in enumerate(caps) if member(cap, side)]
            first, last = inside[0], inside[-1] + 1
            spans.append((first, last))
            scores.append(
                lax.dot_general(
                    query[starts[first] : starts[last]],
                    key,
                    (((1,), (1,)), ((), ())),
                    preferred_element_type=F32,
                )
            )
        weights = [[] for _ in tiles]
        peaks = []
        for at, (cap, side) in enumerate(caps):
            held = []
            for tile, (first, last) in enumerate(spans):
                if first <= at < last:
                    base = starts[first]
                    held.append(
                        (
                            tile,
                            scores[tile][starts[at] - base : starts[at + 1] - base]
                            + tile_bias(tile, cap, side),
                        )
                    )
            peak = functools.reduce(jnp.maximum, [score for _, score in held])
            peak = jnp.max(peak, axis=1, keepdims=True)
            peaks.append(peak)
            for tile, score in held:
                weights[tile].append(jnp.exp(score - peak).astype(BF))
        totals = [None] * len(caps)
        for tile, (first, last) in enumerate(spans):
            part = jnp.dot(
                jnp.concatenate(weights[tile], axis=0), tiles[tile][1], preferred_element_type=F32
            )
            for at in range(first, last):
                rows = part[starts[at] - starts[first] : starts[at + 1] - starts[first]]
                totals[at] = rows if totals[at] is None else totals[at] + rows
        for at, (name, half) in enumerate(groups):
            total, peak = totals[at], peaks[at]
            sums = pltpu.roll(total, 64, 1)
            result = total / sums
            rounded = result.astype(BF)
            for row, u in enumerate(CLASS_U[name]):
                spot = ((u + head) & 15, slice(half * HALF, (half + 1) * HALF), slice(None))
                out[spot] = jnp.where(
                    mine[:HALF], rounded[row * HALF : (row + 1) * HALF, :], out[spot]
                )
            if name == "D":
                rows = slice(half * HALF, (half + 1) * HALF)
                log_total = peak[HALF:] + jnp.log(sums[HALF:])
                o0[rows, :] = jnp.where(mine[:HALF], result[HALF:], o0[rows, :])
                lse0[rows, :] = jnp.where(mine[:HALF], log_total, lse0[rows, :])


def far_kernel(meta, a0, a1, a2, a3, *rest):
    blocks, outs = rest[:8], rest[8:]
    bound = meta[0]
    device = meta[1]
    xpos, zpos, core = device // 8, device // 2 % NZ, device % 2
    low256 = lane_low(256)
    group = zpos
    lane = lax.broadcasted_iota(jnp.int32, (1, 256), 1)
    part = lane >> 6
    pair = jnp.where(group == 0, 0, jnp.where(group == 1, 4, jnp.where(group == 2, 6, 10)))
    lone = jnp.where(group == 0, 2, jnp.where(group == 1, 3, jnp.where(group == 2, 8, 9)))
    results = []
    for which in range(3):
        head = (pair, pair + 1, lone)[which]
        if which < 2:
            mine = low256 if which == 0 else jnp.logical_not(low256)
        else:
            mine = jnp.logical_not(low256)
        keys, values, biases = [], [], []
        for at, block in enumerate(blocks):
            from_x = (xpos - at % 4) & 3
            from_c = core if at < 4 else 1 - core
            from_z = (zpos - part) & 3
            position = ((from_x * NZ + from_z) * NC + from_c) * ROWS + (lane & 63) * 16 + head
            biases.append(jnp.where(position < bound, 0.0, MASKED))
            if which < 2:
                keys.append(block[:, 0:128])
                value = block[:, 128:256]
            else:
                keys.append(block[:, 256:384])
                value = block[:, 256:384]
            values.append(jnp.where(mine, value, jnp.ones_like(value)))
        lanes = slice(0, 128) if which < 2 else slice(128, 256)
        query = jnp.concatenate([source[:, lanes] for source in (a0, a1, a2, a3)], axis=0)
        if which < 2:
            query = jnp.where(mine, query, jnp.zeros_like(query))
        query = (query * 0.125).astype(BF)
        total, peak = softmax_parts(query, keys, values, biases)
        sums = pltpu.roll(total, 64, 1)
        parts = (total / sums, peak + jnp.log(sums), peak + jnp.log(total))
        results.append(parts)
    low = low256[:64]
    for at, out in enumerate(outs):
        first, second, third = (
            [part[at * 64 : (at + 1) * 64] for part in results[which]] for which in range(3)
        )
        out[:, 0:128] = jnp.where(low, first[0], second[0])
        out[:, 128:256] = jnp.where(low, third[2], third[0])
        out[:, 256:384] = jnp.where(low, first[1], second[1])


def part_of(parts, pair):
    for at, (first, many) in enumerate(parts):
        if first <= pair < first + many:
            return at, slice((pair - first) * 128, (pair - first) * 128 + 128)


def merge_kernel(meta, *refs):
    count = len(NEAR_PARTS)
    close, refs = refs[:count], refs[count:]
    count = len(WIDE_PARTS)
    wide, o0, lse0 = refs[:count], refs[count : 2 * count], refs[2 * count : 3 * count]
    r0, r1, r2, r3, out, stage, grid_rows = refs[3 * count :]
    bound = meta[0]
    device = meta[1]
    zpos = device // 2 % NZ
    for slot, ref in enumerate((r0, r1, r2, r3)):
        stage[slot] = ref[...]
    low = lane_low(GROUPS)
    for pair in range(PAIRS):
        lanes = slice(pair * 128, pair * 128 + 128)
        close_part, close_lanes = part_of(NEAR_PARTS, pair)
        piece, inner = part_of(WIDE_PARTS, pair)
        if pair in PAIR_OF:
            slot = (PAIR_OF.index(pair) - zpos) & 3
            away, away_lse = stage[slot, :, 0:128], stage[slot, :, 256:384]
        else:
            first = LONE_OF.index(2 * pair)
            left = stage[(first - zpos) & 3, :, 128:256]
            right = stage[(first + 1 - zpos) & 3, :, 128:256]
            away = jnp.where(low, pltpu.roll(left, 64, 1), right)
            away_lse = jnp.where(low, left, pltpu.roll(right, 64, 1))
        here, here_lse = o0[piece][:, inner], lse0[piece][:, inner]
        top = jnp.maximum(here_lse, away_lse)
        weight = jnp.exp(here_lse - top)
        away_weight = jnp.exp(away_lse - top)
        blended = (here * weight + away * away_weight) / (weight + away_weight)
        blended = blended.astype(BF)
        for res in range(RES):
            sides = []
            for head in (2 * pair, 2 * pair + 1):
                rank = level((res - head) % RES)
                if rank == 4:
                    sides.append(blended)
                elif rank >= 2:
                    sides.append(wide[piece][res, :, inner])
                else:
                    sides.append(close[close_part][res, :, close_lanes])
            rows = jnp.where(low, *sides)
            for block in range(4):
                grid_rows[block, res * 16 : (res + 1) * 16, lanes] = rows[
                    block * 16 : (block + 1) * 16, :
                ]
    swap = swap_matrix()
    index = lax.broadcasted_iota(jnp.int32, (256, WIDTH), 0)
    for block in range(4):
        rows = jnp.dot(swap, grid_rows[block], preferred_element_type=F32)
        position = device * ROWS + block * 256 + index
        out[block * 256 : (block + 1) * 256, :] = jnp.where(position < bound, rows, 0.0).astype(BF)


def smem():
    return pl.BlockSpec(memory_space=pltpu.SMEM)


def vmem():
    return pl.BlockSpec(memory_space=pltpu.VMEM)


def whole(shape):
    return pl.BlockSpec(shape, lambda i: (0,) * len(shape))


def params(mib):
    return pltpu.CompilerParams(vmem_limit_bytes=mib * 1024 * 1024)


def shape(dims, dtype=BF):
    return jax.ShapeDtypeStruct(dims, dtype)


def by_residue():
    return pl.BlockSpec((RES, GROUPS, 128), lambda i: (0, 0, i))


def by_part(parts):
    return pl.BlockSpec((parts, 2, GROUPS, 128), lambda i: (0, 0, 0, i))


def flat(block):
    return pl.BlockSpec((GROUPS, 128), lambda i: (0, i))


def reordered(rows):
    return pl.pallas_call(
        reorder,
        in_specs=[vmem()],
        out_specs=vmem(),
        out_shape=shape((RES, GROUPS, WIDTH)),
        compiler_params=params(20),
        name="residue_order",
    )(rows)


def split(meta, q, k, v):
    kt, vt = reordered(k), reordered(v)
    qt, *rest = pl.pallas_call(
        split_kernel,
        in_specs=[smem()] + [vmem()] * 3,
        out_specs=[vmem()] * 7,
        out_shape=[
            shape((RES, GROUPS, WIDTH)),
            shape((4, 2, GROUPS, WIDTH)),
            shape((2, 2, GROUPS, WIDTH)),
        ]
        + [shape((GROUPS, 640))] * 4,
        scratch_shapes=[pltpu.VMEM((4, GROUPS, 640), BF)],
        compiler_params=params(20),
        name="split_rows",
    )(meta, q, kt, vt)
    return qt, kt, vt, *rest


def local_near(first, many, meta, ints, floats, q, k, v):
    return pl.pallas_call(
        functools.partial(local_kernel, "AB", first, many),
        in_specs=[smem()] + [vmem()] * 5,
        out_specs=vmem(),
        out_shape=shape((RES, GROUPS, many * 128)),
        compiler_params=params(40),
        cost_estimate=pl.CostEstimate(
            flops=many * 500000000, bytes_accessed=1000000, transcendentals=many * 900000
        ),
        name="near_queries",
    )(meta, ints, floats, q, k, v)


def local_far(first, many, meta, ints, floats, q, k, v, sel, near, cross):
    return pl.pallas_call(
        functools.partial(local_kernel, "CD", first, many),
        in_specs=[smem()] + [vmem()] * 8,
        out_specs=[vmem()] * 3,
        out_shape=[
            shape((RES, GROUPS, many * 128)),
            shape((GROUPS, many * 128), F32),
            shape((GROUPS, many * 128), F32),
        ],
        compiler_params=params(40),
        cost_estimate=pl.CostEstimate(
            flops=many * 400000000, bytes_accessed=1000000, transcendentals=many * 600000
        ),
        name="wide_queries",
    )(meta, ints, floats, q, k, v, sel, near, cross)


def slide_wide(meta, queries, blocks):
    return pl.pallas_call(
        far_kernel,
        in_specs=[smem()] + [vmem()] * 12,
        out_specs=[vmem()] * 4,
        out_shape=[shape((GROUPS, 384), F32)] * 4,
        compiler_params=params(40),
        cost_estimate=pl.CostEstimate(flops=800000000, bytes_accessed=2000000, transcendentals=1600000),
        name="slide_queries",
    )(meta, *queries, *blocks)


def merge(meta, close, wide, back):
    return pl.pallas_call(
        merge_kernel,
        in_specs=[smem()] + [vmem()] * (len(NEAR_PARTS) + 3 * len(WIDE_PARTS) + 4),
        out_specs=vmem(),
        out_shape=shape((ROWS, WIDTH)),
        scratch_shapes=[
            pltpu.VMEM((4, GROUPS, 384), F32),
            pltpu.VMEM((4, 256, WIDTH), BF),
        ],
        compiler_params=params(40),
        name="merge_rows",
    )(meta, *close, *[part for parts in zip(*wide) for part in parts], *back)


def at(x, z, c):
    return (x % NX * NZ + z % NZ) * NC + c


def move(block, to):
    route = [
        (at(x, z, c), at(*to(x, z, c))) for x in range(NX) for z in range(NZ) for c in range(NC)
    ]
    return lax.ppermute(block, "seq", route)


def along_x(steps):
    return lambda x, z, c: (x + steps, z, c)


def along_z(steps):
    return lambda x, z, c: (x, z + steps, c)


def other_core(x, z, c):
    return (x, z, 1 - c)


def next_chip(x, z, c):
    return (x, z ^ 1, c)


def per_device(query_tiles, key_tiles, value_tiles, slide_length):
    device = lax.axis_index("seq").astype(jnp.int32)
    meta = jnp.stack([slide_length[0], device])
    ints, floats = (jnp.asarray(table) for table in tables())
    qt, kt, vt, sel, sel8, z0, z1, z2, z3 = split(meta, query_tiles, key_tiles, value_tiles)
    local = (ints, floats, qt, kt, vt)
    slabs = [z0] + [move(slab, along_z(step)) for step, slab in ((1, z1), (2, z2), (3, z3))]
    close = [local_near(*NEAR_PARTS[0], meta, *local)]
    slabs, close[0], sel, sel8, later = lax.optimization_barrier(
        (slabs, close[0], sel, sel8, meta)
    )
    own = jnp.concatenate([slab[:, 256:640] for slab in slabs], axis=0)
    own, later = lax.optimization_barrier((own, later))
    moved = [move(own, along_x(step)) for step in (1, 2, 3)]
    near = move(sel8, next_chip)
    pair = move(sel, other_core)
    close.append(local_near(*NEAR_PARTS[1], later, *local))
    near, close[1], last = lax.optimization_barrier((near, close[1], later))
    cross = move(near, other_core)
    close.append(local_near(*NEAR_PARTS[2], last, *local))
    moved, close[2], last = lax.optimization_barrier((moved, close[2], last))
    blocks = [own] + moved
    blocks += [move(block, other_core) for block in blocks]
    wide = [local_far(*WIDE_PARTS[0], last, *local, pair, near, cross)]
    blocks, wide[0] = lax.optimization_barrier((blocks, wide[0]))
    back = slide_wide(meta, [slab[:, 0:256] for slab in slabs], blocks)
    back, last = lax.optimization_barrier((back, last))
    back = [back[0]] + [move(back[step], along_z(-step)) for step in (1, 2, 3)]
    wide.append(local_far(*WIDE_PARTS[1], last, *local, pair, near, cross))
    return merge(meta, close, wide, back)


def solution(mesh):
    placed = (
        P(("slide", "seq"), None),
        P(("slide", "seq"), None),
        P(("slide", "seq"), None),
        P("slide"),
    )
    return jax.shard_map(
        per_device, mesh=mesh, in_specs=placed, out_specs=P(("slide", "seq"), None), check_vma=False
    )
```

```python
import functools

import jax
import jax.numpy as jnp
import numpy as np
from jax import lax
from jax.experimental import pallas as pl
from jax.experimental.pallas import tpu as pltpu
from jax.sharding import PartitionSpec as P

HEADS = 12
HEAD_DIM = 64
WIDTH = 768
ROWS = 1024
RES = 16
GROUPS = ROWS // RES
HALF = GROUPS // 2
PAIRS = HEADS // 2
NX, NZ, NC = 4, 4, 2
MASKED = -1e30

BF = jnp.bfloat16
F32 = jnp.float32

ODD = [1, 3, 5, 7, 9, 11, 13, 15]
EVEN = [2, 6, 10, 14, 4, 12, 8, 0]
SHARED = [0, 8, 4, 12]
CLASS_U = {"A": ODD, "B": [2, 6, 10, 14], "C": [4, 12], "D": [8, 0]}
PAIR_OF = [0, 2, 3, 5]
LONE_OF = [2, 3, 8, 9]
NEAR_PARTS = [(0, 1), (1, 4), (5, 1)]


def level(u):
    return 4 if u == 0 else min((u & -u).bit_length() - 1, 4)


def tables():
    lane = np.arange(256)
    ints = np.zeros((8, 256), np.int32)
    ints[0] = np.array(ODD)[lane // 32]
    ints[1] = np.array(EVEN)[lane // 32]
    ints[2] = lane % 32 * 16
    ints[3] = np.array(SHARED)[lane // 64]
    ints[4] = lane % 64 * 16
    ints[5] = np.array([0, 8, 0, 8])[lane // 64]
    even = np.array([level(u) for u in EVEN])[lane // 32]
    shared = np.array([level(u) for u in SHARED])[lane // 64]
    floats = np.zeros((8, 256), np.float32)
    floats[1] = np.log(1.0 + np.minimum(even, 1))
    floats[2] = np.log(1.0 + np.minimum(even, 2))
    floats[3] = np.log(1.0 + np.minimum(even, 3))
    floats[4] = np.log(1.0 * np.minimum(even, 2))
    floats[5] = np.log(1.0 * np.minimum(even, 3))
    floats[6] = np.log(np.minimum(shared, 3) - 1.0)
    return ints, floats


def swap_matrix():
    row = lax.broadcasted_iota(jnp.int32, (256, 256), 0)
    col = lax.broadcasted_iota(jnp.int32, (256, 256), 1)
    return jnp.where(((row & 15) * 16 + (row >> 4)) == col, 1.0, 0.0).astype(BF)


def lane_low(rows):
    return lax.broadcasted_iota(jnp.int32, (rows, 128), 1) < 64


def reorder(source, target):
    swap = swap_matrix()
    for block in range(4):
        moved = jnp.dot(
            swap, source[block * 256 : (block + 1) * 256, :], preferred_element_type=F32
        ).astype(BF)
        for res in range(RES):
            target[res, block * 16 : (block + 1) * 16, :] = moved[res * 16 : (res + 1) * 16, :]


def split_kernel(meta, q_in, kt, vt, qt, sel, sel8, z0, z1, z2, z3, stage):
    reorder(q_in, qt)
    zpos = meta[1] // 2 % NZ
    low = lane_low(GROUPS)

    def other(rows):
        return pltpu.roll(rows.astype(F32), 64, 1).astype(BF)

    for pair in range(PAIRS):
        lanes = slice(pair * 128, pair * 128 + 128)

        def picked(ref, u):
            return jnp.where(
                low, ref[(u + 2 * pair) % RES, :, lanes], ref[(u + 2 * pair + 1) % RES, :, lanes]
            )

        for at, u in enumerate(SHARED):
            for kv, ref in enumerate((kt, vt)):
                rows = picked(ref, u)
                sel[at, kv, :, lanes] = rows
                if at < 2:
                    sel8[at, kv, :, lanes] = rows
                if at == 0 and kv == 0:
                    k0 = rows
                if at == 0 and kv == 1:
                    v0 = rows
        q0 = picked(qt, 0)
        for group in range(NZ):
            slot = (group - zpos) & 3
            if pair == PAIR_OF[group]:
                stage[slot, :, 0:128] = q0
                stage[slot, :, 256:384] = k0
                stage[slot, :, 384:512] = v0
            if pair == LONE_OF[group] // 2:
                if LONE_OF[group] % 2 == 0:
                    lone_q, lone_k, lone_v = q0, k0, other(v0)
                else:
                    lone_q, lone_k, lone_v = other(q0), other(k0), v0
                stage[slot, :, 128:256] = jnp.where(low, lone_q, jnp.zeros_like(lone_q))
                stage[slot, :, 512:640] = jnp.where(low, lone_k, lone_v)
    for slot, out in enumerate((z0, z1, z2, z3)):
        out[...] = stage[slot]


def softmax_parts(query, keys, values, biases):
    scores = [
        lax.dot_general(query, key, (((1,), (1,)), ((), ())), preferred_element_type=F32) + bias
        for key, bias in zip(keys, biases)
    ]
    peak = functools.reduce(jnp.maximum, scores)
    peak = jnp.max(peak, axis=1, keepdims=True)
    total = None
    for score, value in zip(scores, values):
        weight = jnp.exp(score - peak).astype(BF)
        part = jnp.dot(weight, value, preferred_element_type=F32)
        total = part if total is None else total + part
    return total, peak


def local_kernel(classes, first, many, meta, ints, floats, *refs):
    def body(step, carry):
        lanes = pl.ds(pl.multiple_of((first + step) * 128, 128), 128)
        here = pl.ds(pl.multiple_of(step * 128, 128), 128)
        views = [ref.at[:, :, lanes] for ref in refs[:3]] + [refs[3].at[:, :, :, lanes]]
        if classes == "D":
            views += [ref.at[:, :, :, lanes] for ref in refs[4:6]]
            views += [refs[6].at[:, :, here]]
            views += [ref.at[:, here] for ref in refs[7:9]]
        else:
            views += [refs[4].at[:, :, here]]
        local_pair(classes, first + step, meta, ints, floats, *views)
        return carry

    lax.fori_loop(0, many, body, 0)


def local_pair(classes, pair, meta, ints, floats, q_ref, k_ref, v_ref, sel, *rest):
    far = classes == "D"
    if far:
        near, cross, out, o0, lse0 = rest
    else:
        (out,) = rest
    bound = meta[0]
    device = meta[1]
    low = lane_low(256)
    low_all = lane_low(128 if far else 896)
    high_all = jnp.logical_not(low_all)
    for parity in range(2):
        head = 2 * pair + parity
        mine = low if parity == 0 else jnp.logical_not(low)

        def gathered(ref, order, half):
            return jnp.concatenate(
                [ref[(u + head) & 15, half * HALF : (half + 1) * HALF, :] for u in order], axis=0
            )

        def widened(value):
            return jnp.where(mine, value, jnp.ones_like(value))

        def bias(kind, place, device_of, offset, row):
            position = (
                device_of * ROWS
                + offset
                + ints[place : place + 1, :]
                + ((ints[kind : kind + 1, :] + head) & 15)
            )
            return jnp.where(position < bound, floats[row : row + 1, :], MASKED)

        odd_k = [gathered(k_ref, ODD, half) for half in range(2)]
        even_k = [gathered(k_ref, EVEN, half) for half in range(2)]
        odd_v = [widened(gathered(v_ref, ODD, half)) for half in range(2)]
        even_v = [widened(gathered(v_ref, EVEN, half)) for half in range(2)]
        pair_k = sel[:, 0].reshape(256, 128)
        pair_v = widened(sel[:, 1].reshape(256, 128))
        if far:
            next_k = jnp.concatenate([near[0, 0], near[1, 0], cross[0, 0], cross[1, 0]], axis=0)
            next_v = widened(
                jnp.concatenate([near[0, 1], near[1, 1], cross[0, 1], cross[1, 1]], axis=0)
            )
            lane = lax.broadcasted_iota(jnp.int32, (1, 256), 1)
            next_device = jnp.where(lane < 128, device ^ 2, device ^ 3)
        groups = [(name, 0) for name in classes] + [(name, 1) for name in classes[::-1]]
        tiles = []
        for half in range(2):
            tiles.append((odd_k[half], odd_v[half], lambda cap, side, half=half: side == half))
            tiles.append(
                (even_k[half], even_v[half], lambda cap, side, half=half: side == half or cap >= 1)
            )
        tiles.append((pair_k, pair_v, lambda cap, side: cap >= 2))
        if far:
            tiles.append((next_k, next_v, lambda cap, side: cap >= 3))

        def tile_bias(tile, cap, side):
            if tile >= 4:
                if tile == 5:
                    return bias(5, 4, next_device, 0, 0)
                return bias(3, 4, device ^ 1, 0, (0, 0, 0, 6)[cap])
            offset = tile // 2 * 512
            if tile % 2 == 0:
                return bias(0, 2, device, offset, 0)
            row = cap if tile // 2 == side else (0, 0, 4, 5)[cap]
            return bias(1, 2, device, offset, row)

        pieces, starts, count = [], [], 0
        for name, side in groups:
            pieces.append(gathered(q_ref, CLASS_U[name], side))
            starts.append(count)
            count += pieces[-1].shape[0]
        starts.append(count)
        query = jnp.concatenate(pieces, axis=0)
        query = (jnp.where(low_all if parity == 0 else high_all, query, jnp.zeros_like(query)) * 0.125).astype(BF)
        caps = [("ABCD".index(name), side) for name, side in groups]
        scores, spans = [], []
        for key, value, member in tiles:
            inside = [at for at, (cap, side) in enumerate(caps) if member(cap, side)]
            first, last = inside[0], inside[-1] + 1
            spans.append((first, last))
            scores.append(
                lax.dot_general(
                    query[starts[first] : starts[last]],
                    key,
                    (((1,), (1,)), ((), ())),
                    preferred_element_type=F32,
                )
            )
        weights = [[] for _ in tiles]
        peaks = []
        for at, (cap, side) in enumerate(caps):
            held = []
            for tile, (first, last) in enumerate(spans):
                if first <= at < last:
                    base = starts[first]
                    held.append(
                        (
                            tile,
                            scores[tile][starts[at] - base : starts[at + 1] - base]
                            + tile_bias(tile, cap, side),
                        )
                    )
            peak = functools.reduce(jnp.maximum, [score for _, score in held])
            peak = jnp.max(peak, axis=1, keepdims=True)
            peaks.append(peak)
            for tile, score in held:
                weights[tile].append(jnp.exp(score - peak).astype(BF))
        totals = [None] * len(caps)
        for tile, (first, last) in enumerate(spans):
            part = jnp.dot(
                jnp.concatenate(weights[tile], axis=0), tiles[tile][1], preferred_element_type=F32
            )
            for at in range(first, last):
                rows = part[starts[at] - starts[first] : starts[at + 1] - starts[first]]
                totals[at] = rows if totals[at] is None else totals[at] + rows
        for at, (name, half) in enumerate(groups):
            total, peak = totals[at], peaks[at]
            sums = pltpu.roll(total, 64, 1)
            result = total / sums
            rounded = result.astype(BF)
            for row, u in enumerate(CLASS_U[name]):
                spot = ((u + head) & 15, slice(half * HALF, (half + 1) * HALF), slice(None))
                out[spot] = jnp.where(
                    mine[:HALF], rounded[row * HALF : (row + 1) * HALF, :], out[spot]
                )
            if name == "D":
                rows = slice(half * HALF, (half + 1) * HALF)
                log_total = peak[HALF:] + jnp.log(sums[HALF:])
                o0[rows, :] = jnp.where(mine[:HALF], result[HALF:], o0[rows, :])
                lse0[rows, :] = jnp.where(mine[:HALF], log_total, lse0[rows, :])


def far_kernel(meta, a0, a1, a2, a3, *rest):
    blocks, outs = rest[:8], rest[8:]
    bound = meta[0]
    device = meta[1]
    xpos, zpos, core = device // 8, device // 2 % NZ, device % 2
    low256 = lane_low(256)
    group = zpos
    lane = lax.broadcasted_iota(jnp.int32, (1, 256), 1)
    part = lane >> 6
    pair = jnp.where(group == 0, 0, jnp.where(group == 1, 4, jnp.where(group == 2, 6, 10)))
    lone = jnp.where(group == 0, 2, jnp.where(group == 1, 3, jnp.where(group == 2, 8, 9)))
    results = []
    for which in range(3):
        head = (pair, pair + 1, lone)[which]
        if which < 2:
            mine = low256 if which == 0 else jnp.logical_not(low256)
        else:
            mine = jnp.logical_not(low256)
        keys, values, biases = [], [], []
        for at, block in enumerate(blocks):
            from_x = (xpos - at % 4) & 3
            from_c = core if at < 4 else 1 - core
            from_z = (zpos - part) & 3
            position = ((from_x * NZ + from_z) * NC + from_c) * ROWS + (lane & 63) * 16 + head
            biases.append(jnp.where(position < bound, 0.0, MASKED))
            if which < 2:
                keys.append(block[:, 0:128])
                value = block[:, 128:256]
            else:
                keys.append(block[:, 256:384])
                value = block[:, 256:384]
            values.append(jnp.where(mine, value, jnp.ones_like(value)))
        lanes = slice(0, 128) if which < 2 else slice(128, 256)
        query = jnp.concatenate([source[:, lanes] for source in (a0, a1, a2, a3)], axis=0)
        if which < 2:
            query = jnp.where(mine, query, jnp.zeros_like(query))
        query = (query * 0.125).astype(BF)
        total, peak = softmax_parts(query, keys, values, biases)
        sums = pltpu.roll(total, 64, 1)
        logs = peak + jnp.log(sums if which < 2 else total)
        results.append((total / sums, logs))
    low = low256[:64]
    lane = lax.broadcasted_iota(jnp.int32, (64, 128), 1)
    for at, out in enumerate(outs):
        rows = slice(at * 64, (at + 1) * 64)
        out[:, 0:128] = jnp.where(low, results[0][0][rows], results[1][0][rows]).astype(BF)
        mixed = results[2][0][rows].astype(BF)
        for which, place in ((0, 0), (1, 64), (2, 0)):
            rest = results[which][1][rows, place : place + 1]
            for term in range(3):
                kept = rest.astype(BF)
                rest = rest - kept.astype(F32)
                mixed = jnp.where(lane == which * 3 + term, kept, mixed)
        out[:, 128:256] = mixed


def part_of(parts, pair):
    for at, (first, many) in enumerate(parts):
        if first <= pair < first + many:
            return at, slice((pair - first) * 128, (pair - first) * 128 + 128)


def merge_kernel(meta, *refs):
    count = len(NEAR_PARTS)
    close, refs = refs[:count], refs[count:]
    wide, o0, lse0, r0, r1, r2, r3, out, stage, grid_rows = refs
    bound = meta[0]
    device = meta[1]
    zpos = device // 2 % NZ
    for slot, ref in enumerate((r0, r1, r2, r3)):
        stage[slot] = ref[...].astype(F32)
    low = lane_low(GROUPS)

    def log_of(slot, which):
        terms = [stage[slot, :, 128 + which * 3 + term : 129 + which * 3 + term] for term in range(3)]
        return terms[0] + terms[1] + terms[2]

    for pair in range(PAIRS):
        lanes = slice(pair * 128, pair * 128 + 128)
        close_part, close_lanes = part_of(NEAR_PARTS, pair)
        if pair in PAIR_OF:
            slot = (PAIR_OF.index(pair) - zpos) & 3
            away = stage[slot, :, 0:128]
            away_lse = jnp.where(low, log_of(slot, 0), log_of(slot, 1))
        else:
            left = (LONE_OF.index(2 * pair) - zpos) & 3
            right = (left + 1) & 3
            away = jnp.where(low, pltpu.roll(stage[left, :, 128:256], 64, 1), stage[right, :, 128:256])
            away_lse = jnp.where(low, log_of(left, 2), log_of(right, 2))
        here, here_lse = o0[:, lanes], lse0[:, lanes]
        top = jnp.maximum(here_lse, away_lse)
        weight = jnp.exp(here_lse - top)
        away_weight = jnp.exp(away_lse - top)
        blended = (here * weight + away * away_weight) / (weight + away_weight)
        blended = blended.astype(BF)
        for res in range(RES):
            sides = []
            for head in (2 * pair, 2 * pair + 1):
                rank = level((res - head) % RES)
                if rank == 4:
                    sides.append(blended)
                elif rank == 3:
                    sides.append(wide[res, :, lanes])
                else:
                    sides.append(close[close_part][res, :, close_lanes])
            rows = jnp.where(low, *sides)
            for block in range(4):
                grid_rows[block, res * 16 : (res + 1) * 16, lanes] = rows[
                    block * 16 : (block + 1) * 16, :
                ]
    swap = swap_matrix()
    index = lax.broadcasted_iota(jnp.int32, (256, WIDTH), 0)
    for block in range(4):
        rows = jnp.dot(swap, grid_rows[block], preferred_element_type=F32)
        position = device * ROWS + block * 256 + index
        out[block * 256 : (block + 1) * 256, :] = jnp.where(position < bound, rows, 0.0).astype(BF)


def smem():
    return pl.BlockSpec(memory_space=pltpu.SMEM)


def vmem():
    return pl.BlockSpec(memory_space=pltpu.VMEM)


def whole(shape):
    return pl.BlockSpec(shape, lambda i: (0,) * len(shape))


def params(mib):
    return pltpu.CompilerParams(vmem_limit_bytes=mib * 1024 * 1024)


def shape(dims, dtype=BF):
    return jax.ShapeDtypeStruct(dims, dtype)


def by_residue():
    return pl.BlockSpec((RES, GROUPS, 128), lambda i: (0, 0, i))


def by_part(parts):
    return pl.BlockSpec((parts, 2, GROUPS, 128), lambda i: (0, 0, 0, i))


def flat(block):
    return pl.BlockSpec((GROUPS, 128), lambda i: (0, i))


def reordered(rows):
    return pl.pallas_call(
        reorder,
        in_specs=[vmem()],
        out_specs=vmem(),
        out_shape=shape((RES, GROUPS, WIDTH)),
        compiler_params=params(20),
        name="residue_order",
    )(rows)


def split(meta, q, k, v):
    kt, vt = reordered(k), reordered(v)
    qt, *rest = pl.pallas_call(
        split_kernel,
        in_specs=[smem()] + [vmem()] * 3,
        out_specs=[vmem()] * 7,
        out_shape=[
            shape((RES, GROUPS, WIDTH)),
            shape((4, 2, GROUPS, WIDTH)),
            shape((2, 2, GROUPS, WIDTH)),
        ]
        + [shape((GROUPS, 640))] * 4,
        scratch_shapes=[pltpu.VMEM((4, GROUPS, 640), BF)],
        compiler_params=params(20),
        name="split_rows",
    )(meta, q, kt, vt)
    return qt, kt, vt, *rest


def local_near(first, many, meta, ints, floats, q, k, v, sel):
    return pl.pallas_call(
        functools.partial(local_kernel, "ABC", first, many),
        in_specs=[smem()] + [vmem()] * 6,
        out_specs=vmem(),
        out_shape=shape((RES, GROUPS, many * 128)),
        compiler_params=params(40),
        cost_estimate=pl.CostEstimate(
            flops=many * 600000000, bytes_accessed=1000000, transcendentals=many * 1200000
        ),
        name="near_queries",
    )(meta, ints, floats, q, k, v, sel)


def local_far(meta, ints, floats, q, k, v, sel, near, cross):
    return pl.pallas_call(
        functools.partial(local_kernel, "D", 0, PAIRS),
        in_specs=[smem()] + [vmem()] * 8,
        out_specs=[vmem()] * 3,
        out_shape=[
            shape((RES, GROUPS, WIDTH)),
            shape((GROUPS, WIDTH), F32),
            shape((GROUPS, WIDTH), F32),
        ],
        compiler_params=params(40),
        cost_estimate=pl.CostEstimate(
            flops=1000000000, bytes_accessed=1000000, transcendentals=2000000
        ),
        name="wide_queries",
    )(meta, ints, floats, q, k, v, sel, near, cross)


def slide_wide(meta, queries, blocks):
    return pl.pallas_call(
        far_kernel,
        in_specs=[smem()] + [vmem()] * 12,
        out_specs=[vmem()] * 4,
        out_shape=[shape((GROUPS, 256))] * 4,
        compiler_params=params(40),
        cost_estimate=pl.CostEstimate(flops=800000000, bytes_accessed=2000000, transcendentals=1600000),
        name="slide_queries",
    )(meta, *queries, *blocks)


def merge(meta, close, wide, back):
    return pl.pallas_call(
        merge_kernel,
        in_specs=[smem()] + [vmem()] * (len(NEAR_PARTS) + 7),
        out_specs=vmem(),
        out_shape=shape((ROWS, WIDTH)),
        scratch_shapes=[
            pltpu.VMEM((4, GROUPS, 256), F32),
            pltpu.VMEM((4, 256, WIDTH), BF),
        ],
        compiler_params=params(40),
        name="merge_rows",
    )(meta, *close, *wide, *back)


def at(x, z, c):
    return (x % NX * NZ + z % NZ) * NC + c


def move(block, to):
    route = [
        (at(x, z, c), at(*to(x, z, c))) for x in range(NX) for z in range(NZ) for c in range(NC)
    ]
    return lax.ppermute(block, "seq", route)


def along_x(steps):
    return lambda x, z, c: (x + steps, z, c)


def along_z(steps):
    return lambda x, z, c: (x, z + steps, c)


def other_core(x, z, c):
    return (x, z, 1 - c)


def next_chip(x, z, c):
    return (x, z ^ 1, c)


def per_device(query_tiles, key_tiles, value_tiles, slide_length):
    device = lax.axis_index("seq").astype(jnp.int32)
    meta = jnp.stack([slide_length[0], device])
    ints, floats = (jnp.asarray(table) for table in tables())
    qt, kt, vt, sel, sel8, z0, z1, z2, z3 = split(meta, query_tiles, key_tiles, value_tiles)
    slabs = [z0] + [move(slab, along_z(step)) for step, slab in ((1, z1), (2, z2), (3, z3))]
    pair = move(sel, other_core)
    local = (ints, floats, qt, kt, vt, pair)
    close = [local_near(*NEAR_PARTS[0], meta, *local)]
    slabs, close[0], sel8, later = lax.optimization_barrier((slabs, close[0], sel8, meta))
    own = jnp.concatenate([slab[:, 256:640] for slab in slabs], axis=0)
    own, later = lax.optimization_barrier((own, later))
    moved = [move(own, along_x(step)) for step in (1, 2, 3)]
    near = move(sel8, next_chip)
    close.append(local_near(*NEAR_PARTS[1], later, *local))
    moved, near, close[1], later = lax.optimization_barrier((moved, near, close[1], later))
    cross = move(near, other_core)
    blocks = [own] + moved
    blocks += [move(block, other_core) for block in blocks]
    close.append(local_near(*NEAR_PARTS[2], later, *local))
    blocks, close[2], later = lax.optimization_barrier((blocks, close[2], later))
    back = slide_wide(meta, [slab[:, 0:256] for slab in slabs], blocks)
    back, later = lax.optimization_barrier((back, later))
    back = [back[0]] + [move(back[step], along_z(-step)) for step in (1, 2, 3)]
    wide = local_far(later, *local, near, cross)
    return merge(meta, close, wide, back)


def solution(mesh):
    placed = (
        P(("slide", "seq"), None),
        P(("slide", "seq"), None),
        P(("slide", "seq"), None),
        P("slide"),
    )
    return jax.shard_map(
        per_device, mesh=mesh, in_specs=placed, out_specs=P(("slide", "seq"), None), check_vma=False
    )
```

```python
import functools

import jax
import jax.numpy as jnp
import numpy as np
from jax import lax
from jax.experimental import pallas as pl
from jax.experimental.pallas import tpu as pltpu
from jax.sharding import PartitionSpec as P

HEADS = 12
HEAD_DIM = 64
WIDTH = 768
ROWS = 1024
RES = 16
GROUPS = ROWS // RES
HALF = GROUPS // 2
PAIRS = HEADS // 2
NX, NZ, NC = 4, 4, 2
MASKED = -1e30

BF = jnp.bfloat16
F32 = jnp.float32

ODD = [1, 3, 5, 7, 9, 11, 13, 15]
SHARED = [0, 8, 4, 12]
CLASS_U = {"A": ODD, "B": [2, 6, 10, 14], "C": [4, 12], "D": [8, 0]}
PAIR_OF = [0, 2, 3, 5]
LONE_OF = [2, 3, 8, 9]
NEAR_PARTS = [(0, 1), (1, 4), (5, 1)]


def level(u):
    return 4 if u == 0 else min((u & -u).bit_length() - 1, 4)


def swap_matrix():
    row = lax.broadcasted_iota(jnp.int32, (256, 256), 0)
    col = lax.broadcasted_iota(jnp.int32, (256, 256), 1)
    return jnp.where(((row & 15) * 16 + (row >> 4)) == col, 1.0, 0.0).astype(BF)


def lane_low(rows):
    return lax.broadcasted_iota(jnp.int32, (rows, 128), 1) < 64


def reorder(source, target):
    swap = swap_matrix()
    for block in range(4):
        moved = jnp.dot(
            swap, source[block * 256 : (block + 1) * 256, :], preferred_element_type=F32
        ).astype(BF)
        for res in range(RES):
            target[res, block * 16 : (block + 1) * 16, :] = moved[res * 16 : (res + 1) * 16, :]


def split_kernel(meta, q_in, kt, vt, qt, sel, sel8, z0, z1, z2, z3, stage):
    reorder(q_in, qt)
    zpos = meta[1] // 2 % NZ
    low = lane_low(GROUPS)

    def other(rows):
        return pltpu.roll(rows.astype(F32), 64, 1).astype(BF)

    for pair in range(PAIRS):
        lanes = slice(pair * 128, pair * 128 + 128)

        def picked(ref, u):
            return jnp.where(
                low, ref[(u + 2 * pair) % RES, :, lanes], ref[(u + 2 * pair + 1) % RES, :, lanes]
            )

        for at, u in enumerate(SHARED):
            for kv, ref in enumerate((kt, vt)):
                rows = picked(ref, u)
                sel[at, kv, :, lanes] = rows
                if at < 2:
                    sel8[at, kv, :, lanes] = rows
                if at == 0 and kv == 0:
                    k0 = rows
                if at == 0 and kv == 1:
                    v0 = rows
        q0 = picked(qt, 0)
        for group in range(NZ):
            slot = (group - zpos) & 3
            if pair == PAIR_OF[group]:
                stage[slot, :, 0:128] = q0
                stage[slot, :, 256:384] = k0
                stage[slot, :, 384:512] = v0
            if pair == LONE_OF[group] // 2:
                if LONE_OF[group] % 2 == 0:
                    lone_q, lone_k, lone_v = q0, k0, other(v0)
                else:
                    lone_q, lone_k, lone_v = other(q0), other(k0), v0
                stage[slot, :, 128:256] = jnp.where(low, lone_q, jnp.zeros_like(lone_q))
                stage[slot, :, 512:640] = jnp.where(low, lone_k, lone_v)
    for slot, out in enumerate((z0, z1, z2, z3)):
        out[...] = stage[slot]


def softmax_parts(query, keys, values, biases):
    scores = [
        lax.dot_general(query, key, (((1,), (1,)), ((), ())), preferred_element_type=F32) + bias
        for key, bias in zip(keys, biases)
    ]
    peak = functools.reduce(jnp.maximum, scores)
    peak = jnp.max(peak, axis=1, keepdims=True)
    total = None
    for score, value in zip(scores, values):
        weight = jnp.exp(score - peak).astype(BF)
        part = jnp.dot(weight, value, preferred_element_type=F32)
        total = part if total is None else total + part
    return total, peak


def local_kernel(classes, first, many, meta, *refs):
    def body(step, carry):
        lanes = pl.ds(pl.multiple_of((first + step) * 128, 128), 128)
        here = pl.ds(pl.multiple_of(step * 128, 128), 128)
        views = [ref.at[:, :, lanes] for ref in refs[:3]] + [refs[3].at[:, :, :, lanes]]
        if classes == "D":
            views += [ref.at[:, :, :, lanes] for ref in refs[4:6]]
            views += [refs[6].at[:, :, here]]
            views += [ref.at[:, here] for ref in refs[7:9]]
        else:
            views += [refs[4].at[:, :, here]]
        local_pair(classes, first + step, meta, *views)
        return carry

    lax.fori_loop(0, many, body, 0, unroll=True)


def local_pair(classes, pair, meta, q_ref, k_ref, v_ref, sel, *rest):
    far = classes == "D"
    if far:
        near, cross, out, o0, lse0 = rest
    else:
        (out,) = rest
    bound = meta[0]
    device = meta[1]
    lane = lax.broadcasted_iota(jnp.int32, (1, 256), 1)
    groups = [(name, 0) for name in classes] + [(name, 1) for name in classes[::-1]]
    caps = [("ABCD".index(name), side) for name, side in groups]
    starts = [0]
    for name, _ in groups:
        starts.append(starts[-1] + len(CLASS_U[name]) * HALF)
    low = lane_low(starts[-1])

    def rows_of(ref, tile):
        half, odd = tile // 2, tile % 2
        rows = slice(half * HALF, (half + 1) * HALF)
        return jnp.concatenate([ref[2 * at + odd, rows, :] for at in range(8)], axis=0)

    keys = [rows_of(k_ref, tile) for tile in range(4)] + [sel[:, 0].reshape(256, 128)]
    values = [rows_of(v_ref, tile) for tile in range(4)] + [sel[:, 1].reshape(256, 128)]
    if far:
        for kv, rows in enumerate((keys, values)):
            rows.append(
                jnp.concatenate([near[0, kv], near[1, kv], cross[0, kv], cross[1, kv]], axis=0)
            )

    def inside(tile, parity, cap, side):
        if tile >= 4:
            return cap >= tile - 2
        return side == tile // 2 or (tile % 2 == parity and cap >= 1)

    def bias(tile, parity, cap, side):
        head = 2 * pair + parity
        logs = jnp.zeros((1, 256), F32)
        if tile < 4:
            half, odd = tile // 2, tile % 2
            res = 2 * (lane >> 5) + odd
            position = device * ROWS + half * 512 + (lane & 31) * 16 + res
            if odd == parity and cap >= 1:
                u = (res - head) & 15
                extra = 1.0 if side == half else 0.0
                one, two, three = (float(np.log(extra + min(cap, rank))) for rank in (1, 2, 3))
                logs = jnp.where(
                    (u & 2) != 0, one, jnp.where((u & 4) != 0, two, three)
                ) + jnp.zeros((1, 256), F32)
        elif tile == 4:
            u = ((lane >> 6) & 1) * 8 + (lane >> 7) * 4
            position = (device ^ 1) * ROWS + (lane & 63) * 16 + ((u + head) & 15)
            if cap == 3:
                logs = jnp.where(lane < 128, float(np.log(2.0)), 0.0)
        else:
            u = ((lane >> 6) & 1) * 8
            source = jnp.where(lane < 128, device ^ 2, device ^ 3)
            position = source * ROWS + (lane & 63) * 16 + ((u + head) & 15)
        return jnp.where(position < bound, logs, MASKED)

    queries = []
    for parity in range(2):
        head = 2 * pair + parity
        query = jnp.concatenate(
            [
                q_ref[(u + head) & 15, side * HALF : (side + 1) * HALF, :]
                for name, side in groups
                for u in CLASS_U[name]
            ],
            axis=0,
        )
        mine = low if parity == 0 else jnp.logical_not(low)
        queries.append((jnp.where(mine, query, jnp.zeros_like(query)) * 0.125).astype(BF))
    scores, spans = {}, {}
    for tile, key in enumerate(keys):
        parts = []
        for parity in range(2):
            held = [at for at, (cap, side) in enumerate(caps) if inside(tile, parity, cap, side)]
            spans[tile, parity] = (held[0], held[-1] + 1)
            parts.append(queries[parity][starts[held[0]] : starts[held[-1] + 1]])
        both = lax.dot_general(
            jnp.concatenate(parts, axis=0),
            key,
            (((1,), (1,)), ((), ())),
            preferred_element_type=F32,
        )
        cut = parts[0].shape[0]
        scores[tile, 0], scores[tile, 1] = both[:cut], both[cut:]
    weights = {spot: [] for spot in spans}
    peaks = {}
    for parity in range(2):
        for at, (cap, side) in enumerate(caps):
            held = []
            for tile in range(len(keys)):
                first, last = spans[tile, parity]
                if first <= at < last:
                    base = starts[first]
                    held.append(
                        (
                            tile,
                            scores[tile, parity][starts[at] - base : starts[at + 1] - base]
                            + bias(tile, parity, cap, side),
                        )
                    )
            peak = functools.reduce(jnp.maximum, [score for _, score in held])
            peak = jnp.max(peak, axis=1, keepdims=True)
            peaks[parity, at] = peak
            for tile, score in held:
                weights[tile, parity].append(jnp.exp(score - peak).astype(BF))
    totals = {}
    for tile, value in enumerate(values):
        for parity in range(2):
            side = lane_low(256) if parity == 0 else jnp.logical_not(lane_low(256))
            part = jnp.dot(
                jnp.concatenate(weights[tile, parity], axis=0),
                jnp.where(side, value, jnp.ones_like(value)),
                preferred_element_type=F32,
            )
            base = 0
            for at in range(*spans[tile, parity]):
                count = starts[at + 1] - starts[at]
                rows = part[base : base + count]
                base += count
                spot = (parity, at)
                totals[spot] = totals[spot] + rows if spot in totals else rows
    for parity in range(2):
        head = 2 * pair + parity
        mine = low[:HALF] if parity == 0 else jnp.logical_not(low[:HALF])
        for at, (name, half) in enumerate(groups):
            total = totals[parity, at]
            sums = pltpu.roll(total, 64, 1)
            result = total / sums
            rounded = result.astype(BF)
            rows = slice(half * HALF, (half + 1) * HALF)
            for row, u in enumerate(CLASS_U[name]):
                spot = ((u + head) & 15, rows, slice(None))
                out[spot] = jnp.where(mine, rounded[row * HALF : (row + 1) * HALF, :], out[spot])
            if name == "D":
                log_total = peaks[parity, at][HALF:] + jnp.log(sums[HALF:])
                o0[rows, :] = jnp.where(mine, result[HALF:], o0[rows, :])
                lse0[rows, :] = jnp.where(mine, log_total, lse0[rows, :])


def far_kernel(meta, a0, a1, a2, a3, *rest):
    blocks, outs = rest[:8], rest[8:]
    bound = meta[0]
    device = meta[1]
    xpos, zpos, core = device // 8, device // 2 % NZ, device % 2
    low256 = lane_low(256)
    group = zpos
    lane = lax.broadcasted_iota(jnp.int32, (1, 256), 1)
    part = lane >> 6
    pair = jnp.where(group == 0, 0, jnp.where(group == 1, 4, jnp.where(group == 2, 6, 10)))
    lone = jnp.where(group == 0, 2, jnp.where(group == 1, 3, jnp.where(group == 2, 8, 9)))
    results = []
    for which in range(3):
        head = (pair, pair + 1, lone)[which]
        if which < 2:
            mine = low256 if which == 0 else jnp.logical_not(low256)
        else:
            mine = jnp.logical_not(low256)
        keys, values, biases = [], [], []
        for at, block in enumerate(blocks):
            from_x = (xpos - at % 4) & 3
            from_c = core if at < 4 else 1 - core
            from_z = (zpos - part) & 3
            position = ((from_x * NZ + from_z) * NC + from_c) * ROWS + (lane & 63) * 16 + head
            biases.append(jnp.where(position < bound, 0.0, MASKED))
            if which < 2:
                keys.append(block[:, 0:128])
                value = block[:, 128:256]
            else:
                keys.append(block[:, 256:384])
                value = block[:, 256:384]
            values.append(jnp.where(mine, value, jnp.ones_like(value)))
        lanes = slice(0, 128) if which < 2 else slice(128, 256)
        query = jnp.concatenate([source[:, lanes] for source in (a0, a1, a2, a3)], axis=0)
        if which < 2:
            query = jnp.where(mine, query, jnp.zeros_like(query))
        query = (query * 0.125).astype(BF)
        total, peak = softmax_parts(query, keys, values, biases)
        sums = pltpu.roll(total, 64, 1)
        logs = peak + jnp.log(sums if which < 2 else total)
        results.append((total / sums, logs))
    low = low256[:64]
    lane = lax.broadcasted_iota(jnp.int32, (64, 128), 1)
    for at, out in enumerate(outs):
        rows = slice(at * 64, (at + 1) * 64)
        out[:, 0:128] = jnp.where(low, results[0][0][rows], results[1][0][rows]).astype(BF)
        mixed = results[2][0][rows].astype(BF)
        for which, place in ((0, 0), (1, 64), (2, 0)):
            rest = results[which][1][rows, place : place + 1]
            for term in range(3):
                kept = rest.astype(BF)
                rest = rest - kept.astype(F32)
                mixed = jnp.where(lane == which * 3 + term, kept, mixed)
        out[:, 128:256] = mixed


def part_of(parts, pair):
    for at, (first, many) in enumerate(parts):
        if first <= pair < first + many:
            return at, slice((pair - first) * 128, (pair - first) * 128 + 128)


def merge_kernel(meta, *refs):
    count = len(NEAR_PARTS)
    close, refs = refs[:count], refs[count:]
    wide, o0, lse0, r0, r1, r2, r3, out, stage, grid_rows, ready, sent = refs
    bound = meta[0]
    device = meta[1]
    zpos = device // 2 % NZ
    for slot, ref in enumerate((r0, r1, r2, r3)):
        stage[slot] = ref[...].astype(F32)
    low = lane_low(GROUPS)

    def log_of(slot, which):
        terms = [stage[slot, :, 128 + which * 3 + term : 129 + which * 3 + term] for term in range(3)]
        return terms[0] + terms[1] + terms[2]

    for pair in range(PAIRS):
        lanes = slice(pair * 128, pair * 128 + 128)
        close_part, close_lanes = part_of(NEAR_PARTS, pair)
        if pair in PAIR_OF:
            slot = (PAIR_OF.index(pair) - zpos) & 3
            away = stage[slot, :, 0:128]
            away_lse = jnp.where(low, log_of(slot, 0), log_of(slot, 1))
        else:
            left = (LONE_OF.index(2 * pair) - zpos) & 3
            right = (left + 1) & 3
            away = jnp.where(low, pltpu.roll(stage[left, :, 128:256], 64, 1), stage[right, :, 128:256])
            away_lse = jnp.where(low, log_of(left, 2), log_of(right, 2))
        here, here_lse = o0[:, lanes], lse0[:, lanes]
        top = jnp.maximum(here_lse, away_lse)
        weight = jnp.exp(here_lse - top)
        away_weight = jnp.exp(away_lse - top)
        blended = (here * weight + away * away_weight) / (weight + away_weight)
        blended = blended.astype(BF)
        for res in range(RES):
            sides = []
            for head in (2 * pair, 2 * pair + 1):
                rank = level((res - head) % RES)
                if rank == 4:
                    sides.append(blended)
                elif rank == 3:
                    sides.append(wide[res, :, lanes])
                else:
                    sides.append(close[close_part][res, :, close_lanes])
            rows = jnp.where(low, *sides)
            for block in range(4):
                grid_rows[block, res * 16 : (res + 1) * 16, lanes] = rows[
                    block * 16 : (block + 1) * 16, :
                ]
    swap = swap_matrix()
    index = lax.broadcasted_iota(jnp.int32, (256, WIDTH), 0)
    copies = []
    for block in range(4):
        rows = jnp.dot(swap, grid_rows[block], preferred_element_type=F32)
        position = device * ROWS + block * 256 + index
        ready[block] = jnp.where(position < bound, rows, 0.0).astype(BF)
        copies.append(
            pltpu.make_async_copy(ready.at[block], out.at[pl.ds(block * 256, 256)], sent.at[block])
        )
        copies[-1].start()
    for copy in copies:
        copy.wait()


def smem():
    return pl.BlockSpec(memory_space=pltpu.SMEM)


def vmem():
    return pl.BlockSpec(memory_space=pltpu.VMEM)


def whole(shape):
    return pl.BlockSpec(shape, lambda i: (0,) * len(shape))


def params(mib):
    return pltpu.CompilerParams(vmem_limit_bytes=mib * 1024 * 1024)


def shape(dims, dtype=BF):
    return jax.ShapeDtypeStruct(dims, dtype)


def by_residue():
    return pl.BlockSpec((RES, GROUPS, 128), lambda i: (0, 0, i))


def by_part(parts):
    return pl.BlockSpec((parts, 2, GROUPS, 128), lambda i: (0, 0, 0, i))


def flat(block):
    return pl.BlockSpec((GROUPS, 128), lambda i: (0, i))


def reordered(rows):
    return pl.pallas_call(
        reorder,
        in_specs=[vmem()],
        out_specs=vmem(),
        out_shape=shape((RES, GROUPS, WIDTH)),
        compiler_params=params(20),
        name="residue_order",
    )(rows)


def split(meta, q, k, v):
    kt, vt = reordered(k), reordered(v)
    qt, *rest = pl.pallas_call(
        split_kernel,
        in_specs=[smem()] + [vmem()] * 3,
        out_specs=[vmem()] * 7,
        out_shape=[
            shape((RES, GROUPS, WIDTH)),
            shape((4, 2, GROUPS, WIDTH)),
            shape((2, 2, GROUPS, WIDTH)),
        ]
        + [shape((GROUPS, 640))] * 4,
        scratch_shapes=[pltpu.VMEM((4, GROUPS, 640), BF)],
        compiler_params=params(20),
        name="split_rows",
    )(meta, q, kt, vt)
    return qt, kt, vt, *rest


def local_near(first, many, meta, q, k, v, sel):
    return pl.pallas_call(
        functools.partial(local_kernel, "ABC", first, many),
        in_specs=[smem()] + [vmem()] * 4,
        out_specs=vmem(),
        out_shape=shape((RES, GROUPS, many * 128)),
        compiler_params=params(40),
        cost_estimate=pl.CostEstimate(
            flops=many * 600000000, bytes_accessed=1000000, transcendentals=many * 1200000
        ),
        name="near_queries",
    )(meta, q, k, v, sel)


def local_far(meta, q, k, v, sel, near, cross):
    return pl.pallas_call(
        functools.partial(local_kernel, "D", 0, PAIRS),
        in_specs=[smem()] + [vmem()] * 6,
        out_specs=[vmem()] * 3,
        out_shape=[
            shape((RES, GROUPS, WIDTH)),
            shape((GROUPS, WIDTH), F32),
            shape((GROUPS, WIDTH), F32),
        ],
        compiler_params=params(40),
        cost_estimate=pl.CostEstimate(
            flops=1000000000, bytes_accessed=1000000, transcendentals=2000000
        ),
        name="wide_queries",
    )(meta, q, k, v, sel, near, cross)


def slide_wide(meta, queries, blocks):
    return pl.pallas_call(
        far_kernel,
        in_specs=[smem()] + [vmem()] * 12,
        out_specs=[vmem()] * 4,
        out_shape=[shape((GROUPS, 256))] * 4,
        compiler_params=params(40),
        cost_estimate=pl.CostEstimate(flops=800000000, bytes_accessed=2000000, transcendentals=1600000),
        name="slide_queries",
    )(meta, *queries, *blocks)


def merge(meta, close, wide, back):
    return pl.pallas_call(
        merge_kernel,
        in_specs=[smem()] + [vmem()] * (len(NEAR_PARTS) + 7),
        out_specs=pl.BlockSpec(memory_space=pltpu.HBM),
        out_shape=shape((ROWS, WIDTH)),
        scratch_shapes=[
            pltpu.VMEM((4, GROUPS, 256), F32),
            pltpu.VMEM((4, 256, WIDTH), BF),
            pltpu.VMEM((4, 256, WIDTH), BF),
            pltpu.SemaphoreType.DMA((4,)),
        ],
        compiler_params=params(40),
        name="merge_rows",
    )(meta, *close, *wide, *back)


def at(x, z, c):
    return (x % NX * NZ + z % NZ) * NC + c


def move(block, to):
    route = [
        (at(x, z, c), at(*to(x, z, c))) for x in range(NX) for z in range(NZ) for c in range(NC)
    ]
    return lax.ppermute(block, "seq", route)


def along_x(steps):
    return lambda x, z, c: (x + steps, z, c)


def along_z(steps):
    return lambda x, z, c: (x, z + steps, c)


def other_core(x, z, c):
    return (x, z, 1 - c)


def next_chip(x, z, c):
    return (x, z ^ 1, c)


def per_device(query_tiles, key_tiles, value_tiles, slide_length):
    device = lax.axis_index("seq").astype(jnp.int32)
    meta = jnp.stack([slide_length[0], device])
    qt, kt, vt, sel, sel8, z0, z1, z2, z3 = split(meta, query_tiles, key_tiles, value_tiles)
    slabs = [z0] + [move(slab, along_z(step)) for step, slab in ((1, z1), (2, z2), (3, z3))]
    pair = move(sel, other_core)
    local = (qt, kt, vt, pair)
    close = [local_near(*NEAR_PARTS[0], meta, *local)]
    slabs, close[0], sel8, later = lax.optimization_barrier((slabs, close[0], sel8, meta))
    own = jnp.concatenate([slab[:, 256:640] for slab in slabs], axis=0)
    own, later = lax.optimization_barrier((own, later))
    moved = [move(own, along_x(step)) for step in (1, 2, 3)]
    near = move(sel8, next_chip)
    close.append(local_near(*NEAR_PARTS[1], later, *local))
    moved, near, close[1], later = lax.optimization_barrier((moved, near, close[1], later))
    cross = move(near, other_core)
    blocks = [own] + moved
    blocks += [move(block, other_core) for block in blocks]
    close.append(local_near(*NEAR_PARTS[2], later, *local))
    blocks, close[2], later = lax.optimization_barrier((blocks, close[2], later))
    back = slide_wide(meta, [slab[:, 0:256] for slab in slabs], blocks)
    back, later = lax.optimization_barrier((back, later))
    back = [back[0]] + [move(back[step], along_z(-step)) for step in (1, 2, 3)]
    wide = local_far(later, *local, near, cross)
    return merge(meta, close, wide, back)


def solution(mesh):
    placed = (
        P(("slide", "seq"), None),
        P(("slide", "seq"), None),
        P(("slide", "seq"), None),
        P("slide"),
    )
    return jax.shard_map(
        per_device, mesh=mesh, in_specs=placed, out_specs=P(("slide", "seq"), None), check_vma=False
    )
```

```python
import functools

import jax
import jax.numpy as jnp
import numpy as np
from jax import lax
from jax.experimental import pallas as pl
from jax.experimental.pallas import tpu as pltpu
from jax.sharding import PartitionSpec as P

HEADS = 12
HEAD_DIM = 64
WIDTH = 768
ROWS = 1024
RES = 16
GROUPS = ROWS // RES
HALF = GROUPS // 2
PAIRS = HEADS // 2
NX, NZ, NC = 4, 4, 2
MASKED = -1e30

BF = jnp.bfloat16
F32 = jnp.float32

ODD = [1, 3, 5, 7, 9, 11, 13, 15]
SHARED = [0, 8, 4, 12]
CLASS_U = {"A": ODD, "B": [2, 6, 10, 14], "C": [4, 12], "D": [8, 0]}
PAIR_OF = [0, 2, 3, 5]
LONE_OF = [2, 3, 8, 9]
NEAR_PARTS = [(0, 1), (1, 5)]
WIDE_PARTS = [(0, 3), (3, 3)]


def level(u):
    return 4 if u == 0 else min((u & -u).bit_length() - 1, 4)


def swap_matrix():
    row = lax.broadcasted_iota(jnp.int32, (256, 256), 0)
    col = lax.broadcasted_iota(jnp.int32, (256, 256), 1)
    return jnp.where(((row & 15) * 16 + (row >> 4)) == col, 1.0, 0.0).astype(BF)


def lane_low(rows):
    return lax.broadcasted_iota(jnp.int32, (rows, 128), 1) < 64


def split_kernel(
    meta, q_in, k_in, v_in, qt, kt, vt, sel, sel8, z0, z1, z2, z3, held, stage, arrived
):
    copies = []
    for at, source in enumerate((k_in, v_in, q_in)):
        copies.append(
            [
                pltpu.make_async_copy(
                    source.at[pl.ds(block * 256, 256)], held.at[at, block], arrived.at[at, block]
                )
                for block in range(4)
            ]
        )
    for copy in copies[0] + copies[1]:
        copy.start()
    swap = swap_matrix()
    for at, target in enumerate((kt, vt, qt)):
        for block in range(4):
            copies[at][block].wait()
            if at == 0:
                copies[2][block].start()
        for block in range(4):
            moved = jnp.dot(swap, held[at, block], preferred_element_type=F32).astype(BF)
            for res in range(RES):
                target[res, block * 16 : (block + 1) * 16, :] = moved[res * 16 : (res + 1) * 16, :]
    zpos = meta[1] // 2 % NZ
    low = lane_low(GROUPS)

    def other(rows):
        return pltpu.roll(rows.astype(F32), 64, 1).astype(BF)

    for pair in range(PAIRS):
        lanes = slice(pair * 128, pair * 128 + 128)

        def picked(ref, u):
            return jnp.where(
                low, ref[(u + 2 * pair) % RES, :, lanes], ref[(u + 2 * pair + 1) % RES, :, lanes]
            )

        for at, u in enumerate(SHARED):
            for kv, ref in enumerate((kt, vt)):
                rows = picked(ref, u)
                sel[at, kv, :, lanes] = rows
                if at < 2:
                    sel8[at, kv, :, lanes] = rows
                if at == 0 and kv == 0:
                    k0 = rows
                if at == 0 and kv == 1:
                    v0 = rows
        q0 = picked(qt, 0)
        for group in range(NZ):
            slot = (group - zpos) & 3
            if pair == PAIR_OF[group]:
                stage[slot, :, 0:128] = q0
                stage[slot, :, 256:384] = k0
                stage[slot, :, 384:512] = v0
            if pair == LONE_OF[group] // 2:
                if LONE_OF[group] % 2 == 0:
                    lone_q, lone_k, lone_v = q0, k0, other(v0)
                else:
                    lone_q, lone_k, lone_v = other(q0), other(k0), v0
                stage[slot, :, 128:256] = jnp.where(low, lone_q, jnp.zeros_like(lone_q))
                stage[slot, :, 512:640] = jnp.where(low, lone_k, lone_v)
    for slot, out in enumerate((z0, z1, z2, z3)):
        out[...] = stage[slot]


def local_kernel(classes, first, many, meta, *refs):
    def body(step, carry):
        lanes = pl.ds(pl.multiple_of((first + step) * 128, 128), 128)
        here = pl.ds(pl.multiple_of(step * 128, 128), 128)
        views = [ref.at[:, :, lanes] for ref in refs[:3]] + [refs[3].at[:, :, :, lanes]]
        if classes == "D":
            views += [ref.at[:, :, :, lanes] for ref in refs[4:6]]
            views += [refs[6].at[:, :, here]]
            views += [ref.at[:, here] for ref in refs[7:9]]
        else:
            views += [refs[4].at[:, :, here]]
        local_pair(classes, first + step, meta, *views)
        return carry

    lax.fori_loop(0, many, body, 0, unroll=True)


def local_pair(classes, pair, meta, q_ref, k_ref, v_ref, sel, *rest):
    far = classes == "D"
    if far:
        near, cross, out, o0, lse0 = rest
    else:
        (out,) = rest
    bound = meta[0]
    device = meta[1]
    lane = lax.broadcasted_iota(jnp.int32, (1, 256), 1)
    groups = [(name, 0) for name in classes] + [(name, 1) for name in classes[::-1]]
    caps = [("ABCD".index(name), side) for name, side in groups]
    starts = [0]
    for name, _ in groups:
        starts.append(starts[-1] + len(CLASS_U[name]) * HALF)
    low = lane_low(starts[-1])

    def rows_of(ref, tile):
        half, odd = tile // 2, tile % 2
        rows = slice(half * HALF, (half + 1) * HALF)
        return jnp.concatenate([ref[2 * at + odd, rows, :] for at in range(8)], axis=0)

    keys = [rows_of(k_ref, tile) for tile in range(4)] + [sel[:, 0].reshape(256, 128)]
    values = [rows_of(v_ref, tile) for tile in range(4)] + [sel[:, 1].reshape(256, 128)]
    if far:
        for kv, rows in enumerate((keys, values)):
            rows.append(
                jnp.concatenate([near[0, kv], near[1, kv], cross[0, kv], cross[1, kv]], axis=0)
            )

    def inside(tile, parity, cap, side):
        if tile >= 4:
            return cap >= tile - 2
        return side == tile // 2 or (tile % 2 == parity and cap >= 1)

    def bias(tile, parity, cap, side):
        head = 2 * pair + parity
        logs = jnp.zeros((1, 256), F32)
        if tile < 4:
            half, odd = tile // 2, tile % 2
            res = 2 * (lane >> 5) + odd
            position = device * ROWS + half * 512 + (lane & 31) * 16 + res
            if odd == parity and cap >= 1:
                u = (res - head) & 15
                extra = 1.0 if side == half else 0.0
                one, two, three = (float(np.log(extra + min(cap, rank))) for rank in (1, 2, 3))
                logs = jnp.where(
                    (u & 2) != 0, one, jnp.where((u & 4) != 0, two, three)
                ) + jnp.zeros((1, 256), F32)
        elif tile == 4:
            u = ((lane >> 6) & 1) * 8 + (lane >> 7) * 4
            position = (device ^ 1) * ROWS + (lane & 63) * 16 + ((u + head) & 15)
            if cap == 3:
                logs = jnp.where(lane < 128, float(np.log(2.0)), 0.0)
        else:
            u = ((lane >> 6) & 1) * 8
            source = jnp.where(lane < 128, device ^ 2, device ^ 3)
            position = source * ROWS + (lane & 63) * 16 + ((u + head) & 15)
        return jnp.where(position < bound, logs, MASKED)

    queries = []
    for parity in range(2):
        head = 2 * pair + parity
        query = jnp.concatenate(
            [
                q_ref[(u + head) & 15, side * HALF : (side + 1) * HALF, :]
                for name, side in groups
                for u in CLASS_U[name]
            ],
            axis=0,
        )
        mine = low if parity == 0 else jnp.logical_not(low)
        queries.append((jnp.where(mine, query, jnp.zeros_like(query)) * 0.125).astype(BF))
    scores, spans = {}, {}
    for tile, key in enumerate(keys):
        parts = []
        for parity in range(2):
            held = [at for at, (cap, side) in enumerate(caps) if inside(tile, parity, cap, side)]
            spans[tile, parity] = (held[0], held[-1] + 1)
            parts.append(queries[parity][starts[held[0]] : starts[held[-1] + 1]])
        both = lax.dot_general(
            jnp.concatenate(parts, axis=0),
            key,
            (((1,), (1,)), ((), ())),
            preferred_element_type=F32,
        )
        cut = parts[0].shape[0]
        scores[tile, 0], scores[tile, 1] = both[:cut], both[cut:]
    weights = {spot: [] for spot in spans}
    peaks = {}
    for parity in range(2):
        for at, (cap, side) in enumerate(caps):
            held = []
            for tile in range(len(keys)):
                first, last = spans[tile, parity]
                if first <= at < last:
                    base = starts[first]
                    held.append(
                        (
                            tile,
                            scores[tile, parity][starts[at] - base : starts[at + 1] - base]
                            + bias(tile, parity, cap, side),
                        )
                    )
            peak = functools.reduce(jnp.maximum, [score for _, score in held])
            peak = jnp.max(peak, axis=1, keepdims=True)
            peaks[parity, at] = peak
            for tile, score in held:
                weights[tile, parity].append(jnp.exp(score - peak).astype(BF))
    totals = {}
    for tile, value in enumerate(values):
        for parity in range(2):
            side = lane_low(256) if parity == 0 else jnp.logical_not(lane_low(256))
            part = jnp.dot(
                jnp.concatenate(weights[tile, parity], axis=0),
                jnp.where(side, value, jnp.ones_like(value)),
                preferred_element_type=F32,
            )
            base = 0
            for at in range(*spans[tile, parity]):
                count = starts[at + 1] - starts[at]
                rows = part[base : base + count]
                base += count
                spot = (parity, at)
                totals[spot] = totals[spot] + rows if spot in totals else rows
    for parity in range(2):
        head = 2 * pair + parity
        mine = low[:HALF] if parity == 0 else jnp.logical_not(low[:HALF])
        for at, (name, half) in enumerate(groups):
            total = totals[parity, at]
            sums = pltpu.roll(total, 64, 1)
            result = total / sums
            rounded = result.astype(BF)
            rows = slice(half * HALF, (half + 1) * HALF)
            for row, u in enumerate(CLASS_U[name]):
                spot = ((u + head) & 15, rows, slice(None))
                out[spot] = jnp.where(mine, rounded[row * HALF : (row + 1) * HALF, :], out[spot])
            if name == "D":
                log_total = peaks[parity, at][HALF:] + jnp.log(sums[HALF:])
                o0[rows, :] = jnp.where(mine, result[HALF:], o0[rows, :])
                lse0[rows, :] = jnp.where(mine, log_total, lse0[rows, :])


def far_kernel(meta, a0, a1, a2, a3, *rest):
    blocks, outs = rest[:8], rest[8:]
    bound = meta[0]
    device = meta[1]
    xpos, zpos, core = device // 8, device // 2 % NZ, device % 2
    low256 = lane_low(256)
    group = zpos
    lane = lax.broadcasted_iota(jnp.int32, (1, 256), 1)
    part = lane >> 6
    pair = jnp.where(group == 0, 0, jnp.where(group == 1, 4, jnp.where(group == 2, 6, 10)))
    lone = jnp.where(group == 0, 2, jnp.where(group == 1, 3, jnp.where(group == 2, 8, 9)))
    def positions(at, head):
        from_x = (xpos - at % 4) & 3
        from_c = core if at < 4 else 1 - core
        from_z = (zpos - part) & 3
        return ((from_x * NZ + from_z) * NC + from_c) * ROWS + (lane & 63) * 16 + head

    results = []
    for heads in ((0, 1), (2,)):
        lanes = slice(0, 128) if heads[0] == 0 else slice(128, 256)
        query = jnp.concatenate([source[:, lanes] for source in (a0, a1, a2, a3)], axis=0)
        query = (query * 0.125).astype(BF)
        sides = [jnp.logical_not(low256) if head else low256 for head in heads]
        queries = [jnp.where(side, query, jnp.zeros_like(query)) for side in sides]
        if heads[0] == 2:
            queries = [query]
        both = jnp.concatenate(queries, axis=0)
        key_lanes = slice(0, 128) if heads[0] == 0 else slice(256, 384)
        value_lanes = slice(128, 256) if heads[0] == 0 else slice(256, 384)
        scores = [
            lax.dot_general(
                both, block[:, key_lanes], (((1,), (1,)), ((), ())), preferred_element_type=F32
            )
            for block in blocks
        ]
        for at, head in enumerate(heads):
            mine = sides[at]
            held = [
                score[at * 256 : (at + 1) * 256]
                + jnp.where(positions(spot, (pair, pair + 1, lone)[head]) < bound, 0.0, MASKED)
                for spot, score in enumerate(scores)
            ]
            peak = jnp.max(functools.reduce(jnp.maximum, held), axis=1, keepdims=True)
            total = None
            for score, block in zip(held, blocks):
                value = block[:, value_lanes]
                weighed = jnp.dot(
                    jnp.exp(score - peak).astype(BF),
                    jnp.where(mine, value, jnp.ones_like(value)),
                    preferred_element_type=F32,
                )
                total = weighed if total is None else total + weighed
            sums = pltpu.roll(total, 64, 1)
            results.append((total / sums, peak + jnp.log(sums if head < 2 else total)))
    low = low256[:64]
    lane = lax.broadcasted_iota(jnp.int32, (64, 128), 1)
    for at, out in enumerate(outs):
        rows = slice(at * 64, (at + 1) * 64)
        out[:, 0:128] = jnp.where(low, results[0][0][rows], results[1][0][rows]).astype(BF)
        mixed = results[2][0][rows].astype(BF)
        for which, place in ((0, 0), (1, 64), (2, 0)):
            rest = results[which][1][rows, place : place + 1]
            for term in range(3):
                kept = rest.astype(BF)
                rest = rest - kept.astype(F32)
                mixed = jnp.where(lane == which * 3 + term, kept, mixed)
        out[:, 128:256] = mixed


def part_of(parts, pair):
    for at, (first, many) in enumerate(parts):
        if first <= pair < first + many:
            return at, slice((pair - first) * 128, (pair - first) * 128 + 128)


def merge_kernel(meta, *refs):
    count = len(NEAR_PARTS)
    close, refs = refs[:count], refs[count:]
    count = len(WIDE_PARTS)
    wide, o0, lse0 = refs[:count], refs[count : 2 * count], refs[2 * count : 3 * count]
    r0, r1, r2, r3, out, stage, grid_rows, ready, sent = refs[3 * count :]
    bound = meta[0]
    device = meta[1]
    zpos = device // 2 % NZ
    for slot, ref in enumerate((r0, r1, r2, r3)):
        stage[slot] = ref[...].astype(F32)
    low = lane_low(GROUPS)

    def log_of(slot, which):
        terms = [stage[slot, :, 128 + which * 3 + term : 129 + which * 3 + term] for term in range(3)]
        return terms[0] + terms[1] + terms[2]

    for pair in range(PAIRS):
        lanes = slice(pair * 128, pair * 128 + 128)
        close_part, close_lanes = part_of(NEAR_PARTS, pair)
        wide_part, wide_lanes = part_of(WIDE_PARTS, pair)
        if pair in PAIR_OF:
            slot = (PAIR_OF.index(pair) - zpos) & 3
            away = stage[slot, :, 0:128]
            away_lse = jnp.where(low, log_of(slot, 0), log_of(slot, 1))
        else:
            left = (LONE_OF.index(2 * pair) - zpos) & 3
            right = (left + 1) & 3
            away = jnp.where(low, pltpu.roll(stage[left, :, 128:256], 64, 1), stage[right, :, 128:256])
            away_lse = jnp.where(low, log_of(left, 2), log_of(right, 2))
        here, here_lse = o0[wide_part][:, wide_lanes], lse0[wide_part][:, wide_lanes]
        top = jnp.maximum(here_lse, away_lse)
        weight = jnp.exp(here_lse - top)
        away_weight = jnp.exp(away_lse - top)
        blended = (here * weight + away * away_weight) / (weight + away_weight)
        blended = blended.astype(BF)
        for res in range(RES):
            sides = []
            for head in (2 * pair, 2 * pair + 1):
                rank = level((res - head) % RES)
                if rank == 4:
                    sides.append(blended)
                elif rank == 3:
                    sides.append(wide[wide_part][res, :, wide_lanes])
                else:
                    sides.append(close[close_part][res, :, close_lanes])
            rows = jnp.where(low, *sides)
            for block in range(4):
                grid_rows[block, res * 16 : (res + 1) * 16, lanes] = rows[
                    block * 16 : (block + 1) * 16, :
                ]
    swap = swap_matrix()
    index = lax.broadcasted_iota(jnp.int32, (256, WIDTH), 0)
    copies = []
    for block in range(4):
        rows = jnp.dot(swap, grid_rows[block], preferred_element_type=F32)
        position = device * ROWS + block * 256 + index
        ready[block] = jnp.where(position < bound, rows, 0.0).astype(BF)
        copies.append(
            pltpu.make_async_copy(ready.at[block], out.at[pl.ds(block * 256, 256)], sent.at[block])
        )
        copies[-1].start()
    for copy in copies:
        copy.wait()


def smem():
    return pl.BlockSpec(memory_space=pltpu.SMEM)


def vmem():
    return pl.BlockSpec(memory_space=pltpu.VMEM)


def whole(shape):
    return pl.BlockSpec(shape, lambda i: (0,) * len(shape))


def params(mib):
    return pltpu.CompilerParams(vmem_limit_bytes=mib * 1024 * 1024)


def shape(dims, dtype=BF):
    return jax.ShapeDtypeStruct(dims, dtype)


def by_residue():
    return pl.BlockSpec((RES, GROUPS, 128), lambda i: (0, 0, i))


def by_part(parts):
    return pl.BlockSpec((parts, 2, GROUPS, 128), lambda i: (0, 0, 0, i))


def flat(block):
    return pl.BlockSpec((GROUPS, 128), lambda i: (0, i))


def split(meta, q, k, v):
    rows = [pltpu.with_memory_space_constraint(array, pltpu.HBM) for array in (q, k, v)]
    return pl.pallas_call(
        split_kernel,
        in_specs=[smem()] + [pl.BlockSpec(memory_space=pltpu.HBM)] * 3,
        out_specs=[vmem()] * 9,
        out_shape=[shape((RES, GROUPS, WIDTH))] * 3
        + [shape((4, 2, GROUPS, WIDTH)), shape((2, 2, GROUPS, WIDTH))]
        + [shape((GROUPS, 640))] * 4,
        scratch_shapes=[
            pltpu.VMEM((3, 4, 256, WIDTH), BF),
            pltpu.VMEM((4, GROUPS, 640), BF),
            pltpu.SemaphoreType.DMA((3, 4)),
        ],
        compiler_params=params(40),
        name="split_rows",
    )(meta, *rows)


def local_near(first, many, meta, q, k, v, sel):
    return pl.pallas_call(
        functools.partial(local_kernel, "ABC", first, many),
        in_specs=[smem()] + [vmem()] * 4,
        out_specs=vmem(),
        out_shape=shape((RES, GROUPS, many * 128)),
        compiler_params=params(40),
        cost_estimate=pl.CostEstimate(
            flops=many * 600000000, bytes_accessed=1000000, transcendentals=many * 1200000
        ),
        name="near_queries",
    )(meta, q, k, v, sel)


def local_far(first, many, meta, q, k, v, sel, near, cross):
    return pl.pallas_call(
        functools.partial(local_kernel, "D", first, many),
        in_specs=[smem()] + [vmem()] * 6,
        out_specs=[vmem()] * 3,
        out_shape=[
            shape((RES, GROUPS, many * 128)),
            shape((GROUPS, many * 128), F32),
            shape((GROUPS, many * 128), F32),
        ],
        compiler_params=params(40),
        cost_estimate=pl.CostEstimate(
            flops=many * 200000000, bytes_accessed=1000000, transcendentals=many * 400000
        ),
        name="wide_queries",
    )(meta, q, k, v, sel, near, cross)


def slide_wide(meta, queries, blocks):
    return pl.pallas_call(
        far_kernel,
        in_specs=[smem()] + [vmem()] * 12,
        out_specs=[vmem()] * 4,
        out_shape=[shape((GROUPS, 256))] * 4,
        compiler_params=params(40),
        cost_estimate=pl.CostEstimate(flops=800000000, bytes_accessed=2000000, transcendentals=1600000),
        name="slide_queries",
    )(meta, *queries, *blocks)


def merge(meta, close, wide, back):
    return pl.pallas_call(
        merge_kernel,
        in_specs=[smem()] + [vmem()] * (len(NEAR_PARTS) + 3 * len(WIDE_PARTS) + 4),
        out_specs=pl.BlockSpec(memory_space=pltpu.HBM),
        out_shape=shape((ROWS, WIDTH)),
        scratch_shapes=[
            pltpu.VMEM((4, GROUPS, 256), F32),
            pltpu.VMEM((4, 256, WIDTH), BF),
            pltpu.VMEM((4, 256, WIDTH), BF),
            pltpu.SemaphoreType.DMA((4,)),
        ],
        compiler_params=params(40),
        name="merge_rows",
    )(meta, *close, *[part for parts in zip(*wide) for part in parts], *back)


def at(x, z, c):
    return (x % NX * NZ + z % NZ) * NC + c


def move(block, to):
    route = [
        (at(x, z, c), at(*to(x, z, c))) for x in range(NX) for z in range(NZ) for c in range(NC)
    ]
    return lax.ppermute(block, "seq", route)


def along_x(steps):
    return lambda x, z, c: (x + steps, z, c)


def along_z(steps):
    return lambda x, z, c: (x, z + steps, c)


def other_core(x, z, c):
    return (x, z, 1 - c)


def next_chip(x, z, c):
    return (x, z ^ 1, c)


def per_device(query_tiles, key_tiles, value_tiles, slide_length):
    device = lax.axis_index("seq").astype(jnp.int32)
    meta = jnp.stack([slide_length[0], device])
    qt, kt, vt, sel, sel8, z0, z1, z2, z3 = split(meta, query_tiles, key_tiles, value_tiles)
    slabs = [z0] + [move(slab, along_z(step)) for step, slab in ((1, z1), (2, z2), (3, z3))]
    pair = move(sel, other_core)
    local = (qt, kt, vt, pair)
    close = [local_near(*NEAR_PARTS[0], meta, *local)]
    slabs, close[0], sel8, later = lax.optimization_barrier((slabs, close[0], sel8, meta))
    own = jnp.concatenate([slab[:, 256:640] for slab in slabs], axis=0)
    own, later = lax.optimization_barrier((own, later))
    moved = [move(own, along_x(step)) for step in (1, 2, 3)]
    near = move(sel8, next_chip)
    close.append(local_near(*NEAR_PARTS[1], later, *local))
    moved, near, close[1], later = lax.optimization_barrier((moved, near, close[1], later))
    cross = move(near, other_core)
    blocks = [own] + moved
    blocks += [move(block, other_core) for block in blocks]
    wide = [local_far(*WIDE_PARTS[0], later, *local, near, cross)]
    blocks, wide[0], later = lax.optimization_barrier((blocks, wide[0], later))
    back = slide_wide(meta, [slab[:, 0:256] for slab in slabs], blocks)
    back, later = lax.optimization_barrier((back, later))
    back = [back[0]] + [move(back[step], along_z(-step)) for step in (1, 2, 3)]
    wide.append(local_far(*WIDE_PARTS[1], later, *local, near, cross))
    return merge(meta, close, wide, back)


def solution(mesh):
    placed = (
        P(("slide", "seq"), None),
        P(("slide", "seq"), None),
        P(("slide", "seq"), None),
        P("slide"),
    )
    return jax.shard_map(
        per_device, mesh=mesh, in_specs=placed, out_specs=P(("slide", "seq"), None), check_vma=False
    )
```

```python
import functools

import jax
import jax.numpy as jnp
import numpy as np
from jax import lax
from jax.experimental import pallas as pl
from jax.experimental.pallas import tpu as pltpu
from jax.sharding import PartitionSpec as P

HEADS = 12
HEAD_DIM = 64
WIDTH = 768
ROWS = 1024
RES = 16
GROUPS = ROWS // RES
HALF = GROUPS // 2
PAIRS = HEADS // 2
NX, NZ, NC = 4, 4, 2
MASKED = -1e30

BF = jnp.bfloat16
F32 = jnp.float32

ODD = [1, 3, 5, 7, 9, 11, 13, 15]
SHARED = [0, 8, 4, 12]
CLASS_U = {"A": ODD, "B": [2, 6, 10, 14], "C": [4, 12], "D": [8, 0]}
PAIR_OF = [0, 2, 3, 5]
LONE_OF = [2, 3, 8, 9]
NEAR_PARTS = [(0, 1), (1, 5)]
WIDE_PARTS = [(0, 2), (2, 4)]


def level(u):
    return 4 if u == 0 else min((u & -u).bit_length() - 1, 4)


def swap_matrix():
    row = lax.broadcasted_iota(jnp.int32, (256, 256), 0)
    col = lax.broadcasted_iota(jnp.int32, (256, 256), 1)
    return jnp.where(((row & 15) * 16 + (row >> 4)) == col, 1.0, 0.0).astype(BF)


def lane_low(rows):
    return lax.broadcasted_iota(jnp.int32, (rows, 128), 1) < 64


def split_kernel(
    meta, q_in, k_in, v_in, qt, kt, vt, sel, sel8, z0, z1, z2, z3, held, stage, arrived
):
    copies = []
    for at, source in enumerate((k_in, v_in, q_in)):
        copies.append(
            [
                pltpu.make_async_copy(
                    source.at[pl.ds(block * 256, 256)], held.at[at, block], arrived.at[at, block]
                )
                for block in range(4)
            ]
        )
    for copy in copies[0] + copies[1]:
        copy.start()
    swap = swap_matrix()
    for at, target in enumerate((kt, vt, qt)):
        for block in range(4):
            copies[at][block].wait()
            if at == 0:
                copies[2][block].start()
        for block in range(4):
            moved = jnp.dot(swap, held[at, block], preferred_element_type=F32).astype(BF)
            for res in range(RES):
                target[res, block * 16 : (block + 1) * 16, :] = moved[res * 16 : (res + 1) * 16, :]
    zpos = meta[1] // 2 % NZ
    low = lane_low(GROUPS)

    def other(rows):
        return pltpu.roll(rows.astype(F32), 64, 1).astype(BF)

    for pair in range(PAIRS):
        lanes = slice(pair * 128, pair * 128 + 128)

        def picked(ref, u):
            return jnp.where(
                low, ref[(u + 2 * pair) % RES, :, lanes], ref[(u + 2 * pair + 1) % RES, :, lanes]
            )

        for at, u in enumerate(SHARED):
            for kv, ref in enumerate((kt, vt)):
                rows = picked(ref, u)
                sel[at, kv, :, lanes] = rows
                if at < 2:
                    sel8[at, kv, :, lanes] = rows
                if at == 0 and kv == 0:
                    k0 = rows
                if at == 0 and kv == 1:
                    v0 = rows
        q0 = picked(qt, 0)
        for group in range(NZ):
            slot = group ^ zpos
            if pair == PAIR_OF[group]:
                stage[slot, :, 0:128] = q0
                stage[slot, :, 256:384] = k0
                stage[slot, :, 384:512] = v0
            if pair == LONE_OF[group] // 2:
                if LONE_OF[group] % 2 == 0:
                    lone_q, lone_k, lone_v = q0, k0, other(v0)
                else:
                    lone_q, lone_k, lone_v = other(q0), other(k0), v0
                stage[slot, :, 128:256] = jnp.where(low, lone_q, jnp.zeros_like(lone_q))
                stage[slot, :, 512:640] = jnp.where(low, lone_k, lone_v)
    for slot, out in enumerate((z0, z1, z2, z3)):
        out[...] = stage[slot]


def local_kernel(classes, first, many, meta, *refs):
    def body(step, carry):
        lanes = pl.ds(pl.multiple_of((first + step) * 128, 128), 128)
        here = pl.ds(pl.multiple_of(step * 128, 128), 128)
        views = [ref.at[:, :, lanes] for ref in refs[:3]] + [refs[3].at[:, :, :, lanes]]
        if classes == "D":
            views += [ref.at[:, :, :, lanes] for ref in refs[4:6]]
            views += [refs[6].at[:, :, here]]
            views += [ref.at[:, here] for ref in refs[7:9]]
        else:
            views += [refs[4].at[:, :, here]]
        local_pair(classes, first + step, meta, *views)
        return carry

    lax.fori_loop(0, many, body, 0, unroll=True)


def local_pair(classes, pair, meta, q_ref, k_ref, v_ref, sel, *rest):
    far = classes == "D"
    if far:
        near, cross, out, o0, lse0 = rest
    else:
        (out,) = rest
    bound = meta[0]
    device = meta[1]
    lane = lax.broadcasted_iota(jnp.int32, (1, 256), 1)
    groups = [(name, 0) for name in classes] + [(name, 1) for name in classes[::-1]]
    caps = [("ABCD".index(name), side) for name, side in groups]
    starts = [0]
    for name, _ in groups:
        starts.append(starts[-1] + len(CLASS_U[name]) * HALF)
    low = lane_low(starts[-1])

    def rows_of(ref, tile):
        half, odd = tile // 2, tile % 2
        rows = slice(half * HALF, (half + 1) * HALF)
        return jnp.concatenate([ref[2 * at + odd, rows, :] for at in range(8)], axis=0)

    keys = [rows_of(k_ref, tile) for tile in range(4)] + [sel[:, 0].reshape(256, 128)]
    values = [rows_of(v_ref, tile) for tile in range(4)] + [sel[:, 1].reshape(256, 128)]
    if far:
        for kv, rows in enumerate((keys, values)):
            rows.append(
                jnp.concatenate([near[0, kv], near[1, kv], cross[0, kv], cross[1, kv]], axis=0)
            )

    def inside(tile, parity, cap, side):
        if tile >= 4:
            return cap >= tile - 2
        return side == tile // 2 or (tile % 2 == parity and cap >= 1)

    def bias(tile, parity, cap, side):
        head = 2 * pair + parity
        logs = jnp.zeros((1, 256), F32)
        if tile < 4:
            half, odd = tile // 2, tile % 2
            res = 2 * (lane >> 5) + odd
            position = device * ROWS + half * 512 + (lane & 31) * 16 + res
            if odd == parity and cap >= 1:
                u = (res - head) & 15
                extra = 1.0 if side == half else 0.0
                one, two, three = (float(np.log(extra + min(cap, rank))) for rank in (1, 2, 3))
                logs = jnp.where(
                    (u & 2) != 0, one, jnp.where((u & 4) != 0, two, three)
                ) + jnp.zeros((1, 256), F32)
        elif tile == 4:
            u = ((lane >> 6) & 1) * 8 + (lane >> 7) * 4
            position = (device ^ 1) * ROWS + (lane & 63) * 16 + ((u + head) & 15)
            if cap == 3:
                logs = jnp.where(lane < 128, float(np.log(2.0)), 0.0)
        else:
            u = ((lane >> 6) & 1) * 8
            source = jnp.where(lane < 128, device ^ 2, device ^ 3)
            position = source * ROWS + (lane & 63) * 16 + ((u + head) & 15)
        return jnp.where(position < bound, logs, MASKED)

    queries = []
    for parity in range(2):
        head = 2 * pair + parity
        query = jnp.concatenate(
            [
                q_ref[(u + head) & 15, side * HALF : (side + 1) * HALF, :]
                for name, side in groups
                for u in CLASS_U[name]
            ],
            axis=0,
        )
        mine = low if parity == 0 else jnp.logical_not(low)
        queries.append((jnp.where(mine, query, jnp.zeros_like(query)) * 0.125).astype(BF))
    scores, spans = {}, {}
    for tile, key in enumerate(keys):
        parts = []
        for parity in range(2):
            held = [at for at, (cap, side) in enumerate(caps) if inside(tile, parity, cap, side)]
            spans[tile, parity] = (held[0], held[-1] + 1)
            parts.append(queries[parity][starts[held[0]] : starts[held[-1] + 1]])
        both = lax.dot_general(
            jnp.concatenate(parts, axis=0),
            key,
            (((1,), (1,)), ((), ())),
            preferred_element_type=F32,
        )
        cut = parts[0].shape[0]
        scores[tile, 0], scores[tile, 1] = both[:cut], both[cut:]
    weights = {spot: [] for spot in spans}
    peaks = {}
    for parity in range(2):
        for at, (cap, side) in enumerate(caps):
            held = []
            for tile in range(len(keys)):
                first, last = spans[tile, parity]
                if first <= at < last:
                    base = starts[first]
                    held.append(
                        (
                            tile,
                            scores[tile, parity][starts[at] - base : starts[at + 1] - base]
                            + bias(tile, parity, cap, side),
                        )
                    )
            peak = functools.reduce(jnp.maximum, [score for _, score in held])
            peak = jnp.max(peak, axis=1, keepdims=True)
            peaks[parity, at] = peak
            for tile, score in held:
                weights[tile, parity].append(jnp.exp(score - peak).astype(BF))
    totals = {}
    for tile, value in enumerate(values):
        for parity in range(2):
            side = lane_low(256) if parity == 0 else jnp.logical_not(lane_low(256))
            part = jnp.dot(
                jnp.concatenate(weights[tile, parity], axis=0),
                jnp.where(side, value, jnp.ones_like(value)),
                preferred_element_type=F32,
            )
            base = 0
            for at in range(*spans[tile, parity]):
                count = starts[at + 1] - starts[at]
                rows = part[base : base + count]
                base += count
                spot = (parity, at)
                totals[spot] = totals[spot] + rows if spot in totals else rows
    for parity in range(2):
        head = 2 * pair + parity
        mine = low[:HALF] if parity == 0 else jnp.logical_not(low[:HALF])
        for at, (name, half) in enumerate(groups):
            total = totals[parity, at]
            sums = pltpu.roll(total, 64, 1)
            result = total / sums
            rounded = result.astype(BF)
            rows = slice(half * HALF, (half + 1) * HALF)
            for row, u in enumerate(CLASS_U[name]):
                spot = ((u + head) & 15, rows, slice(None))
                out[spot] = jnp.where(mine, rounded[row * HALF : (row + 1) * HALF, :], out[spot])
            if name == "D":
                log_total = peaks[parity, at][HALF:] + jnp.log(sums[HALF:])
                o0[rows, :] = jnp.where(mine, result[HALF:], o0[rows, :])
                lse0[rows, :] = jnp.where(mine, log_total, lse0[rows, :])


def far_kernel(meta, a0, a1, a2, a3, *rest):
    blocks, outs = rest[:8], rest[8:]
    bound = meta[0]
    device = meta[1]
    xpos, zpos, core = device // 8, device // 2 % NZ, device % 2
    low256 = lane_low(256)
    group = zpos
    lane = lax.broadcasted_iota(jnp.int32, (1, 256), 1)
    part = lane >> 6
    pair = jnp.where(group == 0, 0, jnp.where(group == 1, 4, jnp.where(group == 2, 6, 10)))
    lone = jnp.where(group == 0, 2, jnp.where(group == 1, 3, jnp.where(group == 2, 8, 9)))
    def positions(at, head):
        from_x = xpos ^ (at % 4)
        from_c = core if at < 4 else 1 - core
        from_z = zpos ^ part
        return ((from_x * NZ + from_z) * NC + from_c) * ROWS + (lane & 63) * 16 + head

    results = []
    for heads in ((0, 1), (2,)):
        lanes = slice(0, 128) if heads[0] == 0 else slice(128, 256)
        query = jnp.concatenate([source[:, lanes] for source in (a0, a1, a2, a3)], axis=0)
        query = (query * 0.125).astype(BF)
        sides = [jnp.logical_not(low256) if head else low256 for head in heads]
        queries = [jnp.where(side, query, jnp.zeros_like(query)) for side in sides]
        if heads[0] == 2:
            queries = [query]
        both = jnp.concatenate(queries, axis=0)
        key_lanes = slice(0, 128) if heads[0] == 0 else slice(256, 384)
        value_lanes = slice(128, 256) if heads[0] == 0 else slice(256, 384)
        scores = [
            lax.dot_general(
                both, block[:, key_lanes], (((1,), (1,)), ((), ())), preferred_element_type=F32
            )
            for block in blocks
        ]
        for at, head in enumerate(heads):
            mine = sides[at]
            held = [
                score[at * 256 : (at + 1) * 256]
                + jnp.where(positions(spot, (pair, pair + 1, lone)[head]) < bound, 0.0, MASKED)
                for spot, score in enumerate(scores)
            ]
            peak = jnp.max(functools.reduce(jnp.maximum, held), axis=1, keepdims=True)
            total = None
            for score, block in zip(held, blocks):
                value = block[:, value_lanes]
                weighed = jnp.dot(
                    jnp.exp(score - peak).astype(BF),
                    jnp.where(mine, value, jnp.ones_like(value)),
                    preferred_element_type=F32,
                )
                total = weighed if total is None else total + weighed
            sums = pltpu.roll(total, 64, 1)
            results.append((total / sums, peak + jnp.log(sums if head < 2 else total)))
    low = low256[:64]
    lane = lax.broadcasted_iota(jnp.int32, (64, 128), 1)
    for at, out in enumerate(outs):
        rows = slice(at * 64, (at + 1) * 64)
        out[:, 0:128] = jnp.where(low, results[0][0][rows], results[1][0][rows]).astype(BF)
        mixed = results[2][0][rows].astype(BF)
        for which, place in ((0, 0), (1, 64), (2, 0)):
            rest = results[which][1][rows, place : place + 1]
            for term in range(3):
                kept = rest.astype(BF)
                rest = rest - kept.astype(F32)
                mixed = jnp.where(lane == which * 3 + term, kept, mixed)
        out[:, 128:256] = mixed


def part_of(parts, pair):
    for at, (first, many) in enumerate(parts):
        if first <= pair < first + many:
            return at, slice((pair - first) * 128, (pair - first) * 128 + 128)


def merge_kernel(meta, *refs):
    count = len(NEAR_PARTS)
    close, refs = refs[:count], refs[count:]
    count = len(WIDE_PARTS)
    wide, o0, lse0 = refs[:count], refs[count : 2 * count], refs[2 * count : 3 * count]
    r0, r1, r2, r3, out, stage, grid_rows, ready, sent = refs[3 * count :]
    bound = meta[0]
    device = meta[1]
    zpos = device // 2 % NZ
    for slot, ref in enumerate((r0, r1, r2, r3)):
        stage[slot] = ref[...].astype(F32)
    low = lane_low(GROUPS)

    def log_of(slot, which):
        terms = [stage[slot, :, 128 + which * 3 + term : 129 + which * 3 + term] for term in range(3)]
        return terms[0] + terms[1] + terms[2]

    for pair in range(PAIRS):
        lanes = slice(pair * 128, pair * 128 + 128)
        close_part, close_lanes = part_of(NEAR_PARTS, pair)
        wide_part, wide_lanes = part_of(WIDE_PARTS, pair)
        if pair in PAIR_OF:
            slot = PAIR_OF.index(pair) ^ zpos
            away = stage[slot, :, 0:128]
            away_lse = jnp.where(low, log_of(slot, 0), log_of(slot, 1))
        else:
            left = LONE_OF.index(2 * pair) ^ zpos
            right = (LONE_OF.index(2 * pair) + 1) ^ zpos
            away = jnp.where(low, pltpu.roll(stage[left, :, 128:256], 64, 1), stage[right, :, 128:256])
            away_lse = jnp.where(low, log_of(left, 2), log_of(right, 2))
        here, here_lse = o0[wide_part][:, wide_lanes], lse0[wide_part][:, wide_lanes]
        top = jnp.maximum(here_lse, away_lse)
        weight = jnp.exp(here_lse - top)
        away_weight = jnp.exp(away_lse - top)
        blended = (here * weight + away * away_weight) / (weight + away_weight)
        blended = blended.astype(BF)
        for res in range(RES):
            sides = []
            for head in (2 * pair, 2 * pair + 1):
                rank = level((res - head) % RES)
                if rank == 4:
                    sides.append(blended)
                elif rank == 3:
                    sides.append(wide[wide_part][res, :, wide_lanes])
                else:
                    sides.append(close[close_part][res, :, close_lanes])
            rows = jnp.where(low, *sides)
            for block in range(4):
                grid_rows[block, res * 16 : (res + 1) * 16, lanes] = rows[
                    block * 16 : (block + 1) * 16, :
                ]
    swap = swap_matrix()
    index = lax.broadcasted_iota(jnp.int32, (256, WIDTH), 0)
    copies = []
    for block in range(4):
        rows = jnp.dot(swap, grid_rows[block], preferred_element_type=F32)
        position = device * ROWS + block * 256 + index
        ready[block] = jnp.where(position < bound, rows, 0.0).astype(BF)
        copies.append(
            pltpu.make_async_copy(ready.at[block], out.at[pl.ds(block * 256, 256)], sent.at[block])
        )
        copies[-1].start()
    for copy in copies:
        copy.wait()


def smem():
    return pl.BlockSpec(memory_space=pltpu.SMEM)


def vmem():
    return pl.BlockSpec(memory_space=pltpu.VMEM)


def whole(shape):
    return pl.BlockSpec(shape, lambda i: (0,) * len(shape))


def params(mib):
    return pltpu.CompilerParams(vmem_limit_bytes=mib * 1024 * 1024)


def shape(dims, dtype=BF):
    return jax.ShapeDtypeStruct(dims, dtype)


def by_residue():
    return pl.BlockSpec((RES, GROUPS, 128), lambda i: (0, 0, i))


def by_part(parts):
    return pl.BlockSpec((parts, 2, GROUPS, 128), lambda i: (0, 0, 0, i))


def flat(block):
    return pl.BlockSpec((GROUPS, 128), lambda i: (0, i))


def split(meta, q, k, v):
    rows = [pltpu.with_memory_space_constraint(array, pltpu.HBM) for array in (q, k, v)]
    return pl.pallas_call(
        split_kernel,
        in_specs=[smem()] + [pl.BlockSpec(memory_space=pltpu.HBM)] * 3,
        out_specs=[vmem()] * 9,
        out_shape=[shape((RES, GROUPS, WIDTH))] * 3
        + [shape((4, 2, GROUPS, WIDTH)), shape((2, 2, GROUPS, WIDTH))]
        + [shape((GROUPS, 640))] * 4,
        scratch_shapes=[
            pltpu.VMEM((3, 4, 256, WIDTH), BF),
            pltpu.VMEM((4, GROUPS, 640), BF),
            pltpu.SemaphoreType.DMA((3, 4)),
        ],
        compiler_params=params(40),
        name="split_rows",
    )(meta, *rows)


def local_near(first, many, meta, q, k, v, sel):
    return pl.pallas_call(
        functools.partial(local_kernel, "ABC", first, many),
        in_specs=[smem()] + [vmem()] * 4,
        out_specs=vmem(),
        out_shape=shape((RES, GROUPS, many * 128)),
        compiler_params=params(40),
        cost_estimate=pl.CostEstimate(
            flops=many * 600000000, bytes_accessed=1000000, transcendentals=many * 1200000
        ),
        name="near_queries",
    )(meta, q, k, v, sel)


def local_far(first, many, meta, q, k, v, sel, near, cross):
    return pl.pallas_call(
        functools.partial(local_kernel, "D", first, many),
        in_specs=[smem()] + [vmem()] * 6,
        out_specs=[vmem()] * 3,
        out_shape=[
            shape((RES, GROUPS, many * 128)),
            shape((GROUPS, many * 128), F32),
            shape((GROUPS, many * 128), F32),
        ],
        compiler_params=params(40),
        cost_estimate=pl.CostEstimate(
            flops=many * 200000000, bytes_accessed=1000000, transcendentals=many * 400000
        ),
        name="wide_queries",
    )(meta, q, k, v, sel, near, cross)


def slide_wide(meta, queries, blocks):
    return pl.pallas_call(
        far_kernel,
        in_specs=[smem()] + [vmem()] * 12,
        out_specs=[vmem()] * 4,
        out_shape=[shape((GROUPS, 256))] * 4,
        compiler_params=params(40),
        cost_estimate=pl.CostEstimate(flops=800000000, bytes_accessed=2000000, transcendentals=1600000),
        name="slide_queries",
    )(meta, *queries, *blocks)


def merge(meta, close, wide, back):
    return pl.pallas_call(
        merge_kernel,
        in_specs=[smem()] + [vmem()] * (len(NEAR_PARTS) + 3 * len(WIDE_PARTS) + 4),
        out_specs=pl.BlockSpec(memory_space=pltpu.HBM),
        out_shape=shape((ROWS, WIDTH)),
        scratch_shapes=[
            pltpu.VMEM((4, GROUPS, 256), F32),
            pltpu.VMEM((4, 256, WIDTH), BF),
            pltpu.VMEM((4, 256, WIDTH), BF),
            pltpu.SemaphoreType.DMA((4,)),
        ],
        compiler_params=params(40),
        name="merge_rows",
    )(meta, *close, *[part for parts in zip(*wide) for part in parts], *back)


def at(x, z, c):
    return (x * NZ + z) * NC + c


def move(block, to):
    route = [
        (at(x, z, c), at(*to(x, z, c))) for x in range(NX) for z in range(NZ) for c in range(NC)
    ]
    return lax.ppermute(block, "seq", route)


def along_x(steps):
    return lambda x, z, c: (x ^ steps, z, c)


def along_z(steps):
    return lambda x, z, c: (x, z ^ steps, c)


def other_core(x, z, c):
    return (x, z, 1 - c)


def next_chip(x, z, c):
    return (x, z ^ 1, c)


def per_device(query_tiles, key_tiles, value_tiles, slide_length):
    device = lax.axis_index("seq").astype(jnp.int32)
    meta = jnp.stack([slide_length[0], device])
    qt, kt, vt, sel, sel8, z0, z1, z2, z3 = split(meta, query_tiles, key_tiles, value_tiles)
    slabs = [z0] + [move(slab, along_z(step)) for step, slab in ((1, z1), (2, z2), (3, z3))]
    pair = move(sel, other_core)
    local = (qt, kt, vt, pair)
    close = [local_near(*NEAR_PARTS[0], meta, *local)]
    slabs, close[0], sel8, later = lax.optimization_barrier((slabs, close[0], sel8, meta))
    own = jnp.concatenate([slab[:, 256:640] for slab in slabs], axis=0)
    own, later = lax.optimization_barrier((own, later))
    moved = [move(own, along_x(step)) for step in (1, 2, 3)]
    near = move(sel8, next_chip)
    close.append(local_near(*NEAR_PARTS[1], later, *local))
    moved, near, close[1], later = lax.optimization_barrier((moved, near, close[1], later))
    cross = move(near, other_core)
    blocks = [own] + moved
    blocks += [move(block, other_core) for block in blocks]
    wide = [local_far(*WIDE_PARTS[0], later, *local, near, cross)]
    blocks, wide[0], later = lax.optimization_barrier((blocks, wide[0], later))
    back = slide_wide(meta, [slab[:, 0:256] for slab in slabs], blocks)
    back, later = lax.optimization_barrier((back, later))
    back = [back[0]] + [move(back[step], along_z(step)) for step in (1, 2, 3)]
    wide.append(local_far(*WIDE_PARTS[1], later, *local, near, cross))
    return merge(meta, close, wide, back)


def solution(mesh):
    placed = (
        P(("slide", "seq"), None),
        P(("slide", "seq"), None),
        P(("slide", "seq"), None),
        P("slide"),
    )
    return jax.shard_map(
        per_device, mesh=mesh, in_specs=placed, out_specs=P(("slide", "seq"), None), check_vma=False
    )
```

```python
import functools

import jax
import jax.numpy as jnp
import numpy as np
from jax import lax
from jax.experimental import pallas as pl
from jax.experimental.pallas import tpu as pltpu
from jax.sharding import PartitionSpec as P

HEADS = 12
HEAD_DIM = 64
WIDTH = 768
ROWS = 1024
RES = 16
GROUPS = ROWS // RES
HALF = GROUPS // 2
PAIRS = HEADS // 2
NX, NZ, NC = 4, 4, 2
MASKED = -1e30

BF = jnp.bfloat16
F32 = jnp.float32

ODD = [1, 3, 5, 7, 9, 11, 13, 15]
SHARED = [0, 8, 4, 12]
CLASS_U = {"A": ODD, "B": [2, 6, 10, 14], "C": [4, 12], "D": [8, 0]}
PAIR_OF = [0, 2, 3, 5]
LONE_OF = [2, 3, 8, 9]
NEAR_PARTS = [(0, 3), (3, 2), (5, 1)]
WIDE_PARTS = [(0, 2), (2, 4)]


def level(u):
    return 4 if u == 0 else min((u & -u).bit_length() - 1, 4)


def swap_matrix():
    row = lax.broadcasted_iota(jnp.int32, (256, 256), 0)
    col = lax.broadcasted_iota(jnp.int32, (256, 256), 1)
    return jnp.where(((row & 15) * 16 + (row >> 4)) == col, 1.0, 0.0).astype(BF)


def lane_low(rows):
    return lax.broadcasted_iota(jnp.int32, (rows, 128), 1) < 64


def split_kernel(
    meta, q_in, k_in, v_in, qt, kt, vt, sel, sel8, z0, z1, z2, z3, held, stage, arrived
):
    copies = []
    for at, source in enumerate((k_in, v_in, q_in)):
        copies.append(
            [
                pltpu.make_async_copy(
                    source.at[pl.ds(block * 256, 256)], held.at[at, block], arrived.at[at, block]
                )
                for block in range(4)
            ]
        )
    for copy in copies[0] + copies[1]:
        copy.start()
    swap = swap_matrix()
    for at, target in enumerate((kt, vt, qt)):
        for block in range(4):
            copies[at][block].wait()
            if at == 0:
                copies[2][block].start()
        for block in range(4):
            moved = jnp.dot(swap, held[at, block], preferred_element_type=F32).astype(BF)
            for res in range(RES):
                target[res, block * 16 : (block + 1) * 16, :] = moved[res * 16 : (res + 1) * 16, :]
    zpos = meta[1] // 2 % NZ
    low = lane_low(GROUPS)

    def other(rows):
        return pltpu.roll(rows.astype(F32), 64, 1).astype(BF)

    for pair in range(PAIRS):
        lanes = slice(pair * 128, pair * 128 + 128)

        def picked(ref, u):
            return jnp.where(
                low, ref[(u + 2 * pair) % RES, :, lanes], ref[(u + 2 * pair + 1) % RES, :, lanes]
            )

        for at, u in enumerate(SHARED):
            for kv, ref in enumerate((kt, vt)):
                rows = picked(ref, u)
                sel[at, kv, :, lanes] = rows
                if at < 2:
                    sel8[at, kv, :, lanes] = rows
                if at == 0 and kv == 0:
                    k0 = rows
                if at == 0 and kv == 1:
                    v0 = rows
        q0 = picked(qt, 0)
        for group in range(NZ):
            slot = group ^ zpos
            if pair == PAIR_OF[group]:
                stage[slot, :, 0:128] = q0
                stage[slot, :, 256:384] = k0
                stage[slot, :, 384:512] = v0
            if pair == LONE_OF[group] // 2:
                if LONE_OF[group] % 2 == 0:
                    lone_q, lone_k, lone_v = q0, k0, other(v0)
                else:
                    lone_q, lone_k, lone_v = other(q0), other(k0), v0
                stage[slot, :, 128:256] = jnp.where(low, lone_q, jnp.zeros_like(lone_q))
                stage[slot, :, 512:640] = jnp.where(low, lone_k, lone_v)
    for slot, out in enumerate((z0, z1, z2, z3)):
        out[...] = stage[slot]


def local_kernel(classes, first, many, meta, *refs):
    def body(step, carry):
        lanes = pl.ds(pl.multiple_of((first + step) * 128, 128), 128)
        here = pl.ds(pl.multiple_of(step * 128, 128), 128)
        views = [ref.at[:, :, lanes] for ref in refs[:3]] + [refs[3].at[:, :, :, lanes]]
        if classes == "D":
            views += [ref.at[:, :, :, lanes] for ref in refs[4:6]]
            views += [refs[6].at[:, :, here]]
            views += [ref.at[:, here] for ref in refs[7:9]]
        else:
            views += [refs[4].at[:, :, here]]
        local_pair(classes, first + step, meta, *views)
        return carry

    lax.fori_loop(0, many, body, 0, unroll=True)


def local_pair(classes, pair, meta, q_ref, k_ref, v_ref, sel, *rest):
    far = classes == "D"
    if far:
        near, cross, out, o0, lse0 = rest
    else:
        (out,) = rest
    bound = meta[0]
    device = meta[1]
    lane = lax.broadcasted_iota(jnp.int32, (1, 256), 1)
    groups = [(name, 0) for name in classes] + [(name, 1) for name in classes[::-1]]
    caps = [("ABCD".index(name), side) for name, side in groups]
    starts = [0]
    for name, _ in groups:
        starts.append(starts[-1] + len(CLASS_U[name]) * HALF)
    low = lane_low(starts[-1])

    def rows_of(ref, tile):
        half, odd = tile // 2, tile % 2
        rows = slice(half * HALF, (half + 1) * HALF)
        return jnp.concatenate([ref[2 * at + odd, rows, :] for at in range(8)], axis=0)

    keys = [rows_of(k_ref, tile) for tile in range(4)] + [sel[:, 0].reshape(256, 128)]
    values = [rows_of(v_ref, tile) for tile in range(4)] + [sel[:, 1].reshape(256, 128)]
    if far:
        for kv, rows in enumerate((keys, values)):
            rows.append(
                jnp.concatenate([near[0, kv], near[1, kv], cross[0, kv], cross[1, kv]], axis=0)
            )

    def inside(tile, parity, cap, side):
        if tile >= 4:
            return cap >= tile - 2
        return side == tile // 2 or (tile % 2 == parity and cap >= 1)

    def bias(tile, parity, cap, side):
        head = 2 * pair + parity
        logs = jnp.zeros((1, 256), F32)
        if tile < 4:
            half, odd = tile // 2, tile % 2
            res = 2 * (lane >> 5) + odd
            position = device * ROWS + half * 512 + (lane & 31) * 16 + res
            if odd == parity and cap >= 1:
                u = (res - head) & 15
                extra = 1.0 if side == half else 0.0
                one, two, three = (float(np.log(extra + min(cap, rank))) for rank in (1, 2, 3))
                logs = jnp.where(
                    (u & 2) != 0, one, jnp.where((u & 4) != 0, two, three)
                ) + jnp.zeros((1, 256), F32)
        elif tile == 4:
            u = ((lane >> 6) & 1) * 8 + (lane >> 7) * 4
            position = (device ^ 1) * ROWS + (lane & 63) * 16 + ((u + head) & 15)
            if cap == 3:
                logs = jnp.where(lane < 128, float(np.log(2.0)), 0.0)
        else:
            u = ((lane >> 6) & 1) * 8
            source = jnp.where(lane < 128, device ^ 2, device ^ 3)
            position = source * ROWS + (lane & 63) * 16 + ((u + head) & 15)
        return jnp.where(position < bound, logs, MASKED)

    queries = []
    for parity in range(2):
        head = 2 * pair + parity
        query = jnp.concatenate(
            [
                q_ref[(u + head) & 15, side * HALF : (side + 1) * HALF, :]
                for name, side in groups
                for u in CLASS_U[name]
            ],
            axis=0,
        )
        mine = low if parity == 0 else jnp.logical_not(low)
        queries.append((jnp.where(mine, query, jnp.zeros_like(query)) * 0.125).astype(BF))
    scores, spans = {}, {}
    for tile, key in enumerate(keys):
        parts = []
        for parity in range(2):
            held = [at for at, (cap, side) in enumerate(caps) if inside(tile, parity, cap, side)]
            spans[tile, parity] = (held[0], held[-1] + 1)
            parts.append(queries[parity][starts[held[0]] : starts[held[-1] + 1]])
        both = lax.dot_general(
            jnp.concatenate(parts, axis=0),
            key,
            (((1,), (1,)), ((), ())),
            preferred_element_type=F32,
        )
        cut = parts[0].shape[0]
        scores[tile, 0], scores[tile, 1] = both[:cut], both[cut:]
    weights = {spot: [] for spot in spans}
    peaks = {}
    for parity in range(2):
        for at, (cap, side) in enumerate(caps):
            held = []
            for tile in range(len(keys)):
                first, last = spans[tile, parity]
                if first <= at < last:
                    base = starts[first]
                    held.append(
                        (
                            tile,
                            scores[tile, parity][starts[at] - base : starts[at + 1] - base]
                            + bias(tile, parity, cap, side),
                        )
                    )
            peak = functools.reduce(jnp.maximum, [score for _, score in held])
            peak = jnp.max(peak, axis=1, keepdims=True)
            peaks[parity, at] = peak
            for tile, score in held:
                weights[tile, parity].append(jnp.exp(score - peak).astype(BF))
    totals = {}
    for tile, value in enumerate(values):
        for parity in range(2):
            side = lane_low(256) if parity == 0 else jnp.logical_not(lane_low(256))
            part = jnp.dot(
                jnp.concatenate(weights[tile, parity], axis=0),
                jnp.where(side, value, jnp.ones_like(value)),
                preferred_element_type=F32,
            )
            base = 0
            for at in range(*spans[tile, parity]):
                count = starts[at + 1] - starts[at]
                rows = part[base : base + count]
                base += count
                spot = (parity, at)
                totals[spot] = totals[spot] + rows if spot in totals else rows
    for parity in range(2):
        head = 2 * pair + parity
        mine = low[:HALF] if parity == 0 else jnp.logical_not(low[:HALF])
        for at, (name, half) in enumerate(groups):
            total = totals[parity, at]
            sums = pltpu.roll(total, 64, 1)
            result = total / sums
            rounded = result.astype(BF)
            rows = slice(half * HALF, (half + 1) * HALF)
            for row, u in enumerate(CLASS_U[name]):
                spot = ((u + head) & 15, rows, slice(None))
                out[spot] = jnp.where(mine, rounded[row * HALF : (row + 1) * HALF, :], out[spot])
            if name == "D":
                log_total = peaks[parity, at][HALF:] + jnp.log(sums[HALF:])
                o0[rows, :] = jnp.where(mine, result[HALF:], o0[rows, :])
                lse0[rows, :] = jnp.where(mine, log_total, lse0[rows, :])


def far_kernel(meta, a0, a1, a2, a3, *rest):
    blocks, outs = rest[:8], rest[8:]
    bound = meta[0]
    device = meta[1]
    xpos, zpos, core = device // 8, device // 2 % NZ, device % 2
    low256 = lane_low(256)
    group = zpos
    lane = lax.broadcasted_iota(jnp.int32, (1, 256), 1)
    part = lane >> 6
    pair = jnp.where(group == 0, 0, jnp.where(group == 1, 4, jnp.where(group == 2, 6, 10)))
    lone = jnp.where(group == 0, 2, jnp.where(group == 1, 3, jnp.where(group == 2, 8, 9)))
    def positions(at, head):
        from_x = xpos ^ (at % 4)
        from_c = core if at < 4 else 1 - core
        from_z = zpos ^ part
        return ((from_x * NZ + from_z) * NC + from_c) * ROWS + (lane & 63) * 16 + head

    results = []
    for heads in ((0, 1), (2,)):
        lanes = slice(0, 128) if heads[0] == 0 else slice(128, 256)
        query = jnp.concatenate([source[:, lanes] for source in (a0, a1, a2, a3)], axis=0)
        query = (query * 0.125).astype(BF)
        sides = [jnp.logical_not(low256) if head else low256 for head in heads]
        queries = [jnp.where(side, query, jnp.zeros_like(query)) for side in sides]
        if heads[0] == 2:
            queries = [query]
        both = jnp.concatenate(queries, axis=0)
        key_lanes = slice(0, 128) if heads[0] == 0 else slice(256, 384)
        value_lanes = slice(128, 256) if heads[0] == 0 else slice(256, 384)
        scores = [
            lax.dot_general(
                both, block[:, key_lanes], (((1,), (1,)), ((), ())), preferred_element_type=F32
            )
            for block in blocks
        ]
        for at, head in enumerate(heads):
            mine = sides[at]
            held = [
                score[at * 256 : (at + 1) * 256]
                + jnp.where(positions(spot, (pair, pair + 1, lone)[head]) < bound, 0.0, MASKED)
                for spot, score in enumerate(scores)
            ]
            peak = jnp.max(functools.reduce(jnp.maximum, held), axis=1, keepdims=True)
            total = None
            for score, block in zip(held, blocks):
                value = block[:, value_lanes]
                weighed = jnp.dot(
                    jnp.exp(score - peak).astype(BF),
                    jnp.where(mine, value, jnp.ones_like(value)),
                    preferred_element_type=F32,
                )
                total = weighed if total is None else total + weighed
            sums = pltpu.roll(total, 64, 1)
            results.append((total / sums, peak + jnp.log(sums if head < 2 else total)))
    low = low256[:64]
    lane = lax.broadcasted_iota(jnp.int32, (64, 128), 1)
    for at, out in enumerate(outs):
        rows = slice(at * 64, (at + 1) * 64)
        out[:, 0:128] = jnp.where(low, results[0][0][rows], results[1][0][rows]).astype(BF)
        mixed = results[2][0][rows].astype(BF)
        for which, place in ((0, 0), (1, 64), (2, 0)):
            rest = results[which][1][rows, place : place + 1]
            for term in range(3):
                kept = rest.astype(BF)
                rest = rest - kept.astype(F32)
                mixed = jnp.where(lane == which * 3 + term, kept, mixed)
        out[:, 128:256] = mixed


def part_of(parts, pair):
    for at, (first, many) in enumerate(parts):
        if first <= pair < first + many:
            return at, slice((pair - first) * 128, (pair - first) * 128 + 128)


def merge_kernel(meta, *refs):
    count = len(NEAR_PARTS)
    close, refs = refs[:count], refs[count:]
    count = len(WIDE_PARTS)
    wide, o0, lse0 = refs[:count], refs[count : 2 * count], refs[2 * count : 3 * count]
    r0, r1, r2, r3, out, stage, grid_rows, ready, sent = refs[3 * count :]
    bound = meta[0]
    device = meta[1]
    zpos = device // 2 % NZ
    for slot, ref in enumerate((r0, r1, r2, r3)):
        stage[slot] = ref[...].astype(F32)
    low = lane_low(GROUPS)

    def log_of(slot, which):
        terms = [stage[slot, :, 128 + which * 3 + term : 129 + which * 3 + term] for term in range(3)]
        return terms[0] + terms[1] + terms[2]

    for pair in range(PAIRS):
        lanes = slice(pair * 128, pair * 128 + 128)
        close_part, close_lanes = part_of(NEAR_PARTS, pair)
        wide_part, wide_lanes = part_of(WIDE_PARTS, pair)
        if pair in PAIR_OF:
            slot = PAIR_OF.index(pair) ^ zpos
            away = stage[slot, :, 0:128]
            away_lse = jnp.where(low, log_of(slot, 0), log_of(slot, 1))
        else:
            left = LONE_OF.index(2 * pair) ^ zpos
            right = (LONE_OF.index(2 * pair) + 1) ^ zpos
            away = jnp.where(low, pltpu.roll(stage[left, :, 128:256], 64, 1), stage[right, :, 128:256])
            away_lse = jnp.where(low, log_of(left, 2), log_of(right, 2))
        here, here_lse = o0[wide_part][:, wide_lanes], lse0[wide_part][:, wide_lanes]
        top = jnp.maximum(here_lse, away_lse)
        weight = jnp.exp(here_lse - top)
        away_weight = jnp.exp(away_lse - top)
        blended = (here * weight + away * away_weight) / (weight + away_weight)
        blended = blended.astype(BF)
        for res in range(RES):
            sides = []
            for head in (2 * pair, 2 * pair + 1):
                rank = level((res - head) % RES)
                if rank == 4:
                    sides.append(blended)
                elif rank == 3:
                    sides.append(wide[wide_part][res, :, wide_lanes])
                else:
                    sides.append(close[close_part][res, :, close_lanes])
            rows = jnp.where(low, *sides)
            for block in range(4):
                grid_rows[block, res * 16 : (res + 1) * 16, lanes] = rows[
                    block * 16 : (block + 1) * 16, :
                ]
    swap = swap_matrix()
    index = lax.broadcasted_iota(jnp.int32, (256, WIDTH), 0)
    copies = []
    for block in range(4):
        rows = jnp.dot(swap, grid_rows[block], preferred_element_type=F32)
        position = device * ROWS + block * 256 + index
        ready[block] = jnp.where(position < bound, rows, 0.0).astype(BF)
        copies.append(
            pltpu.make_async_copy(ready.at[block], out.at[pl.ds(block * 256, 256)], sent.at[block])
        )
        copies[-1].start()
    for copy in copies:
        copy.wait()


def smem():
    return pl.BlockSpec(memory_space=pltpu.SMEM)


def vmem():
    return pl.BlockSpec(memory_space=pltpu.VMEM)


def whole(shape):
    return pl.BlockSpec(shape, lambda i: (0,) * len(shape))


def params(mib):
    return pltpu.CompilerParams(vmem_limit_bytes=mib * 1024 * 1024)


def shape(dims, dtype=BF):
    return jax.ShapeDtypeStruct(dims, dtype)


def by_residue():
    return pl.BlockSpec((RES, GROUPS, 128), lambda i: (0, 0, i))


def by_part(parts):
    return pl.BlockSpec((parts, 2, GROUPS, 128), lambda i: (0, 0, 0, i))


def flat(block):
    return pl.BlockSpec((GROUPS, 128), lambda i: (0, i))


def split(meta, q, k, v):
    rows = [pltpu.with_memory_space_constraint(array, pltpu.HBM) for array in (q, k, v)]
    return pl.pallas_call(
        split_kernel,
        in_specs=[smem()] + [pl.BlockSpec(memory_space=pltpu.HBM)] * 3,
        out_specs=[vmem()] * 9,
        out_shape=[shape((RES, GROUPS, WIDTH))] * 3
        + [shape((4, 2, GROUPS, WIDTH)), shape((2, 2, GROUPS, WIDTH))]
        + [shape((GROUPS, 640))] * 4,
        scratch_shapes=[
            pltpu.VMEM((3, 4, 256, WIDTH), BF),
            pltpu.VMEM((4, GROUPS, 640), BF),
            pltpu.SemaphoreType.DMA((3, 4)),
        ],
        compiler_params=params(40),
        name="split_rows",
    )(meta, *rows)


def local_near(first, many, meta, q, k, v, sel):
    return pl.pallas_call(
        functools.partial(local_kernel, "ABC", first, many),
        in_specs=[smem()] + [vmem()] * 4,
        out_specs=vmem(),
        out_shape=shape((RES, GROUPS, many * 128)),
        compiler_params=params(40),
        cost_estimate=pl.CostEstimate(
            flops=many * 600000000, bytes_accessed=1000000, transcendentals=many * 1200000
        ),
        name="near_queries",
    )(meta, q, k, v, sel)


def local_far(first, many, meta, q, k, v, sel, near, cross):
    return pl.pallas_call(
        functools.partial(local_kernel, "D", first, many),
        in_specs=[smem()] + [vmem()] * 6,
        out_specs=[vmem()] * 3,
        out_shape=[
            shape((RES, GROUPS, many * 128)),
            shape((GROUPS, many * 128), F32),
            shape((GROUPS, many * 128), F32),
        ],
        compiler_params=params(40),
        cost_estimate=pl.CostEstimate(
            flops=many * 200000000, bytes_accessed=1000000, transcendentals=many * 400000
        ),
        name="wide_queries",
    )(meta, q, k, v, sel, near, cross)


def slide_wide(meta, queries, blocks):
    return pl.pallas_call(
        far_kernel,
        in_specs=[smem()] + [vmem()] * 12,
        out_specs=[vmem()] * 4,
        out_shape=[shape((GROUPS, 256))] * 4,
        compiler_params=params(40),
        cost_estimate=pl.CostEstimate(flops=800000000, bytes_accessed=2000000, transcendentals=1600000),
        name="slide_queries",
    )(meta, *queries, *blocks)


def merge(meta, close, wide, back):
    return pl.pallas_call(
        merge_kernel,
        in_specs=[smem()] + [vmem()] * (len(NEAR_PARTS) + 3 * len(WIDE_PARTS) + 4),
        out_specs=pl.BlockSpec(memory_space=pltpu.HBM),
        out_shape=shape((ROWS, WIDTH)),
        scratch_shapes=[
            pltpu.VMEM((4, GROUPS, 256), F32),
            pltpu.VMEM((4, 256, WIDTH), BF),
            pltpu.VMEM((4, 256, WIDTH), BF),
            pltpu.SemaphoreType.DMA((4,)),
        ],
        compiler_params=params(40),
        name="merge_rows",
    )(meta, *close, *[part for parts in zip(*wide) for part in parts], *back)


def at(x, z, c):
    return (x * NZ + z) * NC + c


def move(block, to):
    route = [
        (at(x, z, c), at(*to(x, z, c))) for x in range(NX) for z in range(NZ) for c in range(NC)
    ]
    return lax.ppermute(block, "seq", route)


def along_x(steps):
    return lambda x, z, c: (x ^ steps, z, c)


def along_z(steps):
    return lambda x, z, c: (x, z ^ steps, c)


def relay(x, z, c):
    return (x ^ (3 if c else 1), z, c)


def other_core(x, z, c):
    return (x, z, 1 - c)


def next_chip(x, z, c):
    return (x, z ^ 1, c)


def per_device(query_tiles, key_tiles, value_tiles, slide_length):
    device = lax.axis_index("seq").astype(jnp.int32)
    meta = jnp.stack([slide_length[0], device])
    qt, kt, vt, sel, sel8, z0, z1, z2, z3 = split(meta, query_tiles, key_tiles, value_tiles)
    slabs = [z0] + [move(slab, along_z(step)) for step, slab in ((1, z1), (2, z2), (3, z3))]
    pair = move(sel, other_core)
    local = (qt, kt, vt, pair)
    close = [local_near(*NEAR_PARTS[0], meta, *local)]
    slabs, close[0], sel8, later = lax.optimization_barrier((slabs, close[0], sel8, meta))
    own = jnp.concatenate([slab[:, 256:640] for slab in slabs], axis=0)
    own, later = lax.optimization_barrier((own, later))
    first, third = move(own, along_x(1)), move(own, along_x(3))
    near = move(sel8, next_chip)
    close.append(local_near(*NEAR_PARTS[1], later, *local))
    first, third, near, close[1], later = lax.optimization_barrier(
        (first, third, near, close[1], later)
    )
    relayed = move(jnp.where(device % 2 == 0, third, first), relay)
    others = [move(block, other_core) for block in (own, first, third)]
    cross = move(near, other_core)
    close.append(local_near(*NEAR_PARTS[2], later, *local))
    relayed, close[2], later = lax.optimization_barrier((relayed, close[2], later))
    others.insert(2, move(relayed, other_core))
    blocks = [own, first, relayed, third] + others
    wide = [local_far(*WIDE_PARTS[0], later, *local, near, cross)]
    blocks, wide[0], later = lax.optimization_barrier((blocks, wide[0], later))
    back = slide_wide(meta, [slab[:, 0:256] for slab in slabs], blocks)
    back, later = lax.optimization_barrier((back, later))
    back = [back[0]] + [move(back[step], along_z(step)) for step in (1, 2, 3)]
    wide.append(local_far(*WIDE_PARTS[1], later, *local, near, cross))
    return merge(meta, close, wide, back)


def solution(mesh):
    placed = (
        P(("slide", "seq"), None),
        P(("slide", "seq"), None),
        P(("slide", "seq"), None),
        P("slide"),
    )
    return jax.shard_map(
        per_device, mesh=mesh, in_specs=placed, out_specs=P(("slide", "seq"), None), check_vma=False
    )
```

```python
import functools

import jax
import jax.numpy as jnp
import numpy as np
from jax import lax
from jax.experimental import pallas as pl
from jax.experimental.pallas import tpu as pltpu
from jax.sharding import PartitionSpec as P

HEADS = 12
HEAD_DIM = 64
WIDTH = 768
ROWS = 1024
RES = 16
GROUPS = ROWS // RES
HALF = GROUPS // 2
PAIRS = HEADS // 2
NX, NZ, NC = 4, 4, 2
MASKED = -1e30

BF = jnp.bfloat16
F32 = jnp.float32

ODD = [1, 3, 5, 7, 9, 11, 13, 15]
SHARED = [0, 8, 4, 12]
CLASS_U = {"A": ODD, "B": [2, 6, 10, 14], "C": [4, 12], "D": [8, 0]}
PAIR_OF = [0, 2, 3, 5]
LONE_OF = [2, 3, 8, 9]
NEAR_PARTS = [(0, 3), (3, 2), (5, 1)]
WIDE_PARTS = [(0, 2), (2, 4)]


def level(u):
    return 4 if u == 0 else min((u & -u).bit_length() - 1, 4)


def swap_matrix():
    row = lax.broadcasted_iota(jnp.int32, (256, 256), 0)
    col = lax.broadcasted_iota(jnp.int32, (256, 256), 1)
    return jnp.where(((row & 15) * 16 + (row >> 4)) == col, 1.0, 0.0).astype(BF)


def lane_low(rows):
    return lax.broadcasted_iota(jnp.int32, (rows, 128), 1) < 64


def split_kernel(
    meta, q_in, k_in, v_in, qt, kt, vt, sel, sel8, z0, z1, z2, z3, held, stage, arrived
):
    copies = []
    for at, source in enumerate((k_in, v_in, q_in)):
        copies.append(
            [
                pltpu.make_async_copy(
                    source.at[pl.ds(block * 256, 256)], held.at[at, block], arrived.at[at, block]
                )
                for block in range(4)
            ]
        )
    for copy in copies[0] + copies[1]:
        copy.start()
    swap = swap_matrix()
    for at, target in enumerate((kt, vt, qt)):
        for block in range(4):
            copies[at][block].wait()
            if at == 0:
                copies[2][block].start()
        for block in range(4):
            moved = jnp.dot(swap, held[at, block], preferred_element_type=F32).astype(BF)
            for res in range(RES):
                target[res, block * 16 : (block + 1) * 16, :] = moved[res * 16 : (res + 1) * 16, :]
    zpos = meta[1] // 2 % NZ
    low = lane_low(GROUPS)

    def other(rows):
        return pltpu.roll(rows.astype(F32), 64, 1).astype(BF)

    for pair in range(PAIRS):
        lanes = slice(pair * 128, pair * 128 + 128)

        def picked(ref, u):
            return jnp.where(
                low, ref[(u + 2 * pair) % RES, :, lanes], ref[(u + 2 * pair + 1) % RES, :, lanes]
            )

        for at, u in enumerate(SHARED):
            for kv, ref in enumerate((kt, vt)):
                rows = picked(ref, u)
                sel[at, kv, :, lanes] = rows
                if at < 2:
                    sel8[at, kv, :, lanes] = rows
                if at == 0 and kv == 0:
                    k0 = rows
                if at == 0 and kv == 1:
                    v0 = rows
        q0 = picked(qt, 0)
        for group in range(NZ):
            slot = group ^ zpos
            if pair == PAIR_OF[group]:
                stage[slot, :, 0:128] = q0
                stage[slot, :, 256:384] = k0
                stage[slot, :, 384:512] = v0
            if pair == LONE_OF[group] // 2:
                if LONE_OF[group] % 2 == 0:
                    lone_q, lone_k, lone_v = q0, k0, other(v0)
                else:
                    lone_q, lone_k, lone_v = other(q0), other(k0), v0
                stage[slot, :, 128:256] = jnp.where(low, lone_q, jnp.zeros_like(lone_q))
                stage[slot, :, 512:640] = jnp.where(low, lone_k, lone_v)
    for slot, out in enumerate((z0, z1, z2, z3)):
        out[...] = stage[slot]


def local_kernel(classes, first, many, meta, *refs):
    def body(step, carry):
        lanes = pl.ds(pl.multiple_of((first + step) * 128, 128), 128)
        here = pl.ds(pl.multiple_of(step * 128, 128), 128)
        views = [ref.at[:, :, lanes] for ref in refs[:3]] + [refs[3].at[:, :, :, lanes]]
        if classes == "D":
            views += [ref.at[:, :, :, lanes] for ref in refs[4:6]]
            views += [refs[6].at[:, :, here]]
            views += [ref.at[:, here] for ref in refs[7:9]]
        else:
            views += [refs[4].at[:, :, here]]
        local_pair(classes, first + step, meta, *views)
        return carry

    lax.fori_loop(0, many, body, 0, unroll=True)


def local_pair(classes, pair, meta, q_ref, k_ref, v_ref, sel, *rest):
    far = classes == "D"
    if far:
        near, cross, out, o0, lse0 = rest
    else:
        (out,) = rest
    bound = meta[0]
    device = meta[1]
    lane = lax.broadcasted_iota(jnp.int32, (1, 256), 1)
    groups = [(name, 0) for name in classes] + [(name, 1) for name in classes[::-1]]
    caps = [("ABCD".index(name), side) for name, side in groups]
    starts = [0]
    for name, _ in groups:
        starts.append(starts[-1] + len(CLASS_U[name]) * HALF)
    low = lane_low(starts[-1])

    def rows_of(ref, tile):
        half, odd = tile // 2, tile % 2
        rows = slice(half * HALF, (half + 1) * HALF)
        return jnp.concatenate([ref[2 * at + odd, rows, :] for at in range(8)], axis=0)

    keys = [rows_of(k_ref, tile) for tile in range(4)] + [sel[:, 0].reshape(256, 128)]
    values = [rows_of(v_ref, tile) for tile in range(4)] + [sel[:, 1].reshape(256, 128)]
    if far:
        for kv, rows in enumerate((keys, values)):
            rows.append(
                jnp.concatenate([near[0, kv], near[1, kv], cross[0, kv], cross[1, kv]], axis=0)
            )

    def inside(tile, parity, cap, side):
        if tile >= 4:
            return cap >= tile - 2
        return side == tile // 2 or (tile % 2 == parity and cap >= 1)

    def bias(tile, parity, cap, side):
        head = 2 * pair + parity
        logs = jnp.zeros((1, 256), F32)
        if tile < 4:
            half, odd = tile // 2, tile % 2
            res = 2 * (lane >> 5) + odd
            position = device * ROWS + half * 512 + (lane & 31) * 16 + res
            if odd == parity and cap >= 1:
                u = (res - head) & 15
                extra = 1.0 if side == half else 0.0
                one, two, three = (float(np.log(extra + min(cap, rank))) for rank in (1, 2, 3))
                logs = jnp.where(
                    (u & 2) != 0, one, jnp.where((u & 4) != 0, two, three)
                ) + jnp.zeros((1, 256), F32)
        elif tile == 4:
            u = ((lane >> 6) & 1) * 8 + (lane >> 7) * 4
            position = (device ^ 1) * ROWS + (lane & 63) * 16 + ((u + head) & 15)
            if cap == 3:
                logs = jnp.where(lane < 128, float(np.log(2.0)), 0.0)
        else:
            u = ((lane >> 6) & 1) * 8
            source = jnp.where(lane < 128, device ^ 2, device ^ 3)
            position = source * ROWS + (lane & 63) * 16 + ((u + head) & 15)
        return jnp.where(position < bound, logs, MASKED)

    queries = []
    for parity in range(2):
        head = 2 * pair + parity
        query = jnp.concatenate(
            [
                q_ref[(u + head) & 15, side * HALF : (side + 1) * HALF, :]
                for name, side in groups
                for u in CLASS_U[name]
            ],
            axis=0,
        )
        mine = low if parity == 0 else jnp.logical_not(low)
        queries.append((jnp.where(mine, query, jnp.zeros_like(query)) * 0.125).astype(BF))
    scores, spans = {}, {}
    for tile, key in enumerate(keys):
        parts = []
        for parity in range(2):
            held = [at for at, (cap, side) in enumerate(caps) if inside(tile, parity, cap, side)]
            spans[tile, parity] = (held[0], held[-1] + 1)
            parts.append(queries[parity][starts[held[0]] : starts[held[-1] + 1]])
        both = lax.dot_general(
            jnp.concatenate(parts, axis=0),
            key,
            (((1,), (1,)), ((), ())),
            preferred_element_type=F32,
        )
        cut = parts[0].shape[0]
        scores[tile, 0], scores[tile, 1] = both[:cut], both[cut:]
    weights = {spot: [] for spot in spans}
    peaks = {}
    for parity in range(2):
        for at, (cap, side) in enumerate(caps):
            held = []
            for tile in range(len(keys)):
                first, last = spans[tile, parity]
                if first <= at < last:
                    base = starts[first]
                    held.append(
                        (
                            tile,
                            scores[tile, parity][starts[at] - base : starts[at + 1] - base]
                            + bias(tile, parity, cap, side),
                        )
                    )
            peak = functools.reduce(jnp.maximum, [score for _, score in held])
            peak = jnp.max(peak, axis=1, keepdims=True)
            peaks[parity, at] = peak
            for tile, score in held:
                weights[tile, parity].append(jnp.exp(score - peak).astype(BF))
    totals = {}
    for tile, value in enumerate(values):
        for parity in range(2):
            side = lane_low(256) if parity == 0 else jnp.logical_not(lane_low(256))
            part = jnp.dot(
                jnp.concatenate(weights[tile, parity], axis=0),
                jnp.where(side, value, jnp.ones_like(value)),
                preferred_element_type=F32,
            )
            base = 0
            for at in range(*spans[tile, parity]):
                count = starts[at + 1] - starts[at]
                rows = part[base : base + count]
                base += count
                spot = (parity, at)
                totals[spot] = totals[spot] + rows if spot in totals else rows
    for parity in range(2):
        head = 2 * pair + parity
        mine = low[:HALF] if parity == 0 else jnp.logical_not(low[:HALF])
        for at, (name, half) in enumerate(groups):
            total = totals[parity, at]
            sums = pltpu.roll(total, 64, 1)
            result = total / sums
            rounded = result.astype(BF)
            rows = slice(half * HALF, (half + 1) * HALF)
            for row, u in enumerate(CLASS_U[name]):
                spot = ((u + head) & 15, rows, slice(None))
                out[spot] = jnp.where(mine, rounded[row * HALF : (row + 1) * HALF, :], out[spot])
            if name == "D":
                log_total = peaks[parity, at][HALF:] + jnp.log(sums[HALF:])
                o0[rows, :] = jnp.where(mine, result[HALF:], o0[rows, :])
                lse0[rows, :] = jnp.where(mine, log_total, lse0[rows, :])


def far_kernel(meta, a0, a1, a2, a3, *rest):
    blocks, outs = rest[:8], rest[8:]
    bound = meta[0]
    device = meta[1]
    xpos, zpos, core = device // 8, device // 2 % NZ, device % 2
    low256 = lane_low(256)
    group = zpos
    lane = lax.broadcasted_iota(jnp.int32, (1, 256), 1)
    part = lane >> 6
    pair = jnp.where(group == 0, 0, jnp.where(group == 1, 4, jnp.where(group == 2, 6, 10)))
    lone = jnp.where(group == 0, 2, jnp.where(group == 1, 3, jnp.where(group == 2, 8, 9)))
    def positions(at, head):
        from_x = xpos ^ (at % 4)
        from_c = core if at < 4 else 1 - core
        from_z = zpos ^ part
        return ((from_x * NZ + from_z) * NC + from_c) * ROWS + (lane & 63) * 16 + head

    results = []
    for heads in ((0, 1), (2,)):
        lanes = slice(0, 128) if heads[0] == 0 else slice(128, 256)
        query = jnp.concatenate([source[:, lanes] for source in (a0, a1, a2, a3)], axis=0)
        query = (query * 0.125).astype(BF)
        sides = [jnp.logical_not(low256) if head else low256 for head in heads]
        queries = [jnp.where(side, query, jnp.zeros_like(query)) for side in sides]
        if heads[0] == 2:
            queries = [query]
        both = jnp.concatenate(queries, axis=0)
        key_lanes = slice(0, 128) if heads[0] == 0 else slice(256, 384)
        value_lanes = slice(128, 256) if heads[0] == 0 else slice(256, 384)
        scores = [
            lax.dot_general(
                both, block[:, key_lanes], (((1,), (1,)), ((), ())), preferred_element_type=F32
            )
            for block in blocks
        ]
        for at, head in enumerate(heads):
            mine = sides[at]
            held = [
                score[at * 256 : (at + 1) * 256]
                + jnp.where(positions(spot, (pair, pair + 1, lone)[head]) < bound, 0.0, MASKED)
                for spot, score in enumerate(scores)
            ]
            peak = jnp.max(functools.reduce(jnp.maximum, held), axis=1, keepdims=True)
            total = None
            for score, block in zip(held, blocks):
                value = block[:, value_lanes]
                weighed = jnp.dot(
                    jnp.exp(score - peak).astype(BF),
                    jnp.where(mine, value, jnp.ones_like(value)),
                    preferred_element_type=F32,
                )
                total = weighed if total is None else total + weighed
            sums = pltpu.roll(total, 64, 1)
            results.append((total / sums, peak + jnp.log(sums if head < 2 else total)))
    low = low256[:64]
    lane = lax.broadcasted_iota(jnp.int32, (64, 128), 1)
    for at, out in enumerate(outs):
        rows = slice(at * 64, (at + 1) * 64)
        out[:, 0:128] = jnp.where(low, results[0][0][rows], results[1][0][rows]).astype(BF)
        mixed = results[2][0][rows].astype(BF)
        for which, place in ((0, 0), (1, 64), (2, 0)):
            rest = results[which][1][rows, place : place + 1]
            for term in range(3):
                kept = rest.astype(BF)
                rest = rest - kept.astype(F32)
                mixed = jnp.where(lane == which * 3 + term, kept, mixed)
        out[:, 128:256] = mixed


def part_of(parts, pair):
    for at, (first, many) in enumerate(parts):
        if first <= pair < first + many:
            return at, slice((pair - first) * 128, (pair - first) * 128 + 128)


def merge_kernel(meta, *refs):
    count = len(NEAR_PARTS)
    close, refs = refs[:count], refs[count:]
    count = len(WIDE_PARTS)
    wide, o0, lse0 = refs[:count], refs[count : 2 * count], refs[2 * count : 3 * count]
    r0, r1, r2, r3, out, stage, grid_rows, ready, sent = refs[3 * count :]
    bound = meta[0]
    device = meta[1]
    zpos = device // 2 % NZ
    for slot, ref in enumerate((r0, r1, r2, r3)):
        stage[slot] = ref[...].astype(F32)
    low = lane_low(GROUPS)

    def log_of(slot, which):
        terms = [stage[slot, :, 128 + which * 3 + term : 129 + which * 3 + term] for term in range(3)]
        return terms[0] + terms[1] + terms[2]

    for pair in range(PAIRS):
        lanes = slice(pair * 128, pair * 128 + 128)
        close_part, close_lanes = part_of(NEAR_PARTS, pair)
        wide_part, wide_lanes = part_of(WIDE_PARTS, pair)
        if pair in PAIR_OF:
            slot = PAIR_OF.index(pair) ^ zpos
            away = stage[slot, :, 0:128]
            away_lse = jnp.where(low, log_of(slot, 0), log_of(slot, 1))
        else:
            left = LONE_OF.index(2 * pair) ^ zpos
            right = (LONE_OF.index(2 * pair) + 1) ^ zpos
            away = jnp.where(low, pltpu.roll(stage[left, :, 128:256], 64, 1), stage[right, :, 128:256])
            away_lse = jnp.where(low, log_of(left, 2), log_of(right, 2))
        here, here_lse = o0[wide_part][:, wide_lanes], lse0[wide_part][:, wide_lanes]
        top = jnp.maximum(here_lse, away_lse)
        weight = jnp.exp(here_lse - top)
        away_weight = jnp.exp(away_lse - top)
        blended = (here * weight + away * away_weight) / (weight + away_weight)
        blended = blended.astype(BF)
        for res in range(RES):
            sides = []
            for head in (2 * pair, 2 * pair + 1):
                rank = level((res - head) % RES)
                if rank == 4:
                    sides.append(blended)
                elif rank == 3:
                    sides.append(wide[wide_part][res, :, wide_lanes])
                else:
                    sides.append(close[close_part][res, :, close_lanes])
            rows = jnp.where(low, *sides)
            for block in range(4):
                grid_rows[block, res * 16 : (res + 1) * 16, lanes] = rows[
                    block * 16 : (block + 1) * 16, :
                ]
    swap = swap_matrix()
    index = lax.broadcasted_iota(jnp.int32, (256, WIDTH), 0)
    copies = []
    for block in range(4):
        rows = jnp.dot(swap, grid_rows[block], preferred_element_type=F32)
        position = device * ROWS + block * 256 + index
        ready[block] = jnp.where(position < bound, rows, 0.0).astype(BF)
        copies.append(
            pltpu.make_async_copy(ready.at[block], out.at[pl.ds(block * 256, 256)], sent.at[block])
        )
        copies[-1].start()
    for copy in copies:
        copy.wait()


def smem():
    return pl.BlockSpec(memory_space=pltpu.SMEM)


def vmem():
    return pl.BlockSpec(memory_space=pltpu.VMEM)


def whole(shape):
    return pl.BlockSpec(shape, lambda i: (0,) * len(shape))


def params(mib):
    return pltpu.CompilerParams(vmem_limit_bytes=mib * 1024 * 1024)


def shape(dims, dtype=BF):
    return jax.ShapeDtypeStruct(dims, dtype)


def by_residue():
    return pl.BlockSpec((RES, GROUPS, 128), lambda i: (0, 0, i))


def by_part(parts):
    return pl.BlockSpec((parts, 2, GROUPS, 128), lambda i: (0, 0, 0, i))


def flat(block):
    return pl.BlockSpec((GROUPS, 128), lambda i: (0, i))


def split(meta, q, k, v):
    rows = [pltpu.with_memory_space_constraint(array, pltpu.HBM) for array in (q, k, v)]
    return pl.pallas_call(
        split_kernel,
        in_specs=[smem()] + [pl.BlockSpec(memory_space=pltpu.HBM)] * 3,
        out_specs=[vmem()] * 9,
        out_shape=[shape((RES, GROUPS, WIDTH))] * 3
        + [shape((4, 2, GROUPS, WIDTH)), shape((2, 2, GROUPS, WIDTH))]
        + [shape((GROUPS, 640))] * 4,
        scratch_shapes=[
            pltpu.VMEM((3, 4, 256, WIDTH), BF),
            pltpu.VMEM((4, GROUPS, 640), BF),
            pltpu.SemaphoreType.DMA((3, 4)),
        ],
        compiler_params=params(28),
        name="split_rows",
    )(meta, *rows)


def local_near(first, many, meta, q, k, v, sel):
    return pl.pallas_call(
        functools.partial(local_kernel, "ABC", first, many),
        in_specs=[smem()] + [vmem()] * 4,
        out_specs=vmem(),
        out_shape=shape((RES, GROUPS, many * 128)),
        compiler_params=params(28),
        cost_estimate=pl.CostEstimate(
            flops=many * 600000000, bytes_accessed=1000000, transcendentals=many * 1200000
        ),
        name="near_queries",
    )(meta, q, k, v, sel)


def local_far(first, many, meta, q, k, v, sel, near, cross):
    return pl.pallas_call(
        functools.partial(local_kernel, "D", first, many),
        in_specs=[smem()] + [vmem()] * 6,
        out_specs=[vmem()] * 3,
        out_shape=[
            shape((RES, GROUPS, many * 128)),
            shape((GROUPS, many * 128), F32),
            shape((GROUPS, many * 128), F32),
        ],
        compiler_params=params(28),
        cost_estimate=pl.CostEstimate(
            flops=many * 200000000, bytes_accessed=1000000, transcendentals=many * 400000
        ),
        name="wide_queries",
    )(meta, q, k, v, sel, near, cross)


def slide_wide(meta, queries, blocks):
    return pl.pallas_call(
        far_kernel,
        in_specs=[smem()] + [vmem()] * 12,
        out_specs=[vmem()] * 4,
        out_shape=[shape((GROUPS, 256))] * 4,
        compiler_params=params(28),
        cost_estimate=pl.CostEstimate(flops=800000000, bytes_accessed=2000000, transcendentals=1600000),
        name="slide_queries",
    )(meta, *queries, *blocks)


def merge(meta, close, wide, back):
    return pl.pallas_call(
        merge_kernel,
        in_specs=[smem()] + [vmem()] * (len(NEAR_PARTS) + 3 * len(WIDE_PARTS) + 4),
        out_specs=pl.BlockSpec(memory_space=pltpu.HBM),
        out_shape=shape((ROWS, WIDTH)),
        scratch_shapes=[
            pltpu.VMEM((4, GROUPS, 256), F32),
            pltpu.VMEM((4, 256, WIDTH), BF),
            pltpu.VMEM((4, 256, WIDTH), BF),
            pltpu.SemaphoreType.DMA((4,)),
        ],
        compiler_params=params(28),
        name="merge_rows",
    )(meta, *close, *[part for parts in zip(*wide) for part in parts], *back)


def at(x, z, c):
    return (x * NZ + z) * NC + c


def move(block, to):
    route = [
        (at(x, z, c), at(*to(x, z, c))) for x in range(NX) for z in range(NZ) for c in range(NC)
    ]
    return lax.ppermute(block, "seq", route)


def along_x(steps):
    return lambda x, z, c: (x ^ steps, z, c)


def along_z(steps):
    return lambda x, z, c: (x, z ^ steps, c)


def relay(x, z, c):
    return (x ^ (3 if c else 1), z, c)


def other_core(x, z, c):
    return (x, z, 1 - c)


def next_chip(x, z, c):
    return (x, z ^ 1, c)


def per_device(query_tiles, key_tiles, value_tiles, slide_length):
    device = lax.axis_index("seq").astype(jnp.int32)
    meta = jnp.stack([slide_length[0], device])
    qt, kt, vt, sel, sel8, z0, z1, z2, z3 = split(meta, query_tiles, key_tiles, value_tiles)
    slabs = [z0] + [move(slab, along_z(step)) for step, slab in ((1, z1), (2, z2), (3, z3))]
    pair = move(sel, other_core)
    local = (qt, kt, vt, pair)
    close = [local_near(*NEAR_PARTS[0], meta, *local)]
    slabs, close[0], sel8, later = lax.optimization_barrier((slabs, close[0], sel8, meta))
    own = jnp.concatenate([slab[:, 256:640] for slab in slabs], axis=0)
    own, later = lax.optimization_barrier((own, later))
    first, third = move(own, along_x(1)), move(own, along_x(3))
    near = move(sel8, next_chip)
    close.append(local_near(*NEAR_PARTS[1], later, *local))
    first, third, close[1], later = lax.optimization_barrier((first, third, close[1], later))
    relayed = move(jnp.where(device % 2 == 0, third, first), relay)
    others = [move(block, other_core) for block in (own, first, third)]
    close.append(local_near(*NEAR_PARTS[2], later, *local))
    relayed, near, close[2], later = lax.optimization_barrier((relayed, near, close[2], later))
    cross = move(near, other_core)
    others.insert(2, move(relayed, other_core))
    blocks = [own, first, relayed, third] + others
    wide = [local_far(*WIDE_PARTS[0], later, *local, near, cross)]
    blocks, wide[0], later = lax.optimization_barrier((blocks, wide[0], later))
    back = slide_wide(meta, slabs, blocks)
    back, later = lax.optimization_barrier((back, later))
    back = [back[0]] + [move(back[step], along_z(step)) for step in (1, 2, 3)]
    wide.append(local_far(*WIDE_PARTS[1], later, *local, near, cross))
    return merge(meta, close, wide, back)


def solution(mesh):
    placed = (
        P(("slide", "seq"), None),
        P(("slide", "seq"), None),
        P(("slide", "seq"), None),
        P("slide"),
    )
    return jax.shard_map(
        per_device, mesh=mesh, in_specs=placed, out_specs=P(("slide", "seq"), None), check_vma=False
    )
```

```python
import functools

import jax
import jax.numpy as jnp
import numpy as np
from jax import lax
from jax.experimental import pallas as pl
from jax.experimental.pallas import tpu as pltpu
from jax.sharding import PartitionSpec as P

HEADS = 12
HEAD_DIM = 64
WIDTH = 768
ROWS = 1024
RES = 16
GROUPS = ROWS // RES
HALF = GROUPS // 2
PAIRS = HEADS // 2
NX, NZ, NC = 4, 4, 2
MASKED = -1e30

BF = jnp.bfloat16
F32 = jnp.float32

ODD = [1, 3, 5, 7, 9, 11, 13, 15]
SHARED = [0, 8, 4, 12]
CLASS_U = {"A": ODD, "B": [2, 6, 10, 14], "C": [4, 12], "D": [8, 0]}
PAIR_OF = [0, 2, 3, 5]
LONE_OF = [2, 3, 8, 9]
NEAR_PARTS = [(0, 2), (2, 4)]
WIDE_PARTS = [(0, 2), (2, 4)]


def level(u):
    return 4 if u == 0 else min((u & -u).bit_length() - 1, 4)


def swap_matrix():
    row = lax.broadcasted_iota(jnp.int32, (256, 256), 0)
    col = lax.broadcasted_iota(jnp.int32, (256, 256), 1)
    return jnp.where(((row & 15) * 16 + (row >> 4)) == col, 1.0, 0.0).astype(BF)


def lane_low(rows):
    return lax.broadcasted_iota(jnp.int32, (rows, 128), 1) < 64


def split_kernel(
    meta, q_in, k_in, v_in, qt, kt, vt, sel, sel8, z0, z1, z2, z3, held, stage, arrived
):
    copies = []
    for at, source in enumerate((k_in, v_in, q_in)):
        copies.append(
            [
                pltpu.make_async_copy(
                    source.at[pl.ds(block * 256, 256)], held.at[at, block], arrived.at[at, block]
                )
                for block in range(4)
            ]
        )
    for copy in copies[0] + copies[1]:
        copy.start()
    swap = swap_matrix()
    for at, target in enumerate((kt, vt, qt)):
        for block in range(4):
            copies[at][block].wait()
            if at == 0:
                copies[2][block].start()
        for block in range(4):
            moved = jnp.dot(swap, held[at, block], preferred_element_type=F32).astype(BF)
            for res in range(RES):
                target[res, block * 16 : (block + 1) * 16, :] = moved[res * 16 : (res + 1) * 16, :]
    zpos = meta[1] // 2 % NZ
    low = lane_low(GROUPS)

    def other(rows):
        return pltpu.roll(rows.astype(F32), 64, 1).astype(BF)

    for pair in range(PAIRS):
        lanes = slice(pair * 128, pair * 128 + 128)

        def picked(ref, u):
            return jnp.where(
                low, ref[(u + 2 * pair) % RES, :, lanes], ref[(u + 2 * pair + 1) % RES, :, lanes]
            )

        for at, u in enumerate(SHARED):
            for kv, ref in enumerate((kt, vt)):
                rows = picked(ref, u)
                sel[at, kv, :, lanes] = rows
                if at < 2:
                    sel8[at, kv, :, lanes] = rows
                if at == 0 and kv == 0:
                    k0 = rows
                if at == 0 and kv == 1:
                    v0 = rows
        q0 = picked(qt, 0)
        for group in range(NZ):
            slot = group ^ zpos
            if pair == PAIR_OF[group]:
                stage[slot, :, 0:128] = q0
                stage[slot, :, 256:384] = k0
                stage[slot, :, 384:512] = v0
            if pair == LONE_OF[group] // 2:
                if LONE_OF[group] % 2 == 0:
                    lone_q, lone_k, lone_v = q0, k0, other(v0)
                else:
                    lone_q, lone_k, lone_v = other(q0), other(k0), v0
                stage[slot, :, 128:256] = jnp.where(low, lone_q, jnp.zeros_like(lone_q))
                stage[slot, :, 512:640] = jnp.where(low, lone_k, lone_v)
    for slot, out in enumerate((z0, z1, z2, z3)):
        out[...] = stage[slot]


def local_kernel(classes, first, many, meta, *refs):
    def body(step, carry):
        lanes = pl.ds(pl.multiple_of((first + step) * 128, 128), 128)
        here = pl.ds(pl.multiple_of(step * 128, 128), 128)
        views = [ref.at[:, :, lanes] for ref in refs[:3]] + [refs[3].at[:, :, :, lanes]]
        if classes == "D":
            views += [ref.at[:, :, :, lanes] for ref in refs[4:6]]
            views += [refs[6].at[:, :, here]]
            views += [ref.at[:, here] for ref in refs[7:9]]
        else:
            views += [refs[4].at[:, :, here]]
        local_pair(classes, first + step, meta, *views)
        return carry

    lax.fori_loop(0, many, body, 0, unroll=True)


def local_pair(classes, pair, meta, q_ref, k_ref, v_ref, sel, *rest):
    far = classes == "D"
    if far:
        near, cross, out, o0, lse0 = rest
    else:
        (out,) = rest
    bound = meta[0]
    device = meta[1]
    lane = lax.broadcasted_iota(jnp.int32, (1, 256), 1)
    groups = [(name, 0) for name in classes] + [(name, 1) for name in classes[::-1]]
    caps = [("ABCD".index(name), side) for name, side in groups]
    starts = [0]
    for name, _ in groups:
        starts.append(starts[-1] + len(CLASS_U[name]) * HALF)
    low = lane_low(starts[-1])

    def rows_of(ref, tile):
        half, odd = tile // 2, tile % 2
        rows = slice(half * HALF, (half + 1) * HALF)
        return jnp.concatenate([ref[2 * at + odd, rows, :] for at in range(8)], axis=0)

    keys = [rows_of(k_ref, tile) for tile in range(4)] + [sel[:, 0].reshape(256, 128)]
    values = [rows_of(v_ref, tile) for tile in range(4)] + [sel[:, 1].reshape(256, 128)]
    if far:
        for kv, rows in enumerate((keys, values)):
            rows.append(
                jnp.concatenate([near[0, kv], near[1, kv], cross[0, kv], cross[1, kv]], axis=0)
            )

    def inside(tile, parity, cap, side):
        if tile >= 4:
            return cap >= tile - 2
        return side == tile // 2 or (tile % 2 == parity and cap >= 1)

    def bias(tile, parity, cap, side):
        head = 2 * pair + parity
        logs = jnp.zeros((1, 256), F32)
        if tile < 4:
            half, odd = tile // 2, tile % 2
            res = 2 * (lane >> 5) + odd
            position = device * ROWS + half * 512 + (lane & 31) * 16 + res
            if odd == parity and cap >= 1:
                u = (res - head) & 15
                extra = 1.0 if side == half else 0.0
                one, two, three = (float(np.log(extra + min(cap, rank))) for rank in (1, 2, 3))
                logs = jnp.where(
                    (u & 2) != 0, one, jnp.where((u & 4) != 0, two, three)
                ) + jnp.zeros((1, 256), F32)
        elif tile == 4:
            u = ((lane >> 6) & 1) * 8 + (lane >> 7) * 4
            position = (device ^ 1) * ROWS + (lane & 63) * 16 + ((u + head) & 15)
            if cap == 3:
                logs = jnp.where(lane < 128, float(np.log(2.0)), 0.0)
        else:
            u = ((lane >> 6) & 1) * 8
            source = jnp.where(lane < 128, device ^ 2, device ^ 3)
            position = source * ROWS + (lane & 63) * 16 + ((u + head) & 15)
        return jnp.where(position < bound, logs, MASKED)

    queries = []
    for parity in range(2):
        head = 2 * pair + parity
        query = jnp.concatenate(
            [
                q_ref[(u + head) & 15, side * HALF : (side + 1) * HALF, :]
                for name, side in groups
                for u in CLASS_U[name]
            ],
            axis=0,
        )
        mine = low if parity == 0 else jnp.logical_not(low)
        queries.append((jnp.where(mine, query, jnp.zeros_like(query)) * 0.125).astype(BF))
    scores, spans = {}, {}
    for tile, key in enumerate(keys):
        parts = []
        for parity in range(2):
            held = [at for at, (cap, side) in enumerate(caps) if inside(tile, parity, cap, side)]
            spans[tile, parity] = (held[0], held[-1] + 1)
            parts.append(queries[parity][starts[held[0]] : starts[held[-1] + 1]])
        both = lax.dot_general(
            jnp.concatenate(parts, axis=0),
            key,
            (((1,), (1,)), ((), ())),
            preferred_element_type=F32,
        )
        cut = parts[0].shape[0]
        scores[tile, 0], scores[tile, 1] = both[:cut], both[cut:]
    weights = {spot: [] for spot in spans}
    peaks = {}
    for parity in range(2):
        for at, (cap, side) in enumerate(caps):
            held = []
            for tile in range(len(keys)):
                first, last = spans[tile, parity]
                if first <= at < last:
                    base = starts[first]
                    held.append(
                        (
                            tile,
                            scores[tile, parity][starts[at] - base : starts[at + 1] - base]
                            + bias(tile, parity, cap, side),
                        )
                    )
            peak = functools.reduce(jnp.maximum, [score for _, score in held])
            peak = jnp.max(peak, axis=1, keepdims=True)
            peaks[parity, at] = peak
            for tile, score in held:
                weights[tile, parity].append(jnp.exp(score - peak).astype(BF))
    totals = {}
    for tile, value in enumerate(values):
        for parity in range(2):
            side = lane_low(256) if parity == 0 else jnp.logical_not(lane_low(256))
            part = jnp.dot(
                jnp.concatenate(weights[tile, parity], axis=0),
                jnp.where(side, value, jnp.ones_like(value)),
                preferred_element_type=F32,
            )
            base = 0
            for at in range(*spans[tile, parity]):
                count = starts[at + 1] - starts[at]
                rows = part[base : base + count]
                base += count
                spot = (parity, at)
                totals[spot] = totals[spot] + rows if spot in totals else rows
    for parity in range(2):
        head = 2 * pair + parity
        mine = low[:HALF] if parity == 0 else jnp.logical_not(low[:HALF])
        for at, (name, half) in enumerate(groups):
            total = totals[parity, at]
            sums = pltpu.roll(total, 64, 1)
            result = total / sums
            rounded = result.astype(BF)
            rows = slice(half * HALF, (half + 1) * HALF)
            for row, u in enumerate(CLASS_U[name]):
                spot = ((u + head) & 15, rows, slice(None))
                out[spot] = jnp.where(mine, rounded[row * HALF : (row + 1) * HALF, :], out[spot])
            if name == "D":
                log_total = peaks[parity, at][HALF:] + jnp.log(sums[HALF:])
                o0[rows, :] = jnp.where(mine, result[HALF:], o0[rows, :])
                lse0[rows, :] = jnp.where(mine, log_total, lse0[rows, :])


def far_kernel(meta, a0, a1, a2, a3, *rest):
    blocks, outs = rest[:8], rest[8:]
    bound = meta[0]
    device = meta[1]
    xpos, zpos, core = device // 8, device // 2 % NZ, device % 2
    low256 = lane_low(256)
    group = zpos
    lane = lax.broadcasted_iota(jnp.int32, (1, 256), 1)
    part = lane >> 6
    pair = jnp.where(group == 0, 0, jnp.where(group == 1, 4, jnp.where(group == 2, 6, 10)))
    lone = jnp.where(group == 0, 2, jnp.where(group == 1, 3, jnp.where(group == 2, 8, 9)))
    def positions(at, head):
        from_x = xpos ^ (at % 4)
        from_c = core if at < 4 else 1 - core
        from_z = zpos ^ part
        return ((from_x * NZ + from_z) * NC + from_c) * ROWS + (lane & 63) * 16 + head

    results = []
    for heads in ((0, 1), (2,)):
        lanes = slice(0, 128) if heads[0] == 0 else slice(128, 256)
        query = jnp.concatenate([source[:, lanes] for source in (a0, a1, a2, a3)], axis=0)
        query = (query * 0.125).astype(BF)
        sides = [jnp.logical_not(low256) if head else low256 for head in heads]
        queries = [jnp.where(side, query, jnp.zeros_like(query)) for side in sides]
        if heads[0] == 2:
            queries = [query]
        both = jnp.concatenate(queries, axis=0)
        key_lanes = slice(0, 128) if heads[0] == 0 else slice(256, 384)
        value_lanes = slice(128, 256) if heads[0] == 0 else slice(256, 384)
        scores = [
            lax.dot_general(
                both, block[:, key_lanes], (((1,), (1,)), ((), ())), preferred_element_type=F32
            )
            for block in blocks
        ]
        for at, head in enumerate(heads):
            mine = sides[at]
            held = [
                score[at * 256 : (at + 1) * 256]
                + jnp.where(positions(spot, (pair, pair + 1, lone)[head]) < bound, 0.0, MASKED)
                for spot, score in enumerate(scores)
            ]
            peak = jnp.max(functools.reduce(jnp.maximum, held), axis=1, keepdims=True)
            total = None
            for score, block in zip(held, blocks):
                value = block[:, value_lanes]
                weighed = jnp.dot(
                    jnp.exp(score - peak).astype(BF),
                    jnp.where(mine, value, jnp.ones_like(value)),
                    preferred_element_type=F32,
                )
                total = weighed if total is None else total + weighed
            sums = pltpu.roll(total, 64, 1)
            results.append((total / sums, peak + jnp.log(sums if head < 2 else total)))
    low = low256[:64]
    lane = lax.broadcasted_iota(jnp.int32, (64, 128), 1)
    for at, out in enumerate(outs):
        rows = slice(at * 64, (at + 1) * 64)
        out[:, 0:128] = jnp.where(low, results[0][0][rows], results[1][0][rows]).astype(BF)
        mixed = results[2][0][rows].astype(BF)
        for which, place in ((0, 0), (1, 64), (2, 0)):
            rest = results[which][1][rows, place : place + 1]
            for term in range(3):
                kept = rest.astype(BF)
                rest = rest - kept.astype(F32)
                mixed = jnp.where(lane == which * 3 + term, kept, mixed)
        out[:, 128:256] = mixed


def part_of(parts, pair):
    for at, (first, many) in enumerate(parts):
        if first <= pair < first + many:
            return at, slice((pair - first) * 128, (pair - first) * 128 + 128)


def merge_kernel(meta, *refs):
    count = len(NEAR_PARTS)
    close, refs = refs[:count], refs[count:]
    count = len(WIDE_PARTS)
    wide, o0, lse0 = refs[:count], refs[count : 2 * count], refs[2 * count : 3 * count]
    r0, r1, r2, r3, out, stage, grid_rows, ready, sent = refs[3 * count :]
    bound = meta[0]
    device = meta[1]
    zpos = device // 2 % NZ
    for slot, ref in enumerate((r0, r1, r2, r3)):
        stage[slot] = ref[...].astype(F32)
    low = lane_low(GROUPS)

    def log_of(slot, which):
        terms = [stage[slot, :, 128 + which * 3 + term : 129 + which * 3 + term] for term in range(3)]
        return terms[0] + terms[1] + terms[2]

    for pair in range(PAIRS):
        lanes = slice(pair * 128, pair * 128 + 128)
        close_part, close_lanes = part_of(NEAR_PARTS, pair)
        wide_part, wide_lanes = part_of(WIDE_PARTS, pair)
        if pair in PAIR_OF:
            slot = PAIR_OF.index(pair) ^ zpos
            away = stage[slot, :, 0:128]
            away_lse = jnp.where(low, log_of(slot, 0), log_of(slot, 1))
        else:
            left = LONE_OF.index(2 * pair) ^ zpos
            right = (LONE_OF.index(2 * pair) + 1) ^ zpos
            away = jnp.where(low, pltpu.roll(stage[left, :, 128:256], 64, 1), stage[right, :, 128:256])
            away_lse = jnp.where(low, log_of(left, 2), log_of(right, 2))
        here, here_lse = o0[wide_part][:, wide_lanes], lse0[wide_part][:, wide_lanes]
        top = jnp.maximum(here_lse, away_lse)
        weight = jnp.exp(here_lse - top)
        away_weight = jnp.exp(away_lse - top)
        blended = (here * weight + away * away_weight) / (weight + away_weight)
        blended = blended.astype(BF)
        for res in range(RES):
            sides = []
            for head in (2 * pair, 2 * pair + 1):
                rank = level((res - head) % RES)
                if rank == 4:
                    sides.append(blended)
                elif rank == 3:
                    sides.append(wide[wide_part][res, :, wide_lanes])
                else:
                    sides.append(close[close_part][res, :, close_lanes])
            rows = jnp.where(low, *sides)
            for block in range(4):
                grid_rows[block, res * 16 : (res + 1) * 16, lanes] = rows[
                    block * 16 : (block + 1) * 16, :
                ]
    swap = swap_matrix()
    index = lax.broadcasted_iota(jnp.int32, (256, WIDTH), 0)
    copies = []
    for block in range(4):
        rows = jnp.dot(swap, grid_rows[block], preferred_element_type=F32)
        position = device * ROWS + block * 256 + index
        ready[block] = jnp.where(position < bound, rows, 0.0).astype(BF)
        copies.append(
            pltpu.make_async_copy(ready.at[block], out.at[pl.ds(block * 256, 256)], sent.at[block])
        )
        copies[-1].start()
    for copy in copies:
        copy.wait()


def smem():
    return pl.BlockSpec(memory_space=pltpu.SMEM)


def vmem():
    return pl.BlockSpec(memory_space=pltpu.VMEM)


def whole(shape):
    return pl.BlockSpec(shape, lambda i: (0,) * len(shape))


def params(mib):
    return pltpu.CompilerParams(vmem_limit_bytes=mib * 1024 * 1024)


def shape(dims, dtype=BF):
    return jax.ShapeDtypeStruct(dims, dtype)


def by_residue():
    return pl.BlockSpec((RES, GROUPS, 128), lambda i: (0, 0, i))


def by_part(parts):
    return pl.BlockSpec((parts, 2, GROUPS, 128), lambda i: (0, 0, 0, i))


def flat(block):
    return pl.BlockSpec((GROUPS, 128), lambda i: (0, i))


def split(meta, q, k, v):
    rows = [pltpu.with_memory_space_constraint(array, pltpu.HBM) for array in (q, k, v)]
    return pl.pallas_call(
        split_kernel,
        in_specs=[smem()] + [pl.BlockSpec(memory_space=pltpu.HBM)] * 3,
        out_specs=[vmem()] * 9,
        out_shape=[shape((RES, GROUPS, WIDTH))] * 3
        + [shape((4, 2, GROUPS, WIDTH)), shape((2, 2, GROUPS, WIDTH))]
        + [shape((GROUPS, 640))] * 4,
        scratch_shapes=[
            pltpu.VMEM((3, 4, 256, WIDTH), BF),
            pltpu.VMEM((4, GROUPS, 640), BF),
            pltpu.SemaphoreType.DMA((3, 4)),
        ],
        compiler_params=params(40),
        name="split_rows",
    )(meta, *rows)


def local_near(first, many, meta, q, k, v, sel):
    return pl.pallas_call(
        functools.partial(local_kernel, "ABC", first, many),
        in_specs=[smem()] + [vmem()] * 4,
        out_specs=vmem(),
        out_shape=shape((RES, GROUPS, many * 128)),
        compiler_params=params(40),
        cost_estimate=pl.CostEstimate(
            flops=many * 600000000, bytes_accessed=1000000, transcendentals=many * 1200000
        ),
        name="near_queries",
    )(meta, q, k, v, sel)


def local_far(first, many, meta, q, k, v, sel, near, cross):
    return pl.pallas_call(
        functools.partial(local_kernel, "D", first, many),
        in_specs=[smem()] + [vmem()] * 6,
        out_specs=[vmem()] * 3,
        out_shape=[
            shape((RES, GROUPS, many * 128)),
            shape((GROUPS, many * 128), F32),
            shape((GROUPS, many * 128), F32),
        ],
        compiler_params=params(40),
        cost_estimate=pl.CostEstimate(
            flops=many * 200000000, bytes_accessed=1000000, transcendentals=many * 400000
        ),
        name="wide_queries",
    )(meta, q, k, v, sel, near, cross)


def slide_wide(meta, queries, blocks):
    return pl.pallas_call(
        far_kernel,
        in_specs=[smem()] + [vmem()] * 12,
        out_specs=[vmem()] * 4,
        out_shape=[shape((GROUPS, 256))] * 4,
        compiler_params=params(40),
        cost_estimate=pl.CostEstimate(flops=800000000, bytes_accessed=2000000, transcendentals=1600000),
        name="slide_queries",
    )(meta, *queries, *blocks)


def merge(meta, close, wide, back):
    return pl.pallas_call(
        merge_kernel,
        in_specs=[smem()] + [vmem()] * (len(NEAR_PARTS) + 3 * len(WIDE_PARTS) + 4),
        out_specs=pl.BlockSpec(memory_space=pltpu.HBM),
        out_shape=shape((ROWS, WIDTH)),
        scratch_shapes=[
            pltpu.VMEM((4, GROUPS, 256), F32),
            pltpu.VMEM((4, 256, WIDTH), BF),
            pltpu.VMEM((4, 256, WIDTH), BF),
            pltpu.SemaphoreType.DMA((4,)),
        ],
        compiler_params=params(40),
        name="merge_rows",
    )(meta, *close, *[part for parts in zip(*wide) for part in parts], *back)


def at(x, z, c):
    return (x * NZ + z) * NC + c


def move(block, to):
    route = [
        (at(x, z, c), at(*to(x, z, c))) for x in range(NX) for z in range(NZ) for c in range(NC)
    ]
    return lax.ppermute(block, "seq", route)


def along_x(steps):
    return lambda x, z, c: (x ^ steps, z, c)


def along_z(steps):
    return lambda x, z, c: (x, z ^ steps, c)


def other_core(x, z, c):
    return (x, z, 1 - c)


def next_chip(x, z, c):
    return (x, z ^ 1, c)


def per_device(query_tiles, key_tiles, value_tiles, slide_length):
    device = lax.axis_index("seq").astype(jnp.int32)
    meta = jnp.stack([slide_length[0], device])
    qt, kt, vt, sel, sel8, z0, z1, z2, z3 = split(meta, query_tiles, key_tiles, value_tiles)
    slabs = [z0] + [move(slab, along_z(step)) for step, slab in ((1, z1), (2, z2), (3, z3))]
    pair = move(sel, other_core)
    local = (qt, kt, vt, pair)
    close = [local_near(*NEAR_PARTS[0], meta, *local)]
    slabs, close[0], sel8, later = lax.optimization_barrier((slabs, close[0], sel8, meta))
    own = jnp.concatenate([slab[:, 256:640] for slab in slabs], axis=0)
    own, later = lax.optimization_barrier((own, later))
    moved = [move(own, along_x(step)) for step in (1, 2, 3)]
    near = move(sel8, next_chip)
    close.append(local_near(*NEAR_PARTS[1], later, *local))
    moved, near, close[1], later = lax.optimization_barrier((moved, near, close[1], later))
    cross = move(near, other_core)
    blocks = [own] + moved
    blocks += [move(block, other_core) for block in blocks]
    wide = [local_far(*WIDE_PARTS[0], later, *local, near, cross)]
    blocks, wide[0], later = lax.optimization_barrier((blocks, wide[0], later))
    back = slide_wide(meta, slabs, blocks)
    back, later = lax.optimization_barrier((back, later))
    back = [back[0]] + [move(back[step], along_z(step)) for step in (1, 2, 3)]
    wide.append(local_far(*WIDE_PARTS[1], later, *local, near, cross))
    return merge(meta, close, wide, back)


def solution(mesh):
    placed = (
        P(("slide", "seq"), None),
        P(("slide", "seq"), None),
        P(("slide", "seq"), None),
        P("slide"),
    )
    return jax.shard_map(
        per_device, mesh=mesh, in_specs=placed, out_specs=P(("slide", "seq"), None), check_vma=False
    )
```

```python
import functools

import jax
import jax.numpy as jnp
import numpy as np
from jax import lax
from jax.experimental import pallas as pl
from jax.experimental.pallas import tpu as pltpu
from jax.sharding import PartitionSpec as P

HEADS = 12
HEAD_DIM = 64
WIDTH = 768
ROWS = 1024
RES = 16
GROUPS = ROWS // RES
HALF = GROUPS // 2
PAIRS = HEADS // 2
NX, NZ, NC = 4, 4, 2
MASKED = -1e30

BF = jnp.bfloat16
F32 = jnp.float32

ODD = [1, 3, 5, 7, 9, 11, 13, 15]
SHARED = [0, 8, 4, 12]
CLASS_U = {"A": ODD, "B": [2, 6, 10, 14], "C": [4, 12], "D": [8, 0]}
PAIR_OF = [0, 2, 3, 5]
LONE_OF = [2, 3, 8, 9]
NEAR_PARTS = [(0, 2), (2, 4)]
WIDE_PARTS = [(0, 2), (2, 4)]


def level(u):
    return 4 if u == 0 else min((u & -u).bit_length() - 1, 4)


def swap_matrix():
    row = lax.broadcasted_iota(jnp.int32, (256, 256), 0)
    col = lax.broadcasted_iota(jnp.int32, (256, 256), 1)
    return jnp.where(((row & 15) * 16 + (row >> 4)) == col, 1.0, 0.0).astype(BF)


def lane_low(rows):
    return lax.broadcasted_iota(jnp.int32, (rows, 128), 1) < 64


def split_kernel(
    meta, q_in, k_in, v_in, qt, kt, vt, sel, sel8, z0, z1, z2, z3, held, stage, arrived
):
    copies = []
    for at, source in enumerate((k_in, v_in, q_in)):
        copies.append(
            [
                pltpu.make_async_copy(
                    source.at[pl.ds(block * 256, 256)], held.at[at, block], arrived.at[at, block]
                )
                for block in range(4)
            ]
        )
    for copy in copies[0] + copies[1]:
        copy.start()
    swap = swap_matrix()
    for at, target in enumerate((kt, vt, qt)):
        for block in range(4):
            copies[at][block].wait()
            if at == 0:
                copies[2][block].start()
        for block in range(4):
            moved = jnp.dot(swap, held[at, block], preferred_element_type=F32).astype(BF)
            for res in range(RES):
                target[res, block * 16 : (block + 1) * 16, :] = moved[res * 16 : (res + 1) * 16, :]
    zpos = meta[1] // 2 % NZ
    low = lane_low(GROUPS)

    def other(rows):
        return pltpu.roll(rows.astype(F32), 64, 1).astype(BF)

    for pair in range(PAIRS):
        lanes = slice(pair * 128, pair * 128 + 128)

        def picked(ref, u):
            return jnp.where(
                low, ref[(u + 2 * pair) % RES, :, lanes], ref[(u + 2 * pair + 1) % RES, :, lanes]
            )

        for at, u in enumerate(SHARED):
            for kv, ref in enumerate((kt, vt)):
                rows = picked(ref, u)
                sel[at, kv, :, lanes] = rows
                if at < 2:
                    sel8[at, kv, :, lanes] = rows
                if at == 0 and kv == 0:
                    k0 = rows
                if at == 0 and kv == 1:
                    v0 = rows
        q0 = picked(qt, 0)
        for group in range(NZ):
            slot = group ^ zpos
            if pair == PAIR_OF[group]:
                stage[slot, :, 0:128] = q0
                stage[slot, :, 256:384] = k0
                stage[slot, :, 384:512] = v0
            if pair == LONE_OF[group] // 2:
                if LONE_OF[group] % 2 == 0:
                    lone_q, lone_k, lone_v = q0, k0, other(v0)
                else:
                    lone_q, lone_k, lone_v = other(q0), other(k0), v0
                stage[slot, :, 128:256] = jnp.where(low, lone_q, jnp.zeros_like(lone_q))
                stage[slot, :, 512:640] = jnp.where(low, lone_k, lone_v)
    for slot, out in enumerate((z0, z1, z2, z3)):
        out[...] = stage[slot]


def local_kernel(classes, first, many, meta, *refs):
    def body(step, carry):
        lanes = pl.ds(pl.multiple_of((first + step) * 128, 128), 128)
        here = pl.ds(pl.multiple_of(step * 128, 128), 128)
        views = [ref.at[:, :, lanes] for ref in refs[:3]] + [refs[3].at[:, :, :, lanes]]
        if classes == "D":
            views += [ref.at[:, :, :, lanes] for ref in refs[4:6]]
            views += [refs[6].at[:, :, here]]
            views += [ref.at[:, here] for ref in refs[7:9]]
        else:
            views += [refs[4].at[:, :, here]]
        local_pair(classes, first + step, meta, *views)
        return carry

    lax.fori_loop(0, many, body, 0, unroll=True)


def local_pair(classes, pair, meta, q_ref, k_ref, v_ref, sel, *rest):
    far = classes == "D"
    if far:
        near, cross, out, o0, lse0 = rest
    else:
        (out,) = rest
    bound = meta[0]
    device = meta[1]
    lane = lax.broadcasted_iota(jnp.int32, (1, 256), 1)
    groups = [(name, 0) for name in classes] + [(name, 1) for name in classes[::-1]]
    caps = [("ABCD".index(name), side) for name, side in groups]
    starts = [0]
    for name, _ in groups:
        starts.append(starts[-1] + len(CLASS_U[name]) * HALF)
    low = lane_low(starts[-1])

    def rows_of(ref, tile):
        half, odd = tile // 2, tile % 2
        rows = slice(half * HALF, (half + 1) * HALF)
        return jnp.concatenate([ref[2 * at + odd, rows, :] for at in range(8)], axis=0)

    keys = [rows_of(k_ref, tile) for tile in range(4)] + [sel[:, 0].reshape(256, 128)]
    values = [rows_of(v_ref, tile) for tile in range(4)] + [sel[:, 1].reshape(256, 128)]
    if far:
        for kv, rows in enumerate((keys, values)):
            rows.append(
                jnp.concatenate([near[0, kv], near[1, kv], cross[0, kv], cross[1, kv]], axis=0)
            )

    def inside(tile, parity, cap, side):
        if tile >= 4:
            return cap >= tile - 2
        return side == tile // 2 or (tile % 2 == parity and cap >= 1)

    def bias(tile, parity, cap, side):
        head = 2 * pair + parity
        logs = jnp.zeros((1, 256), F32)
        if tile < 4:
            half, odd = tile // 2, tile % 2
            res = 2 * (lane >> 5) + odd
            position = device * ROWS + half * 512 + (lane & 31) * 16 + res
            if odd == parity and cap >= 1:
                u = (res - head) & 15
                extra = 1.0 if side == half else 0.0
                one, two, three = (float(np.log(extra + min(cap, rank))) for rank in (1, 2, 3))
                logs = jnp.where(
                    (u & 2) != 0, one, jnp.where((u & 4) != 0, two, three)
                ) + jnp.zeros((1, 256), F32)
        elif tile == 4:
            u = ((lane >> 6) & 1) * 8 + (lane >> 7) * 4
            position = (device ^ 1) * ROWS + (lane & 63) * 16 + ((u + head) & 15)
            if cap == 3:
                logs = jnp.where(lane < 128, float(np.log(2.0)), 0.0)
        else:
            u = ((lane >> 6) & 1) * 8
            source = jnp.where(lane < 128, device ^ 2, device ^ 3)
            position = source * ROWS + (lane & 63) * 16 + ((u + head) & 15)
        return jnp.where(position < bound, logs, MASKED)

    queries = []
    for parity in range(2):
        head = 2 * pair + parity
        query = jnp.concatenate(
            [
                q_ref[(u + head) & 15, side * HALF : (side + 1) * HALF, :]
                for name, side in groups
                for u in CLASS_U[name]
            ],
            axis=0,
        )
        mine = low if parity == 0 else jnp.logical_not(low)
        queries.append((jnp.where(mine, query, jnp.zeros_like(query)) * 0.125).astype(BF))
    scores, spans = {}, {}
    for tile, key in enumerate(keys):
        parts = []
        for parity in range(2):
            held = [at for at, (cap, side) in enumerate(caps) if inside(tile, parity, cap, side)]
            spans[tile, parity] = (held[0], held[-1] + 1)
            parts.append(queries[parity][starts[held[0]] : starts[held[-1] + 1]])
        both = lax.dot_general(
            jnp.concatenate(parts, axis=0),
            key,
            (((1,), (1,)), ((), ())),
            preferred_element_type=F32,
        )
        cut = parts[0].shape[0]
        scores[tile, 0], scores[tile, 1] = both[:cut], both[cut:]
    weights = {spot: [] for spot in spans}
    peaks = {}
    for parity in range(2):
        for at, (cap, side) in enumerate(caps):
            held = []
            for tile in range(len(keys)):
                first, last = spans[tile, parity]
                if first <= at < last:
                    base = starts[first]
                    held.append(
                        (
                            tile,
                            scores[tile, parity][starts[at] - base : starts[at + 1] - base]
                            + bias(tile, parity, cap, side),
                        )
                    )
            peak = functools.reduce(jnp.maximum, [score for _, score in held])
            peak = jnp.max(peak, axis=1, keepdims=True)
            peaks[parity, at] = peak
            for tile, score in held:
                weights[tile, parity].append(jnp.exp(score - peak).astype(BF))
    totals = {}
    for tile, value in enumerate(values):
        for parity in range(2):
            side = lane_low(256) if parity == 0 else jnp.logical_not(lane_low(256))
            part = jnp.dot(
                jnp.concatenate(weights[tile, parity], axis=0),
                jnp.where(side, value, jnp.ones_like(value)),
                preferred_element_type=F32,
            )
            base = 0
            for at in range(*spans[tile, parity]):
                count = starts[at + 1] - starts[at]
                rows = part[base : base + count]
                base += count
                spot = (parity, at)
                totals[spot] = totals[spot] + rows if spot in totals else rows
    for parity in range(2):
        head = 2 * pair + parity
        mine = low[:HALF] if parity == 0 else jnp.logical_not(low[:HALF])
        for at, (name, half) in enumerate(groups):
            total = totals[parity, at]
            sums = pltpu.roll(total, 64, 1)
            result = total / sums
            rounded = result.astype(BF)
            rows = slice(half * HALF, (half + 1) * HALF)
            for row, u in enumerate(CLASS_U[name]):
                spot = ((u + head) & 15, rows, slice(None))
                out[spot] = jnp.where(mine, rounded[row * HALF : (row + 1) * HALF, :], out[spot])
            if name == "D":
                log_total = peaks[parity, at][HALF:] + jnp.log(sums[HALF:])
                o0[rows, :] = jnp.where(mine, result[HALF:], o0[rows, :])
                lse0[rows, :] = jnp.where(mine, log_total, lse0[rows, :])


def far_kernel(meta, a0, a1, a2, a3, *rest):
    blocks, outs = rest[:8], rest[8:]
    bound = meta[0]
    device = meta[1]
    xpos, zpos, core = device // 8, device // 2 % NZ, device % 2
    low256 = lane_low(256)
    group = zpos
    lane = lax.broadcasted_iota(jnp.int32, (1, 256), 1)
    part = lane >> 6
    pair = jnp.where(group == 0, 0, jnp.where(group == 1, 4, jnp.where(group == 2, 6, 10)))
    lone = jnp.where(group == 0, 2, jnp.where(group == 1, 3, jnp.where(group == 2, 8, 9)))
    def positions(at, head):
        from_x = xpos ^ (at % 4)
        from_c = core if at < 4 else 1 - core
        from_z = zpos ^ part
        return ((from_x * NZ + from_z) * NC + from_c) * ROWS + (lane & 63) * 16 + head

    results = []
    for heads in ((0, 1), (2,)):
        lanes = slice(0, 128) if heads[0] == 0 else slice(128, 256)
        query = jnp.concatenate([source[:, lanes] for source in (a0, a1, a2, a3)], axis=0)
        query = (query * 0.125).astype(BF)
        sides = [jnp.logical_not(low256) if head else low256 for head in heads]
        queries = [jnp.where(side, query, jnp.zeros_like(query)) for side in sides]
        if heads[0] == 2:
            queries = [query]
        both = jnp.concatenate(queries, axis=0)
        key_lanes = slice(0, 128) if heads[0] == 0 else slice(256, 384)
        value_lanes = slice(128, 256) if heads[0] == 0 else slice(256, 384)
        scores = [
            lax.dot_general(
                both, block[:, key_lanes], (((1,), (1,)), ((), ())), preferred_element_type=F32
            )
            for block in blocks
        ]
        for at, head in enumerate(heads):
            mine = sides[at]
            held = [
                score[at * 256 : (at + 1) * 256]
                + jnp.where(positions(spot, (pair, pair + 1, lone)[head]) < bound, 0.0, MASKED)
                for spot, score in enumerate(scores)
            ]
            peak = jnp.max(functools.reduce(jnp.maximum, held), axis=1, keepdims=True)
            total = None
            for score, block in zip(held, blocks):
                value = block[:, value_lanes]
                weighed = jnp.dot(
                    jnp.exp(score - peak).astype(BF),
                    jnp.where(mine, value, jnp.ones_like(value)),
                    preferred_element_type=F32,
                )
                total = weighed if total is None else total + weighed
            sums = pltpu.roll(total, 64, 1)
            results.append((total / sums, peak + jnp.log(sums if head < 2 else total)))
    low = low256[:64]
    lane = lax.broadcasted_iota(jnp.int32, (64, 128), 1)
    for at, out in enumerate(outs):
        rows = slice(at * 64, (at + 1) * 64)
        out[:, 0:128] = jnp.where(low, results[0][0][rows], results[1][0][rows]).astype(BF)
        mixed = results[2][0][rows].astype(BF)
        for which, place in ((0, 0), (1, 64), (2, 0)):
            rest = results[which][1][rows, place : place + 1]
            for term in range(3):
                kept = rest.astype(BF)
                rest = rest - kept.astype(F32)
                mixed = jnp.where(lane == which * 3 + term, kept, mixed)
        out[:, 128:256] = mixed


def part_of(parts, pair):
    for at, (first, many) in enumerate(parts):
        if first <= pair < first + many:
            return at, slice((pair - first) * 128, (pair - first) * 128 + 128)


def merge_kernel(meta, *refs):
    count = len(NEAR_PARTS)
    close, refs = refs[:count], refs[count:]
    count = len(WIDE_PARTS)
    wide, o0, lse0 = refs[:count], refs[count : 2 * count], refs[2 * count : 3 * count]
    r0, r1, r2, r3, out, stage, grid_rows, ready, sent = refs[3 * count :]
    bound = meta[0]
    device = meta[1]
    zpos = device // 2 % NZ
    for slot, ref in enumerate((r0, r1, r2, r3)):
        stage[slot] = ref[...].astype(F32)
    low = lane_low(GROUPS)

    def log_of(slot, which):
        terms = [stage[slot, :, 128 + which * 3 + term : 129 + which * 3 + term] for term in range(3)]
        return terms[0] + terms[1] + terms[2]

    for pair in range(PAIRS):
        lanes = slice(pair * 128, pair * 128 + 128)
        close_part, close_lanes = part_of(NEAR_PARTS, pair)
        wide_part, wide_lanes = part_of(WIDE_PARTS, pair)
        if pair in PAIR_OF:
            slot = PAIR_OF.index(pair) ^ zpos
            away = stage[slot, :, 0:128]
            away_lse = jnp.where(low, log_of(slot, 0), log_of(slot, 1))
        else:
            left = LONE_OF.index(2 * pair) ^ zpos
            right = (LONE_OF.index(2 * pair) + 1) ^ zpos
            away = jnp.where(low, pltpu.roll(stage[left, :, 128:256], 64, 1), stage[right, :, 128:256])
            away_lse = jnp.where(low, log_of(left, 2), log_of(right, 2))
        here, here_lse = o0[wide_part][:, wide_lanes], lse0[wide_part][:, wide_lanes]
        top = jnp.maximum(here_lse, away_lse)
        weight = jnp.exp(here_lse - top)
        away_weight = jnp.exp(away_lse - top)
        blended = (here * weight + away * away_weight) / (weight + away_weight)
        blended = blended.astype(BF)
        for res in range(RES):
            sides = []
            for head in (2 * pair, 2 * pair + 1):
                rank = level((res - head) % RES)
                if rank == 4:
                    sides.append(blended)
                elif rank == 3:
                    sides.append(wide[wide_part][res, :, wide_lanes])
                else:
                    sides.append(close[close_part][res, :, close_lanes])
            rows = jnp.where(low, *sides)
            for block in range(4):
                grid_rows[block, res * 16 : (res + 1) * 16, lanes] = rows[
                    block * 16 : (block + 1) * 16, :
                ]
    swap = swap_matrix()
    index = lax.broadcasted_iota(jnp.int32, (256, WIDTH), 0)
    copies = []
    for block in range(4):
        rows = jnp.dot(swap, grid_rows[block], preferred_element_type=F32)
        position = device * ROWS + block * 256 + index
        ready[block] = jnp.where(position < bound, rows, 0.0).astype(BF)
        copies.append(
            pltpu.make_async_copy(ready.at[block], out.at[pl.ds(block * 256, 256)], sent.at[block])
        )
        copies[-1].start()
    for copy in copies:
        copy.wait()


def smem():
    return pl.BlockSpec(memory_space=pltpu.SMEM)


def vmem():
    return pl.BlockSpec(memory_space=pltpu.VMEM)


def whole(shape):
    return pl.BlockSpec(shape, lambda i: (0,) * len(shape))


def params(mib):
    return pltpu.CompilerParams(vmem_limit_bytes=mib * 1024 * 1024)


def shape(dims, dtype=BF):
    return jax.ShapeDtypeStruct(dims, dtype)


def by_residue():
    return pl.BlockSpec((RES, GROUPS, 128), lambda i: (0, 0, i))


def by_part(parts):
    return pl.BlockSpec((parts, 2, GROUPS, 128), lambda i: (0, 0, 0, i))


def flat(block):
    return pl.BlockSpec((GROUPS, 128), lambda i: (0, i))


def split(meta, q, k, v):
    rows = [pltpu.with_memory_space_constraint(array, pltpu.HBM) for array in (q, k, v)]
    return pl.pallas_call(
        split_kernel,
        in_specs=[smem()] + [pl.BlockSpec(memory_space=pltpu.HBM)] * 3,
        out_specs=[vmem()] * 9,
        out_shape=[shape((RES, GROUPS, WIDTH))] * 3
        + [shape((4, 2, GROUPS, WIDTH)), shape((2, 2, GROUPS, WIDTH))]
        + [shape((GROUPS, 640))] * 4,
        scratch_shapes=[
            pltpu.VMEM((3, 4, 256, WIDTH), BF),
            pltpu.VMEM((4, GROUPS, 640), BF),
            pltpu.SemaphoreType.DMA((3, 4)),
        ],
        compiler_params=params(40),
        name="split_rows",
    )(meta, *rows)


def local_near(first, many, meta, q, k, v, sel):
    return pl.pallas_call(
        functools.partial(local_kernel, "ABC", first, many),
        in_specs=[smem()] + [vmem()] * 4,
        out_specs=vmem(),
        out_shape=shape((RES, GROUPS, many * 128)),
        compiler_params=params(40),
        cost_estimate=pl.CostEstimate(
            flops=many * 600000000, bytes_accessed=1000000, transcendentals=many * 1200000
        ),
        name="near_queries",
    )(meta, q, k, v, sel)


def local_far(first, many, meta, q, k, v, sel, near, cross):
    return pl.pallas_call(
        functools.partial(local_kernel, "D", first, many),
        in_specs=[smem()] + [vmem()] * 6,
        out_specs=[vmem()] * 3,
        out_shape=[
            shape((RES, GROUPS, many * 128)),
            shape((GROUPS, many * 128), F32),
            shape((GROUPS, many * 128), F32),
        ],
        compiler_params=params(40),
        cost_estimate=pl.CostEstimate(
            flops=many * 200000000, bytes_accessed=1000000, transcendentals=many * 400000
        ),
        name="wide_queries",
    )(meta, q, k, v, sel, near, cross)


def slide_wide(meta, queries, blocks):
    return pl.pallas_call(
        far_kernel,
        in_specs=[smem()] + [vmem()] * 12,
        out_specs=[vmem()] * 4,
        out_shape=[shape((GROUPS, 256))] * 4,
        compiler_params=params(40),
        cost_estimate=pl.CostEstimate(flops=800000000, bytes_accessed=2000000, transcendentals=1600000),
        name="slide_queries",
    )(meta, *queries, *blocks)


def merge(meta, close, wide, back):
    return pl.pallas_call(
        merge_kernel,
        in_specs=[smem()] + [vmem()] * (len(NEAR_PARTS) + 3 * len(WIDE_PARTS) + 4),
        out_specs=pl.BlockSpec(memory_space=pltpu.HBM),
        out_shape=shape((ROWS, WIDTH)),
        scratch_shapes=[
            pltpu.VMEM((4, GROUPS, 256), F32),
            pltpu.VMEM((4, 256, WIDTH), BF),
            pltpu.VMEM((4, 256, WIDTH), BF),
            pltpu.SemaphoreType.DMA((4,)),
        ],
        compiler_params=params(40),
        name="merge_rows",
    )(meta, *close, *[part for parts in zip(*wide) for part in parts], *back)


def at(x, z, c):
    return (x * NZ + z) * NC + c


def move(block, to):
    route = [
        (at(x, z, c), at(*to(x, z, c))) for x in range(NX) for z in range(NZ) for c in range(NC)
    ]
    return lax.ppermute(block, "seq", route)


def along_x(steps):
    return lambda x, z, c: (x ^ steps, z, c)


def along_z(steps):
    return lambda x, z, c: (x, z ^ steps, c)


def other_core(x, z, c):
    return (x, z, 1 - c)


def next_chip(x, z, c):
    return (x, z ^ 1, c)


def per_device(query_tiles, key_tiles, value_tiles, slide_length):
    device = lax.axis_index("seq").astype(jnp.int32)
    meta = jnp.stack([slide_length[0], device])
    qt, kt, vt, sel, sel8, z0, z1, z2, z3 = split(meta, query_tiles, key_tiles, value_tiles)
    slabs = [z0] + [move(slab, along_z(step)) for step, slab in ((1, z1), (2, z2), (3, z3))]
    pair = move(sel, other_core)
    near = move(sel8, next_chip)
    local = (qt, kt, vt, pair)
    close = [local_near(*NEAR_PARTS[0], meta, *local)]
    slabs, close[0], later = lax.optimization_barrier((slabs, close[0], meta))
    own = jnp.concatenate([slab[:, 256:640] for slab in slabs], axis=0)
    own, later = lax.optimization_barrier((own, later))
    moved = [move(own, along_x(step)) for step in (1, 2, 3)]
    close.append(local_near(*NEAR_PARTS[1], later, *local))
    moved, near, close[1], later = lax.optimization_barrier((moved, near, close[1], later))
    cross = move(near, other_core)
    blocks = [own] + moved
    blocks += [move(block, other_core) for block in blocks]
    wide = [local_far(*WIDE_PARTS[0], later, *local, near, cross)]
    blocks, wide[0], later = lax.optimization_barrier((blocks, wide[0], later))
    back = slide_wide(meta, slabs, blocks)
    back, later = lax.optimization_barrier((back, later))
    back = [back[0]] + [move(back[step], along_z(step)) for step in (1, 2, 3)]
    wide.append(local_far(*WIDE_PARTS[1], later, *local, near, cross))
    return merge(meta, close, wide, back)


def solution(mesh):
    placed = (
        P(("slide", "seq"), None),
        P(("slide", "seq"), None),
        P(("slide", "seq"), None),
        P("slide"),
    )
    return jax.shard_map(
        per_device, mesh=mesh, in_specs=placed, out_specs=P(("slide", "seq"), None), check_vma=False
    )
```

```python
import functools

import jax
import jax.numpy as jnp
import numpy as np
from jax import lax
from jax.experimental import pallas as pl
from jax.experimental.pallas import tpu as pltpu
from jax.sharding import PartitionSpec as P

HEADS = 12
HEAD_DIM = 64
WIDTH = 768
ROWS = 1024
RES = 16
GROUPS = ROWS // RES
HALF = GROUPS // 2
PAIRS = HEADS // 2
NX, NZ, NC = 4, 4, 2
MASKED = -1e30

BF = jnp.bfloat16
F32 = jnp.float32

ODD = [1, 3, 5, 7, 9, 11, 13, 15]
SHARED = [0, 8, 4, 12]
CLASS_U = {"A": ODD, "B": [2, 6, 10, 14], "C": [4, 12], "D": [8, 0]}
PAIR_OF = [0, 2, 3, 5]
LONE_OF = [2, 3, 8, 9]
NEAR_PARTS = [(0, 2), (2, 4)]
WIDE_PARTS = [(0, 2), (2, 4)]


def level(u):
    return 4 if u == 0 else min((u & -u).bit_length() - 1, 4)


def swap_matrix():
    row = lax.broadcasted_iota(jnp.int32, (256, 256), 0)
    col = lax.broadcasted_iota(jnp.int32, (256, 256), 1)
    return jnp.where(((row & 15) * 16 + (row >> 4)) == col, 1.0, 0.0).astype(BF)


def lane_low(rows):
    return lax.broadcasted_iota(jnp.int32, (rows, 128), 1) < 64


def split_kernel(
    meta, q_in, k_in, v_in, qt, kt, vt, sel, sel8, z0, z1, z2, z3, held, stage, arrived
):
    copies = []
    for at, source in enumerate((k_in, v_in, q_in)):
        copies.append(
            [
                pltpu.make_async_copy(
                    source.at[pl.ds(block * 256, 256)], held.at[at, block], arrived.at[at, block]
                )
                for block in range(4)
            ]
        )
    for copy in copies[0] + copies[1]:
        copy.start()
    swap = swap_matrix()
    for at, target in enumerate((kt, vt, qt)):
        for block in range(4):
            copies[at][block].wait()
            if at == 0:
                copies[2][block].start()
        for block in range(4):
            moved = jnp.dot(swap, held[at, block], preferred_element_type=F32).astype(BF)
            for res in range(RES):
                target[res, block * 16 : (block + 1) * 16, :] = moved[res * 16 : (res + 1) * 16, :]
    zpos = meta[1] // 2 % NZ
    low = lane_low(GROUPS)

    def other(rows):
        return pltpu.roll(rows.astype(F32), 64, 1).astype(BF)

    for pair in range(PAIRS):
        lanes = slice(pair * 128, pair * 128 + 128)

        def picked(ref, u):
            return jnp.where(
                low, ref[(u + 2 * pair) % RES, :, lanes], ref[(u + 2 * pair + 1) % RES, :, lanes]
            )

        for at, u in enumerate(SHARED):
            for kv, ref in enumerate((kt, vt)):
                rows = picked(ref, u)
                sel[at, kv, :, lanes] = rows
                if at < 2:
                    sel8[at, kv, :, lanes] = rows
                if at == 0 and kv == 0:
                    k0 = rows
                if at == 0 and kv == 1:
                    v0 = rows
        q0 = picked(qt, 0)
        for group in range(NZ):
            slot = group ^ zpos
            if pair == PAIR_OF[group]:
                stage[slot, :, 0:128] = q0
                stage[slot, :, 256:384] = k0
                stage[slot, :, 384:512] = v0
            if pair == LONE_OF[group] // 2:
                if LONE_OF[group] % 2 == 0:
                    lone_q, lone_k, lone_v = q0, k0, other(v0)
                else:
                    lone_q, lone_k, lone_v = other(q0), other(k0), v0
                stage[slot, :, 128:256] = jnp.where(low, lone_q, jnp.zeros_like(lone_q))
                stage[slot, :, 512:640] = jnp.where(low, lone_k, lone_v)
    for slot, out in enumerate((z0, z1, z2, z3)):
        out[...] = stage[slot]


def local_kernel(classes, first, many, meta, *refs):
    def body(step, carry):
        lanes = pl.ds(pl.multiple_of((first + step) * 128, 128), 128)
        here = pl.ds(pl.multiple_of(step * 128, 128), 128)
        views = [ref.at[:, :, lanes] for ref in refs[:3]] + [refs[3].at[:, :, :, lanes]]
        if classes == "D":
            views += [ref.at[:, :, :, lanes] for ref in refs[4:6]]
            views += [refs[6].at[:, :, here]]
            views += [ref.at[:, here] for ref in refs[7:9]]
        else:
            views += [refs[4].at[:, :, here]]
        local_pair(classes, first + step, meta, *views)
        return carry

    lax.fori_loop(0, many, body, 0, unroll=True)


def local_pair(classes, pair, meta, q_ref, k_ref, v_ref, sel, *rest):
    far = classes == "D"
    if far:
        near, cross, out, o0, lse0 = rest
    else:
        (out,) = rest
    bound = meta[0]
    device = meta[1]
    lane = lax.broadcasted_iota(jnp.int32, (1, 256), 1)
    groups = [(name, 0) for name in classes] + [(name, 1) for name in classes[::-1]]
    caps = [("ABCD".index(name), side) for name, side in groups]
    starts = [0]
    for name, _ in groups:
        starts.append(starts[-1] + len(CLASS_U[name]) * HALF)
    low = lane_low(starts[-1])

    def rows_of(ref, tile):
        half, odd = tile // 2, tile % 2
        rows = slice(half * HALF, (half + 1) * HALF)
        return jnp.concatenate([ref[2 * at + odd, rows, :] for at in range(8)], axis=0)

    keys = [rows_of(k_ref, tile) for tile in range(4)] + [sel[:, 0].reshape(256, 128)]
    values = [rows_of(v_ref, tile) for tile in range(4)] + [sel[:, 1].reshape(256, 128)]
    if far:
        for kv, rows in enumerate((keys, values)):
            rows.append(
                jnp.concatenate([near[0, kv], near[1, kv], cross[0, kv], cross[1, kv]], axis=0)
            )

    def inside(tile, parity, cap, side):
        if tile >= 4:
            return cap >= tile - 2
        return side == tile // 2 or (tile % 2 == parity and cap >= 1)

    def bias(tile, parity, cap, side):
        head = 2 * pair + parity
        logs = jnp.zeros((1, 256), F32)
        if tile < 4:
            half, odd = tile // 2, tile % 2
            res = 2 * (lane >> 5) + odd
            position = device * ROWS + half * 512 + (lane & 31) * 16 + res
            if odd == parity and cap >= 1:
                u = (res - head) & 15
                extra = 1.0 if side == half else 0.0
                one, two, three = (float(np.log(extra + min(cap, rank))) for rank in (1, 2, 3))
                logs = jnp.where(
                    (u & 2) != 0, one, jnp.where((u & 4) != 0, two, three)
                ) + jnp.zeros((1, 256), F32)
        elif tile == 4:
            u = ((lane >> 6) & 1) * 8 + (lane >> 7) * 4
            position = (device ^ 1) * ROWS + (lane & 63) * 16 + ((u + head) & 15)
            if cap == 3:
                logs = jnp.where(lane < 128, float(np.log(2.0)), 0.0)
        else:
            u = ((lane >> 6) & 1) * 8
            source = jnp.where(lane < 128, device ^ 2, device ^ 3)
            position = source * ROWS + (lane & 63) * 16 + ((u + head) & 15)
        return jnp.where(position < bound, logs, MASKED)

    queries = []
    for parity in range(2):
        head = 2 * pair + parity
        query = jnp.concatenate(
            [
                q_ref[(u + head) & 15, side * HALF : (side + 1) * HALF, :]
                for name, side in groups
                for u in CLASS_U[name]
            ],
            axis=0,
        )
        mine = low if parity == 0 else jnp.logical_not(low)
        queries.append((jnp.where(mine, query, jnp.zeros_like(query)) * 0.125).astype(BF))
    scores, spans = {}, {}
    for tile, key in enumerate(keys):
        parts = []
        for parity in range(2):
            held = [at for at, (cap, side) in enumerate(caps) if inside(tile, parity, cap, side)]
            spans[tile, parity] = (held[0], held[-1] + 1)
            parts.append(queries[parity][starts[held[0]] : starts[held[-1] + 1]])
        both = lax.dot_general(
            jnp.concatenate(parts, axis=0),
            key,
            (((1,), (1,)), ((), ())),
            preferred_element_type=F32,
        )
        cut = parts[0].shape[0]
        scores[tile, 0], scores[tile, 1] = both[:cut], both[cut:]
    weights = {spot: [] for spot in spans}
    peaks = {}
    for parity in range(2):
        for at, (cap, side) in enumerate(caps):
            held = []
            for tile in range(len(keys)):
                first, last = spans[tile, parity]
                if first <= at < last:
                    base = starts[first]
                    held.append(
                        (
                            tile,
                            scores[tile, parity][starts[at] - base : starts[at + 1] - base]
                            + bias(tile, parity, cap, side),
                        )
                    )
            peak = functools.reduce(jnp.maximum, [score for _, score in held])
            peak = jnp.max(peak, axis=1, keepdims=True)
            peaks[parity, at] = peak
            for tile, score in held:
                weights[tile, parity].append(jnp.exp(score - peak).astype(BF))
    totals = {}
    for tile, value in enumerate(values):
        for parity in range(2):
            side = lane_low(256) if parity == 0 else jnp.logical_not(lane_low(256))
            part = jnp.dot(
                jnp.concatenate(weights[tile, parity], axis=0),
                jnp.where(side, value, jnp.ones_like(value)),
                preferred_element_type=F32,
            )
            base = 0
            for at in range(*spans[tile, parity]):
                count = starts[at + 1] - starts[at]
                rows = part[base : base + count]
                base += count
                spot = (parity, at)
                totals[spot] = totals[spot] + rows if spot in totals else rows
    for parity in range(2):
        head = 2 * pair + parity
        mine = low[:HALF] if parity == 0 else jnp.logical_not(low[:HALF])
        for at, (name, half) in enumerate(groups):
            total = totals[parity, at]
            sums = pltpu.roll(total, 64, 1)
            result = total / sums
            rounded = result.astype(BF)
            rows = slice(half * HALF, (half + 1) * HALF)
            for row, u in enumerate(CLASS_U[name]):
                spot = ((u + head) & 15, rows, slice(None))
                out[spot] = jnp.where(mine, rounded[row * HALF : (row + 1) * HALF, :], out[spot])
            if name == "D":
                log_total = peaks[parity, at][HALF:] + jnp.log(sums[HALF:])
                o0[rows, :] = jnp.where(mine, result[HALF:], o0[rows, :])
                lse0[rows, :] = jnp.where(mine, log_total, lse0[rows, :])


def far_kernel(meta, a0, a1, a2, a3, *rest):
    blocks, outs = rest[:8], rest[8:]
    bound = meta[0]
    device = meta[1]
    xpos, zpos, core = device // 8, device // 2 % NZ, device % 2
    low256 = lane_low(256)
    group = zpos
    lane = lax.broadcasted_iota(jnp.int32, (1, 256), 1)
    part = lane >> 6
    pair = jnp.where(group == 0, 0, jnp.where(group == 1, 4, jnp.where(group == 2, 6, 10)))
    lone = jnp.where(group == 0, 2, jnp.where(group == 1, 3, jnp.where(group == 2, 8, 9)))
    def positions(at, head):
        from_x = xpos ^ (at % 4)
        from_c = core if at < 4 else 1 - core
        from_z = zpos ^ part
        return ((from_x * NZ + from_z) * NC + from_c) * ROWS + (lane & 63) * 16 + head

    results = []
    for heads in ((0, 1), (2,)):
        lanes = slice(0, 128) if heads[0] == 0 else slice(128, 256)
        query = jnp.concatenate([source[:, lanes] for source in (a0, a1, a2, a3)], axis=0)
        query = (query * 0.125).astype(BF)
        sides = [jnp.logical_not(low256) if head else low256 for head in heads]
        queries = [jnp.where(side, query, jnp.zeros_like(query)) for side in sides]
        if heads[0] == 2:
            queries = [query]
        both = jnp.concatenate(queries, axis=0)
        key_lanes = slice(0, 128) if heads[0] == 0 else slice(256, 384)
        value_lanes = slice(128, 256) if heads[0] == 0 else slice(256, 384)
        scores = [
            lax.dot_general(
                both, block[:, key_lanes], (((1,), (1,)), ((), ())), preferred_element_type=F32
            )
            for block in blocks
        ]
        for at, head in enumerate(heads):
            mine = sides[at]
            held = [
                score[at * 256 : (at + 1) * 256]
                + jnp.where(positions(spot, (pair, pair + 1, lone)[head]) < bound, 0.0, MASKED)
                for spot, score in enumerate(scores)
            ]
            peak = jnp.max(functools.reduce(jnp.maximum, held), axis=1, keepdims=True)
            total = None
            for score, block in zip(held, blocks):
                value = block[:, value_lanes]
                weighed = jnp.dot(
                    jnp.exp(score - peak).astype(BF),
                    jnp.where(mine, value, jnp.ones_like(value)),
                    preferred_element_type=F32,
                )
                total = weighed if total is None else total + weighed
            sums = pltpu.roll(total, 64, 1)
            results.append((total / sums, peak + jnp.log(sums if head < 2 else total)))
    low = low256[:64]
    lane = lax.broadcasted_iota(jnp.int32, (64, 128), 1)
    for at, out in enumerate(outs):
        rows = slice(at * 64, (at + 1) * 64)
        out[:, 0:128] = jnp.where(low, results[0][0][rows], results[1][0][rows]).astype(BF)
        mixed = results[2][0][rows].astype(BF)
        for which, place in ((0, 0), (1, 64), (2, 0)):
            rest = results[which][1][rows, place : place + 1]
            for term in range(3):
                kept = rest.astype(BF)
                rest = rest - kept.astype(F32)
                mixed = jnp.where(lane == which * 3 + term, kept, mixed)
        out[:, 128:256] = mixed


def part_of(parts, pair):
    for at, (first, many) in enumerate(parts):
        if first <= pair < first + many:
            return at, slice((pair - first) * 128, (pair - first) * 128 + 128)


def merge_kernel(meta, *refs):
    count = len(NEAR_PARTS)
    close, refs = refs[:count], refs[count:]
    count = len(WIDE_PARTS)
    wide, o0, lse0 = refs[:count], refs[count : 2 * count], refs[2 * count : 3 * count]
    r0, r1, r2, r3, out, stage, grid_rows, ready, sent = refs[3 * count :]
    bound = meta[0]
    device = meta[1]
    zpos = device // 2 % NZ
    for slot, ref in enumerate((r0, r1, r2, r3)):
        stage[slot] = ref[...].astype(F32)
    low = lane_low(GROUPS)

    def log_of(slot, which):
        terms = [stage[slot, :, 128 + which * 3 + term : 129 + which * 3 + term] for term in range(3)]
        return terms[0] + terms[1] + terms[2]

    for pair in range(PAIRS):
        lanes = slice(pair * 128, pair * 128 + 128)
        close_part, close_lanes = part_of(NEAR_PARTS, pair)
        wide_part, wide_lanes = part_of(WIDE_PARTS, pair)
        if pair in PAIR_OF:
            slot = PAIR_OF.index(pair) ^ zpos
            away = stage[slot, :, 0:128]
            away_lse = jnp.where(low, log_of(slot, 0), log_of(slot, 1))
        else:
            left = LONE_OF.index(2 * pair) ^ zpos
            right = (LONE_OF.index(2 * pair) + 1) ^ zpos
            away = jnp.where(low, pltpu.roll(stage[left, :, 128:256], 64, 1), stage[right, :, 128:256])
            away_lse = jnp.where(low, log_of(left, 2), log_of(right, 2))
        here, here_lse = o0[wide_part][:, wide_lanes], lse0[wide_part][:, wide_lanes]
        top = jnp.maximum(here_lse, away_lse)
        weight = jnp.exp(here_lse - top)
        away_weight = jnp.exp(away_lse - top)
        blended = (here * weight + away * away_weight) / (weight + away_weight)
        blended = blended.astype(BF)
        for res in range(RES):
            sides = []
            for head in (2 * pair, 2 * pair + 1):
                rank = level((res - head) % RES)
                if rank == 4:
                    sides.append(blended)
                elif rank == 3:
                    sides.append(wide[wide_part][res, :, wide_lanes])
                else:
                    sides.append(close[close_part][res, :, close_lanes])
            rows = jnp.where(low, *sides)
            for block in range(4):
                grid_rows[block, res * 16 : (res + 1) * 16, lanes] = rows[
                    block * 16 : (block + 1) * 16, :
                ]
    swap = swap_matrix()
    index = lax.broadcasted_iota(jnp.int32, (256, WIDTH), 0)
    copies = []
    for block in range(4):
        rows = jnp.dot(swap, grid_rows[block], preferred_element_type=F32)
        position = device * ROWS + block * 256 + index
        ready[block] = jnp.where(position < bound, rows, 0.0).astype(BF)
        copies.append(
            pltpu.make_async_copy(ready.at[block], out.at[pl.ds(block * 256, 256)], sent.at[block])
        )
        copies[-1].start()
    for copy in copies:
        copy.wait()


def smem():
    return pl.BlockSpec(memory_space=pltpu.SMEM)


def vmem():
    return pl.BlockSpec(memory_space=pltpu.VMEM)


def whole(shape):
    return pl.BlockSpec(shape, lambda i: (0,) * len(shape))


def params(mib):
    return pltpu.CompilerParams(vmem_limit_bytes=mib * 1024 * 1024)


def shape(dims, dtype=BF):
    return jax.ShapeDtypeStruct(dims, dtype)


def by_residue():
    return pl.BlockSpec((RES, GROUPS, 128), lambda i: (0, 0, i))


def by_part(parts):
    return pl.BlockSpec((parts, 2, GROUPS, 128), lambda i: (0, 0, 0, i))


def flat(block):
    return pl.BlockSpec((GROUPS, 128), lambda i: (0, i))


def split(meta, q, k, v):
    rows = [pltpu.with_memory_space_constraint(array, pltpu.HBM) for array in (q, k, v)]
    return pl.pallas_call(
        split_kernel,
        in_specs=[smem()] + [pl.BlockSpec(memory_space=pltpu.HBM)] * 3,
        out_specs=[vmem()] * 9,
        out_shape=[shape((RES, GROUPS, WIDTH))] * 3
        + [shape((4, 2, GROUPS, WIDTH)), shape((2, 2, GROUPS, WIDTH))]
        + [shape((GROUPS, 640))] * 4,
        scratch_shapes=[
            pltpu.VMEM((3, 4, 256, WIDTH), BF),
            pltpu.VMEM((4, GROUPS, 640), BF),
            pltpu.SemaphoreType.DMA((3, 4)),
        ],
        compiler_params=params(40),
        name="split_rows",
    )(meta, *rows)


def local_near(first, many, meta, q, k, v, sel):
    return pl.pallas_call(
        functools.partial(local_kernel, "ABC", first, many),
        in_specs=[smem()] + [vmem()] * 4,
        out_specs=vmem(),
        out_shape=shape((RES, GROUPS, many * 128)),
        compiler_params=params(40),
        cost_estimate=pl.CostEstimate(
            flops=many * 600000000, bytes_accessed=1000000, transcendentals=many * 1200000
        ),
        name="near_queries",
    )(meta, q, k, v, sel)


def local_far(first, many, meta, q, k, v, sel, near, cross):
    return pl.pallas_call(
        functools.partial(local_kernel, "D", first, many),
        in_specs=[smem()] + [vmem()] * 6,
        out_specs=[vmem()] * 3,
        out_shape=[
            shape((RES, GROUPS, many * 128)),
            shape((GROUPS, many * 128), F32),
            shape((GROUPS, many * 128), F32),
        ],
        compiler_params=params(40),
        cost_estimate=pl.CostEstimate(
            flops=many * 200000000, bytes_accessed=1000000, transcendentals=many * 400000
        ),
        name="wide_queries",
    )(meta, q, k, v, sel, near, cross)


def slide_wide(meta, queries, blocks):
    return pl.pallas_call(
        far_kernel,
        in_specs=[smem()] + [vmem()] * 12,
        out_specs=[vmem()] * 4,
        out_shape=[shape((GROUPS, 256))] * 4,
        compiler_params=params(40),
        cost_estimate=pl.CostEstimate(flops=800000000, bytes_accessed=2000000, transcendentals=1600000),
        name="slide_queries",
    )(meta, *queries, *blocks)


def merge(meta, close, wide, back):
    return pl.pallas_call(
        merge_kernel,
        in_specs=[smem()] + [vmem()] * (len(NEAR_PARTS) + 3 * len(WIDE_PARTS) + 4),
        out_specs=pl.BlockSpec(memory_space=pltpu.HBM),
        out_shape=shape((ROWS, WIDTH)),
        scratch_shapes=[
            pltpu.VMEM((4, GROUPS, 256), F32),
            pltpu.VMEM((4, 256, WIDTH), BF),
            pltpu.VMEM((4, 256, WIDTH), BF),
            pltpu.SemaphoreType.DMA((4,)),
        ],
        compiler_params=params(40),
        name="merge_rows",
    )(meta, *close, *[part for parts in zip(*wide) for part in parts], *back)


def at(x, z, c):
    return (x * NZ + z) * NC + c


def move(block, to):
    route = [
        (at(x, z, c), at(*to(x, z, c))) for x in range(NX) for z in range(NZ) for c in range(NC)
    ]
    return lax.ppermute(block, "seq", route)


def along_x(steps):
    return lambda x, z, c: (x ^ steps, z, c)


def along_z(steps):
    return lambda x, z, c: (x, z ^ steps, c)


def other_core(x, z, c):
    return (x, z, 1 - c)


def next_chip(x, z, c):
    return (x, z ^ 1, c)


def per_device(query_tiles, key_tiles, value_tiles, slide_length):
    device = lax.axis_index("seq").astype(jnp.int32)
    meta = jnp.stack([slide_length[0], device])
    qt, kt, vt, sel, sel8, z0, z1, z2, z3 = split(meta, query_tiles, key_tiles, value_tiles)
    slabs = [z0] + [move(slab, along_z(step)) for step, slab in ((1, z1), (2, z2), (3, z3))]
    pair = move(sel, other_core)
    near = move(sel8, next_chip)
    local = (qt, kt, vt, pair)
    close = [local_near(*NEAR_PARTS[0], meta, *local)]
    slabs, close[0], later = lax.optimization_barrier((slabs, close[0], meta))
    own = jnp.concatenate([slab[:, 256:640] for slab in slabs], axis=0)
    own, later = lax.optimization_barrier((own, later))
    moved = [move(own, along_x(step)) for step in (1, 2, 3)]
    close.append(local_near(*NEAR_PARTS[1], later, *local))
    cross = move(near, other_core)
    moved, close[1], later = lax.optimization_barrier((moved, close[1], later))
    blocks = [own] + moved
    blocks += [move(block, other_core) for block in blocks]
    wide = [local_far(*WIDE_PARTS[0], later, *local, near, cross)]
    blocks, wide[0], later = lax.optimization_barrier((blocks, wide[0], later))
    back = slide_wide(meta, slabs, blocks)
    back, later = lax.optimization_barrier((back, later))
    back = [back[0]] + [move(back[step], along_z(step)) for step in (1, 2, 3)]
    wide.append(local_far(*WIDE_PARTS[1], later, *local, near, cross))
    return merge(meta, close, wide, back)


def solution(mesh):
    placed = (
        P(("slide", "seq"), None),
        P(("slide", "seq"), None),
        P(("slide", "seq"), None),
        P("slide"),
    )
    return jax.shard_map(
        per_device, mesh=mesh, in_specs=placed, out_specs=P(("slide", "seq"), None), check_vma=False
    )
```
